32 devices in a mesh: section: 4 (over z), dp: 8 (over y, x, core).
Axes of the slice: x: 2, y: 2, z: 4, core: 2. Of those that a mesh axis runs over, the one named last changes fastest.
Arguments:
- tokens: bfloat16 [2560, 3072], P('dp'), may hold values from -6 to 6
- cotangent: bfloat16 [2560, 3072], P('dp'), may hold values from -6 to 6
- live_counts: int32 [8, 4], P('dp'), may hold values from 1 to 80, 240 in all within a row
- weight: bfloat16 [4, 3072, 3072], P('section'), may hold values from -0.0546875 to 0.0546875
- inverse_in: float32 [4, 16, 192, 192], P('section', 'dp'), may hold values from -3 to 4, as said below
- inverse_out: float32 [4, 16, 192, 192], P('section'), may hold values from -3 to 4, as said below
Outputs:
- update: bfloat16 [4, 3072, 3072], P('section', 'dp')
- factor_in: float32 [4, 16, 192, 192], P('section', 'dp')
- factor_out: float32 [4, 16, 192, 192], P('section', 'dp')
The draws below stay inside these ranges and needn't reach their ends.
Inputs may be any that keep to these rules, and one draw needn't show every extreme that they name: `live_counts`: on each data rank the live counts of the micro-batches sum to 240, and one of them is 80. `inverse_in`: each block is symmetric. `inverse_out`: each block is symmetric.
All inputs are finite; a program needn't handle non-finite values.
Results may differ from the reference program's by a relative error of at most 0.025.
Values may be sent and summed in bfloat16 or wider, within the bound.
No kernel may reach another device: no remote copies, remote signals or barrier semaphores. Data moves between devices by JAX's collectives and lax.ppermute only.
A program may use at most 192 MiB of HBM per device.

```python
import math
import jax
import jax.numpy as jnp
import numpy as np
from jax import lax

D = 3072
BLOCK = 192
MICRO = 4
ROWS = 80
TOK_DEV = 320
TOKENS = 2560
LAYERS = 4
NBLK = 16
N_DP = 8


def symmetric_blocks(key, diag_lo, diag_hi, spread):
    key_diag, key_off = jax.random.split(key)
    diag = jnp.exp(jax.random.uniform(key_diag, (LAYERS, NBLK, BLOCK), jnp.float32, jnp.log(diag_lo), jnp.log(diag_hi)))
    std = spread / (2.0 * BLOCK) ** 0.5
    noise = jnp.clip(jax.random.normal(key_off, (LAYERS, NBLK, BLOCK, BLOCK), jnp.float32), -4.0, 4.0) * std
    sym = noise + jnp.swapaxes(noise, 2, 3)
    eye = jnp.eye(BLOCK, dtype=jnp.float32)
    return sym * (1.0 - eye) + diag[:, :, :, None] * eye


def draw_inverse_in(key, part):
    key = jax.random.fold_in(key, 11)
    return symmetric_blocks(key, 0.5, 2.0, 0.5)


def draw_inverse_out(key, part):
    key = jax.random.fold_in(key, 23)
    return symmetric_blocks(key, 0.5, 2.0, 0.5)


def levels(key, shape, shards, low, high):
    gain = 1.0
    for dim, parts in shards:
        steps = jax.random.uniform(jax.random.fold_in(jax.random.fold_in(key, 6), dim), (parts,), jnp.float32, low / len(shards), high / len(shards))
        gain = gain * jnp.repeat(jnp.exp(steps), shape[dim] // parts).reshape((-1,) + (1,) * (len(shape) - 1 - dim))
    return gain


def split_up(number_of, total, most, lean):
    portions = [(1 << 20) // math.isqrt(grade ** lean) + 1 for grade in range(2, number_of + 1)]
    spare, given = total - most - (number_of - 1), [1] * (number_of - 1)
    while spare > 0:
        candidates = [i for i in range(number_of - 1) if given[i] < most]
        pool, remaining = sum([portions[i] for i in candidates]), spare
        for i in candidates:
            addition = min(most - given[i], max(1, remaining * portions[i] // pool), spare)
            given[i] = given[i] + addition
            spare = spare - addition
    return np.array([most] + given)


def uneven(rng, number_of, total, reach, skew):
    if number_of == 2:
        one = jax.random.randint(rng, (), max(1, total - reach), min(reach, total - 1) + 1)
        return jnp.stack([one, total - one])
    sizes = jnp.asarray(split_up(number_of, total, reach, skew), jnp.int32)
    twos = (number_of - 1) // 2
    source_of, sink = sizes[1:1 + 2 * twos:2], sizes[2:2 + 2 * twos:2]
    room = jnp.minimum(source_of - 1, reach - sink)
    moved = jax.random.randint(jax.random.fold_in(rng, 1), (twos,), 0, 1 << 20) % (room + 1)
    sizes = sizes.at[1:1 + 2 * twos:2].set(source_of - moved).at[2:2 + 2 * twos:2].set(sink + moved)
    return sizes[jax.random.permutation(jax.random.fold_in(rng, 2), number_of)]


def centred(own_key, shape, scale, reach, pieces=(), kind=jnp.bfloat16):
    array = scale * jax.random.normal(own_key, shape, jnp.float32)
    if pieces:
        array = array * levels(own_key, shape, pieces, -0.22, 0.18)
    return jnp.clip(array, -reach, reach).astype(kind)


def setup_inputs(seed: int = 0) -> dict:
    seeds = jax.random.split(jax.random.key(seed), 7)
    tokens = centred(seeds[0], (TOKENS, D), 1.0, 6.0, ((0, 8),))
    cotangent = centred(seeds[1], (TOKENS, D), 1.0, 6.0, ((0, 8),))
    live_counts = jax.vmap(lambda own: uneven(own, MICRO, 3 * ROWS, ROWS, 0))(jax.random.split(seeds[2], N_DP)).reshape((N_DP, MICRO)).astype(jnp.int32)
    weight = centred(seeds[3], (LAYERS, D, D), (4 * D) ** -0.5, 0.0546875, ((0, 4),))
    inverse_in = draw_inverse_in(jax.random.fold_in(seeds[6], 71), 0)
    inverse_out = draw_inverse_out(jax.random.fold_in(seeds[6], 71), 0)
    return dict(tokens=tokens, cotangent=cotangent, live_counts=live_counts, weight=weight, inverse_in=inverse_in, inverse_out=inverse_out)


C_ZERO = 0.7978845608028654
C_ONE = 0.044715

def activate(value):
    return 0.5 * value * (1.0 + jnp.tanh(C_ZERO * (value + C_ONE * value * value * value)))

def slope(value):
    hyper = jnp.tanh(C_ZERO * (value + C_ONE * value * value * value))
    return 0.5 * (1.0 + hyper) + 0.5 * value * (1.0 - hyper * hyper) * C_ZERO * (1.0 + 3.0 * C_ONE * value * value)

def block_gram(rows_data, total):
    blocks = rows_data.astype(jnp.float32).reshape(rows_data.shape[0], NBLK, BLOCK)
    return jnp.einsum('tkb,tkc->kbc', blocks, blocks) / total

def reference(tokens, cotangent, live_counts, weight, inverse_in, inverse_out):
    slots = jnp.arange(ROWS, dtype=jnp.int32)
    live = (slots[None, None, :] < live_counts[:, :, None]).reshape(TOKENS, 1).astype(jnp.float32)
    state = tokens
    inputs = []
    preacts = []
    for layer in range(LAYERS):
        pre = jnp.dot(state, weight[layer], preferred_element_type=jnp.float32)
        inputs.append(state)
        preacts.append(pre)
        state = (state.astype(jnp.float32) + activate(pre)).astype(jnp.bfloat16)
    flow = cotangent
    updates = [None] * LAYERS
    grams_in = [None] * LAYERS
    grams_out = [None] * LAYERS
    total = jnp.float32(TOKENS)
    for layer in range(LAYERS - 1, -1, -1):
        pre = preacts[layer]
        layer_in = inputs[layer]
        scaled = (flow.astype(jnp.float32) * slope(pre) * live).astype(jnp.bfloat16)
        flow = (flow.astype(jnp.float32) + jnp.dot(scaled, weight[layer].T, preferred_element_type=jnp.float32)).astype(jnp.bfloat16)

        def add_rank(carry, pair):
            rank_in, rank_scaled = pair
            term = jnp.dot(rank_in.T, rank_scaled, preferred_element_type=jnp.float32).astype(jnp.bfloat16)
            term = lax.optimization_barrier(term)
            return (carry + term.astype(jnp.float32), None)
        grad, unused = lax.scan(add_rank, jnp.zeros((D, D), jnp.float32), (layer_in.reshape(N_DP, TOK_DEV, D), scaled.reshape(N_DP, TOK_DEV, D)))
        live_in = layer_in * live.astype(jnp.bfloat16)
        grams_in[layer] = block_gram(live_in, total)
        grams_out[layer] = block_gram(scaled, total)
        left = jnp.einsum('kbc,kcd->kbd', inverse_in[layer], grad.reshape(NBLK, BLOCK, D), precision=lax.Precision.HIGHEST)
        right = jnp.einsum('rkc,kce->rke', left.reshape(D, NBLK, BLOCK), inverse_out[layer], precision=lax.Precision.HIGHEST)
        updates[layer] = (right.reshape(D, D) / jnp.sqrt(total)).astype(jnp.bfloat16)
    return (jnp.stack(updates), jnp.stack(grams_in), jnp.stack(grams_out))
```

```python
import functools
import math

import jax
import jax.numpy as jnp
from jax import lax
from jax.experimental import pallas as pl
from jax.experimental.pallas import tpu as pltpu
from jax.sharding import PartitionSpec as P

D = 3072
BLOCK = 192
MICRO = 4
ROWS = 80
TOK_DEV = 320
LIVE = 240
NBLK = 16

PIECE = 48
PIECES = LIVE // PIECE
WIDE = 1024
PAIR = 2 * BLOCK

C_ZERO = 0.7978845608028654
C_ONE = 0.044715

BF = jnp.bfloat16
F32 = jnp.float32
VM = pl.BlockSpec(memory_space=pltpu.VMEM)
SM = pl.BlockSpec(memory_space=pltpu.SMEM)
HB = pl.BlockSpec(memory_space=pl.ANY)
MIB = 1 << 20


def resident(x):
    return pltpu.with_memory_space_constraint(x, pltpu.VMEM)


def cost(flops, moved):
    return pl.CostEstimate(flops=int(flops), bytes_accessed=int(moved), transcendentals=0)


def pack_kernel(sections, counts_ref, tokens_ref, cot_ref, tok_out, cot_out, *unset):
    here = lax.axis_index("section")

    def pack(source, target):
        row = lax.broadcasted_iota(jnp.int32, (LIVE, TOK_DEV), 0)
        column = lax.broadcasted_iota(jnp.int32, (LIVE, TOK_DEV), 1)
        origin = row
        edge = jnp.int32(0)
        for micro in range(MICRO):
            count = counts_ref[0, micro]
            edge = edge + count
            origin = origin + jnp.where(row >= edge, ROWS - count, 0)
        pick = (column == origin).astype(F32).astype(BF)
        for start in range(0, D, WIDE):
            part = jnp.dot(
                pick, source[:, start : start + WIDE], preferred_element_type=F32
            ).astype(BF)
            for piece in range(PIECES):
                target[piece, :, start : start + WIDE] = part[piece * PIECE : (piece + 1) * PIECE]

    @pl.when(here == 0)
    def _():
        pack(tokens_ref, tok_out)

    @pl.when(here == sections - 1)
    def _():
        pack(cot_ref, cot_out)


def pack(sections, ranks, counts, tokens, cotangent):
    shape = jax.ShapeDtypeStruct((PIECES, PIECE, D), BF)
    store = jax.ShapeDtypeStruct((ranks, LIVE, D // ranks), BF)
    slopes = jax.ShapeDtypeStruct((PIECES, PIECE, D), F32)
    kept = [jax.ShapeDtypeStruct((PIECE, D), BF)] * PIECES
    return pl.pallas_call(
        functools.partial(pack_kernel, sections),
        out_shape=(shape, shape, store, slopes, *kept),
        in_specs=[SM, VM, VM],
        out_specs=(VM, VM, *[HB] * (2 + PIECES)),
        compiler_params=pltpu.CompilerParams(vmem_limit_bytes=24 * MIB),
        cost_estimate=cost(2 * LIVE * TOK_DEV * D, 8e6),
    )(counts, tokens, cotangent)


def forward_kernel(tick, sections, ranks, *refs):
    if tick == 0:
        tok_ref, w_ref, _, _, next_ref, store_ref, slope_ref, held = refs
        from_ref = None
    else:
        from_ref, tok_ref, w_ref, _, _, next_ref, store_ref, slope_ref, held = refs
    here = lax.axis_index("section")
    piece = tick - here
    own = D // ranks

    @pl.when(jnp.logical_and(piece >= 0, piece < PIECES))
    def _():
        if tick < PIECES:

            @pl.when(here == 0)
            def _():
                held[...] = tok_ref[tick]

        if tick > 0:

            @pl.when(here > 0)
            def _():
                held[...] = from_ref[...]

        rows = pl.ds(pl.multiple_of(piece * PIECE, PIECE), PIECE)
        for rank in range(ranks):
            store_ref[rank, rows, :] = held[:, rank * own : (rank + 1) * own]

        @pl.loop(0, D // WIDE)
        def _(step):
            columns = pl.ds(pl.multiple_of(step * WIDE, WIDE), WIDE)
            pre = jnp.dot(held[...], w_ref[:, columns], preferred_element_type=F32)
            square = pre * pre
            hyper = jnp.tanh(C_ZERO * (pre + C_ONE * pre * square))
            half = 0.5 * (1.0 + hyper)
            next_ref[:, columns] = (held[:, columns].astype(F32) + pre * half).astype(BF)
            slope_ref[piece, :, columns] = half + 0.5 * pre * (1.0 - hyper * hyper) * C_ZERO * (
                1.0 + 3.0 * C_ONE * square
            )


def forward(tick, sections, ranks, arrived, tokens, matrix, store, slopes):
    first = [] if tick == 0 else [arrived]
    base = len(first)
    return pl.pallas_call(
        functools.partial(forward_kernel, tick, sections, ranks),
        out_shape=(
            jax.ShapeDtypeStruct((PIECE, D), BF),
            jax.ShapeDtypeStruct(store.shape, store.dtype),
            jax.ShapeDtypeStruct(slopes.shape, slopes.dtype),
        ),
        in_specs=[VM] * (base + 4),
        out_specs=(VM, VM, VM),
        scratch_shapes=[pltpu.VMEM((PIECE, D), BF)],
        input_output_aliases={base + 2: 1, base + 3: 2},
        compiler_params=pltpu.CompilerParams(vmem_limit_bytes=12 * MIB),
        cost_estimate=cost(2 * 256 * D * D, 0),
    )(*first, resident(tokens), resident(matrix), resident(store), resident(slopes))


def backward_kernel(tick, sections, span, *refs):
    keeps = len(span)
    lead = 4 if tick > sections - 1 else 3
    ins = refs[:lead]
    w_ref, slope_ref, cot_ref = ins[:3]
    from_ref = ins[3] if lead == 4 else None
    next_ref = refs[lead + keeps]
    outs = refs[lead + keeps + 1 : lead + 2 * keeps + 1]
    flow, scaled, sem = refs[lead + 2 * keeps + 1 :]
    here = lax.axis_index("section")
    piece = tick - 2 * (sections - 1) + here

    @pl.when(jnp.logical_and(piece >= 0, piece < PIECES))
    def _():
        if 0 <= tick - (sections - 1) < PIECES:

            @pl.when(here == sections - 1)
            def _():
                flow[...] = cot_ref[tick - (sections - 1)]

        if from_ref is not None:

            @pl.when(here < sections - 1)
            def _():
                flow[...] = from_ref[...]

        scaled[...] = (flow[...].astype(F32) * slope_ref[piece]).astype(BF)
        for out, index in zip(outs, span):

            @pl.when(piece == index)
            def _():
                pltpu.make_async_copy(scaled, out, sem).start()

        @pl.when(here > 0)
        def _():
            @pl.loop(0, D // WIDE)
            def _(step):
                part = pl.ds(pl.multiple_of(step * WIDE, WIDE), WIDE)
                back = lax.dot_general(
                    scaled[...], w_ref[part, :], (((1,), (1,)), ((), ())), preferred_element_type=F32
                )
                next_ref[:, part] = (flow[:, part].astype(F32) + back).astype(BF)

        for out, index in zip(outs, span):

            @pl.when(piece == index)
            def _():
                pltpu.make_async_copy(scaled, out, sem).wait()


def backward(tick, sections, arrived, matrix, slopes, cotangent, kept):
    low = max(0, tick - 2 * (sections - 1))
    high = min(PIECES - 1, tick - (sections - 1))
    span = list(range(low, high + 1))
    first = [] if arrived is None else [arrived]
    base = 3 + len(first)
    out = pl.pallas_call(
        functools.partial(backward_kernel, tick, sections, span),
        out_shape=(
            jax.ShapeDtypeStruct((PIECE, D), BF),
            *[jax.ShapeDtypeStruct((PIECE, D), BF) for _ in span],
        ),
        in_specs=[VM] * base + [HB] * len(span),
        out_specs=(VM, *[HB for _ in span]),
        scratch_shapes=[
            pltpu.VMEM((PIECE, D), BF),
            pltpu.VMEM((PIECE, D), BF),
            pltpu.SemaphoreType.DMA,
        ],
        input_output_aliases={base + k: 1 + k for k in range(len(span))},
        compiler_params=pltpu.CompilerParams(vmem_limit_bytes=12 * MIB),
        cost_estimate=cost(2 * 256 * D * D, 0),
    )(resident(matrix), resident(slopes), resident(cotangent), *first, *[kept[k] for k in span])
    kept = list(kept)
    for k, index in enumerate(span):
        kept[index] = out[1 + k]
    return out[0], kept


def prepare_kernel(ranks, total, x_ref, pin_ref, pout_ref, xt_ref, factor_ref, left_ref, right_ref):
    own = D // ranks
    width = ranks * PIECE
    for piece in range(PIECES):
        part = x_ref[:, piece * PIECE : (piece + 1) * PIECE, :].reshape(width, own)
        xt_ref[:, piece * width : (piece + 1) * width] = part.T
    for block in range(own // BLOCK):
        rows = xt_ref[block * BLOCK : (block + 1) * BLOCK, :]
        gram = lax.dot_general(rows, rows, (((1,), (1,)), ((), ())), preferred_element_type=F32)
        factor_ref[block] = gram * (1.0 / total)
        left_ref[block] = pin_ref[block].astype(BF)
    row = lax.broadcasted_iota(jnp.int32, (BLOCK, PAIR), 0)
    column = lax.broadcasted_iota(jnp.int32, (BLOCK, PAIR), 1)

    @pl.loop(0, NBLK // 2)
    def _(pair):
        for side in range(2):
            place = (column == row + side * BLOCK).astype(F32).astype(BF)
            wide = jnp.dot(pout_ref[2 * pair + side].astype(BF), place, preferred_element_type=F32)
            right_ref[pair, side * BLOCK : (side + 1) * BLOCK, :] = wide.astype(BF)


def prepare(ranks, total, gathered, inverse_in, inverse_out):
    own = D // ranks
    blocks = own // BLOCK
    return pl.pallas_call(
        functools.partial(prepare_kernel, ranks, total),
        out_shape=(
            jax.ShapeDtypeStruct((own, ranks * LIVE), BF),
            jax.ShapeDtypeStruct((blocks, BLOCK, BLOCK), F32),
            jax.ShapeDtypeStruct((blocks, BLOCK, BLOCK), BF),
            jax.ShapeDtypeStruct((NBLK // 2, PAIR, PAIR), BF),
        ),
        in_specs=[VM, VM, VM],
        out_specs=(VM, VM, VM, VM),
        compiler_params=pltpu.CompilerParams(vmem_limit_bytes=24 * MIB),
        cost_estimate=cost(2 * ranks * LIVE * own * BLOCK, 6e6),
    )(gathered, inverse_in, inverse_out)


def finish_kernel(ranks, total, *refs):
    parts = refs[:PIECES]
    xt_ref, left_ref, right_ref, update_ref, factor_ref, every, sems = refs[PIECES:]
    own = D // ranks
    width = ranks * PIECE
    copies = [
        pltpu.make_async_copy(parts[k], every.at[pl.ds(k * width, width), :], sems.at[k])
        for k in range(PIECES)
    ]
    for copy in copies:
        copy.start()
    for copy in copies:
        copy.wait()
    rank = lax.axis_index("dp")
    if own % 128 == 0:
        columns = pl.ds(pl.multiple_of(rank * own, 128), own)
        turned = every[:, columns].T
    else:
        columns = pl.ds(pl.multiple_of((rank // 2) * (2 * own), 128), 2 * own)
        both = every[:, columns].T
        turned = jnp.where(lax.rem(rank, 2) == 0, both[:own], both[own:])
    for block in range(own // BLOCK):
        rows = turned[block * BLOCK : (block + 1) * BLOCK]
        gram = lax.dot_general(rows, rows, (((1,), (1,)), ((), ())), preferred_element_type=F32)
        factor_ref[block] = gram * (1.0 / total)

    @pl.loop(0, D // (2 * PAIR))
    def _(step):
        columns = pl.ds(pl.multiple_of(step * 2 * PAIR, 2 * PAIR), 2 * PAIR)
        grad = jnp.dot(xt_ref[...], every[:, columns], preferred_element_type=F32).astype(BF)
        for block in range(own // BLOCK):
            rows = slice(block * BLOCK, (block + 1) * BLOCK)
            left = jnp.dot(left_ref[block], grad[rows], preferred_element_type=F32).astype(BF)
            for side in range(2):
                right = jnp.dot(
                    left[:, side * PAIR : (side + 1) * PAIR],
                    right_ref[2 * step + side],
                    preferred_element_type=F32,
                )
                place = pl.ds(pl.multiple_of((2 * step + side) * PAIR, PAIR), PAIR)
                update_ref[rows, place] = (right * (1.0 / math.sqrt(total))).astype(BF)


def finish(ranks, total, parts, turned, left, right):
    own = D // ranks
    blocks = own // BLOCK
    return pl.pallas_call(
        functools.partial(finish_kernel, ranks, total),
        out_shape=(
            jax.ShapeDtypeStruct((own, D), BF),
            jax.ShapeDtypeStruct((blocks, BLOCK, BLOCK), F32),
        ),
        in_specs=[HB] * PIECES + [VM] * 3,
        out_specs=(VM, VM),
        scratch_shapes=[
            pltpu.VMEM((ranks * LIVE, D), BF),
            pltpu.SemaphoreType.DMA((PIECES,)),
        ],
        compiler_params=pltpu.CompilerParams(vmem_limit_bytes=48 * MIB),
        cost_estimate=cost(2 * ranks * LIVE * own * D, 18e6),
    )(*parts, turned, left, right)


def shards(sections, ranks, tokens, cotangent, live_counts, weight, inverse_in, inverse_out):
    matrix = weight[0]
    total = float(TOK_DEV * ranks)
    packed_tokens, packed_cot, store, slopes, *kept = pack(
        sections, ranks, live_counts, tokens, cotangent
    )
    parts = []
    ahead, behind = None, None
    gathered = None
    for tick in range(PIECES + 2 * (sections - 1)):
        arrived_ahead = arrived_behind = None
        if 0 < tick < PIECES + sections - 1:
            pairs = [(s - 1, s) for s in range(1, sections) if 0 <= tick - s < PIECES]
            arrived_ahead = lax.ppermute(ahead, "section", pairs)
        if tick > sections - 1:
            pairs = [
                (s + 1, s)
                for s in range(sections - 1)
                if 0 <= tick - 2 * (sections - 1) + s < PIECES
            ]
            arrived_behind = lax.ppermute(behind, "section", pairs)
        if tick < PIECES + sections - 1:
            ahead, store, slopes = forward(
                tick, sections, ranks, arrived_ahead, packed_tokens, matrix, store, slopes
            )
        if tick == PIECES + sections - 2:
            gathered = lax.all_to_all(store, "dp", split_axis=0, concat_axis=0, tiled=True)
        if tick >= sections - 1:
            behind, kept = backward(
                tick, sections, arrived_behind, matrix, slopes, packed_cot, kept
            )
        done = tick - 2 * (sections - 1)
        if 0 <= done < PIECES:
            parts.append(lax.all_gather(kept[done], "dp", axis=0, tiled=True))
    turned, factor_in, left, right = prepare(ranks, total, gathered, inverse_in[0], inverse_out[0])
    update, factor_out = finish(ranks, total, parts, turned, left, right)
    return (update[None], factor_in[None], factor_out[None])


def solution(mesh):
    in_specs = (
        P("dp", None),
        P("dp", None),
        P("dp", None),
        P("section", None, None),
        P("section", "dp", None, None),
        P("section", None, None, None),
    )
    out_specs = (
        P("section", "dp", None),
        P("section", "dp", None, None),
        P("section", "dp", None, None),
    )
    body = functools.partial(shards, mesh.shape["section"], mesh.shape["dp"])
    return jax.shard_map(body, mesh=mesh, in_specs=in_specs, out_specs=out_specs, check_vma=False)
```

```python
import functools
import math

import jax
import jax.numpy as jnp
from jax import lax
from jax.experimental import pallas as pl
from jax.experimental.pallas import tpu as pltpu
from jax.sharding import PartitionSpec as P

D = 3072
BLOCK = 192
MICRO = 4
ROWS = 80
TOK_DEV = 320
LIVE = 240
NBLK = 16

PIECE = 80
PIECES = LIVE // PIECE
WIDE = 1024
LOAD = 512
PAIR = 2 * BLOCK
SIDE = 256

C_ZERO = 0.7978845608028654
C_ONE = 0.044715

BF = jnp.bfloat16
F32 = jnp.float32
VM = pl.BlockSpec(memory_space=pltpu.VMEM)
SM = pl.BlockSpec(memory_space=pltpu.SMEM)
HB = pl.BlockSpec(memory_space=pl.ANY)
MIB = 1 << 20


def resident(x):
    return pltpu.with_memory_space_constraint(x, pltpu.VMEM)


def distant(x):
    return pltpu.with_memory_space_constraint(x, pltpu.HBM)


SMALL = pl.CostEstimate(flops=1000, bytes_accessed=1000, transcendentals=0)


def shape(*sizes, kind=BF):
    return jax.ShapeDtypeStruct(sizes, kind)


def near(*sizes, kind=BF):
    return pltpu.VMEM(sizes, kind)


def limit(size):
    return pltpu.CompilerParams(vmem_limit_bytes=size * MIB)


def swap(x, ranks, flip):
    return lax.ppermute(x, "dp", [(r, r ^ flip) for r in range(ranks)])


def contract_last(a, b):
    return lax.dot_general(a, b, (((1,), (1,)), ((), ())), preferred_element_type=F32)


def forward_columns(columns, held, w_ref, next_ref, slope_ref, piece):
    pre = jnp.dot(held[...], w_ref[:, columns], preferred_element_type=F32)
    square = pre * pre
    hyper = jnp.tanh(C_ZERO * (pre + C_ONE * pre * square))
    half = 0.5 * (1.0 + hyper)
    next_ref[:, columns] = (held[:, columns].astype(F32) + pre * half).astype(BF)
    slope_ref[piece, :, columns] = half + 0.5 * pre * (1.0 - hyper * hyper) * C_ZERO * (
        1.0 + 3.0 * C_ONE * square
    )


def keep_columns(piece, held, stores):
    chips = len(stores)
    width = D // chips
    chip = lax.div(lax.axis_index("dp"), 2)
    rows = pl.ds(pl.multiple_of(piece * PIECE, 16), PIECE)
    for offset, store in enumerate(stores):
        columns = pl.ds(pl.multiple_of((chip ^ offset) * width, 128), width)
        store[rows, :] = held[:, columns]


def begin_kernel(sections, chips, counts_ref, tokens_ref, cot_ref, weight_ref, *refs):
    w_ref, next_ref, tok_out, cot_out, slope_ref = refs[:5]
    stores = refs[5 : 5 + chips]
    held, raw, raw_sem, sems = refs[5 + chips + PIECES :]
    here = lax.axis_index("section")
    core = lax.rem(lax.axis_index("dp"), 2)
    loads = [
        pltpu.make_async_copy(
            weight_ref.at[:, pl.ds(k * LOAD, LOAD)], w_ref.at[:, pl.ds(k * LOAD, LOAD)], sems.at[k]
        )
        for k in range(D // LOAD)
    ]

    def pack(source, target):
        copy = pltpu.make_async_copy(source, raw, raw_sem)
        copy.start()
        for load in loads:
            load.start()
        row = lax.broadcasted_iota(jnp.int32, (LIVE, TOK_DEV), 0)
        column = lax.broadcasted_iota(jnp.int32, (LIVE, TOK_DEV), 1)
        origin = row
        edge = jnp.int32(0)
        for micro in range(MICRO):
            count = counts_ref[0, micro]
            edge = edge + count
            origin = origin + jnp.where(row >= edge, ROWS - count, 0)
        pick = (column == origin).astype(F32).astype(BF)
        copy.wait()
        for start in range(0, D, WIDE):
            part = jnp.dot(
                pick, raw[:, start : start + WIDE], preferred_element_type=F32
            ).astype(BF)
            for piece in range(PIECES):
                target[piece, :, start : start + WIDE] = part[piece * PIECE : (piece + 1) * PIECE]

    @pl.when(here == 0)
    def _():
        pack(tokens_ref, tok_out)
        held[...] = tok_out[0]
        keep_columns(0, held, stores)

    @pl.when(here == sections - 1)
    def _():
        if sections > 1:
            pack(cot_ref, cot_out)

    @pl.when(jnp.logical_and(here > 0, here < sections - 1))
    def _():
        for load in loads:
            load.start()

    lead = jnp.logical_and(here == 0, core == 0)
    for k, load in enumerate(loads):
        load.wait()

        @pl.when(lead)
        def _():
            forward_columns(pl.ds(k * LOAD, LOAD), held, w_ref, next_ref, slope_ref, 0)

    @pl.when(jnp.logical_and(here == 0, core != 0))
    def _():
        @pl.loop(0, D // WIDE)
        def _(step):
            columns = pl.ds(pl.multiple_of(step * WIDE, WIDE), WIDE)
            forward_columns(columns, held, w_ref, next_ref, slope_ref, 0)


def begin(sections, chips, counts, tokens, cotangent, matrix):
    packed = near(PIECES, PIECE, D)
    return pl.pallas_call(
        functools.partial(begin_kernel, sections, chips),
        out_shape=(
            near(D, D),
            near(PIECE, D),
            packed,
            packed,
            near(PIECES, PIECE, D, kind=F32),
            *[near(LIVE, D // chips)] * chips,
            *[near(PIECE, D)] * PIECES,
        ),
        in_specs=[SM, HB, HB, HB],
        out_specs=[VM] * (5 + chips) + [HB] * PIECES,
        scratch_shapes=[
            pltpu.VMEM((PIECE, D), BF),
            pltpu.VMEM((TOK_DEV, D), BF),
            pltpu.SemaphoreType.DMA,
            pltpu.SemaphoreType.DMA((D // LOAD,)),
        ],
        compiler_params=limit(6),
        cost_estimate=SMALL,
    )(counts, distant(tokens), distant(cotangent), distant(matrix))


def forward_kernel(tick, chips, from_ref, tok_ref, w_ref, *refs):
    next_ref, _, slope_ref = refs[1 + chips : 4 + chips]
    stores = refs[4 + chips : 4 + 2 * chips]
    (held,) = refs[4 + 2 * chips :]
    here = lax.axis_index("section")
    piece = tick - here

    @pl.when(jnp.logical_and(piece >= 0, piece < PIECES))
    def _():
        if tick < PIECES:

            @pl.when(here == 0)
            def _():
                held[...] = tok_ref[tick]

        @pl.when(here > 0)
        def _():
            held[...] = from_ref[...]

        @pl.loop(0, D // WIDE)
        def _(step):
            columns = pl.ds(pl.multiple_of(step * WIDE, WIDE), WIDE)
            forward_columns(columns, held, w_ref, next_ref, slope_ref, piece)

        keep_columns(piece, held, stores)


def forward(tick, arrived, tokens, matrix, slopes, stores):
    chips = len(stores)
    outs = pl.pallas_call(
        functools.partial(forward_kernel, tick, chips),
        out_shape=(
            near(PIECE, D),
            near(*matrix.shape),
            near(*slopes.shape, kind=F32),
            *[near(*s.shape) for s in stores],
        ),
        in_specs=[VM] * (4 + chips),
        out_specs=[VM] * (3 + chips),
        scratch_shapes=[pltpu.VMEM((PIECE, D), BF)],
        input_output_aliases={2 + k: 1 + k for k in range(2 + chips)},
        compiler_params=limit(6),
        cost_estimate=SMALL,
    )(
        resident(arrived),
        resident(tokens),
        resident(matrix),
        resident(slopes),
        *[resident(s) for s in stores],
    )
    return outs[0], outs[1], outs[2], list(outs[3:])


def backward_kernel(tick, sections, span, late, *refs):
    keeps = len(span)
    lead = 4 if tick > sections - 1 else 3
    w_ref, slope_ref, cot_ref = refs[:3]
    from_ref = refs[3] if lead == 4 else None
    outs = refs[lead + keeps + late :]
    next_ref, kept = outs[0], outs[2 : 2 + keeps]
    flow, scaled = outs[2 + keeps :]
    here = lax.axis_index("section")
    piece = tick - 2 * (sections - 1) + here

    @pl.when(jnp.logical_and(piece >= 0, piece < PIECES))
    def _():
        if 0 <= tick - (sections - 1) < PIECES:

            @pl.when(here == sections - 1)
            def _():
                flow[...] = cot_ref[tick - (sections - 1)]

        if from_ref is not None:

            @pl.when(here < sections - 1)
            def _():
                flow[...] = from_ref[...]

        scaled[...] = (flow[...].astype(F32) * slope_ref[piece]).astype(BF)
        for out, index in zip(kept, span):

            @pl.when(piece == index)
            def _():
                out[...] = scaled[...]

        @pl.when(here > 0)
        def _():
            @pl.loop(0, D // WIDE)
            def _(step):
                part = pl.ds(pl.multiple_of(step * WIDE, WIDE), WIDE)
                back = contract_last(scaled[...], w_ref[part, :])
                next_ref[:, part] = (flow[:, part].astype(F32) + back).astype(BF)


def backward(tick, sections, arrived, matrix, slopes, cotangent, kept, after):
    low = max(0, tick - 2 * (sections - 1))
    high = min(PIECES - 1, tick - (sections - 1))
    span = list(range(low, high + 1))
    first = [] if arrived is None else [resident(arrived)]
    base = 3 + len(first)
    out = pl.pallas_call(
        functools.partial(backward_kernel, tick, sections, span, len(after)),
        out_shape=(near(PIECE, D), near(D, D), *[near(PIECE, D) for _ in span]),
        in_specs=[VM] * (base + len(span)) + [HB] * len(after),
        out_specs=[VM] * (2 + len(span)),
        scratch_shapes=[pltpu.VMEM((PIECE, D), BF), pltpu.VMEM((PIECE, D), BF)],
        input_output_aliases={0: 1, **{base + k: 2 + k for k in range(len(span))}},
        compiler_params=limit(6),
        cost_estimate=SMALL,
    )(
        resident(matrix),
        resident(slopes),
        resident(cotangent),
        *first,
        *[resident(kept[k]) for k in span],
        *after,
    )
    kept = list(kept)
    for k, index in enumerate(span):
        kept[index] = out[2 + k]
    return out[0], out[1], kept


def prepare_kernel(chips, blocks, *refs):
    parts = refs[:chips]
    pin_ref, pout_ref, xt_ref, gram_ref, left_ref, right_ref = refs[chips:]
    for piece in range(PIECES):
        rows = slice(piece * PIECE, (piece + 1) * PIECE)
        both = jnp.concatenate([part[rows, :] for part in parts], axis=0)
        xt_ref[piece] = both.T
    for block in range(2 * blocks):
        rows = slice(block * BLOCK, (block + 1) * BLOCK)
        gram = jnp.zeros((BLOCK, BLOCK), F32)
        for piece in range(PIECES):
            some = xt_ref[piece, rows, :]
            gram = gram + contract_last(some, some)
        gram_ref[rows, :] = gram
    for block in range(blocks):
        left_ref[block] = pin_ref[block].astype(BF)
    row = lax.broadcasted_iota(jnp.int32, (BLOCK, PAIR), 0)
    column = lax.broadcasted_iota(jnp.int32, (BLOCK, PAIR), 1)

    @pl.loop(0, NBLK // 2)
    def _(pair):
        for side in range(2):
            place = (column == row + side * BLOCK).astype(F32).astype(BF)
            wide = jnp.dot(pout_ref[2 * pair + side].astype(BF), place, preferred_element_type=F32)
            right_ref[pair, side * BLOCK : (side + 1) * BLOCK, :] = wide.astype(BF)


def prepare(parts, inverse_in, inverse_out):
    chips = len(parts)
    width = D // chips
    blocks = inverse_in.shape[0]
    return pl.pallas_call(
        functools.partial(prepare_kernel, chips, blocks),
        out_shape=(
            near(PIECES, width, chips * PIECE),
            near(width, BLOCK, kind=F32),
            near(blocks, BLOCK, BLOCK),
            near(NBLK // 2, PAIR, PAIR),
        ),
        in_specs=[VM] * (chips + 2),
        out_specs=(VM, VM, VM, VM),
        compiler_params=limit(8),
        cost_estimate=SMALL,
    )(*[resident(p) for p in parts], inverse_in, inverse_out)


def add_gram(chips, every, gram_ref, begins):
    width = D // chips
    chip = lax.div(lax.axis_index("dp"), 2)
    columns = pl.ds(pl.multiple_of(chip * width, 128), width)
    turned = every[:, columns].T
    for block in range(width // BLOCK):
        rows = slice(block * BLOCK, (block + 1) * BLOCK)
        gram = contract_last(turned[rows], turned[rows])
        gram_ref[rows, :] = gram if begins else gram + gram_ref[rows, :]


def gather_kernel(chips, index, *refs):
    parts = refs[:chips]
    xt_ref = refs[chips]
    acc_ref, gram_ref, every = refs[-3:]
    for k, part in enumerate(parts):
        every[k * PIECE : (k + 1) * PIECE, :] = part[...]
    add_gram(chips, every, gram_ref, index == 0)

    @pl.loop(0, D // LOAD)
    def _(step):
        columns = pl.ds(pl.multiple_of(step * LOAD, LOAD), LOAD)
        term = jnp.dot(xt_ref[index], every[:, columns], preferred_element_type=F32)
        acc_ref[:, columns] = term if index == 0 else acc_ref[:, columns] + term


def gather(chips, index, parts, turned, so_far):
    width = D // chips
    return pl.pallas_call(
        functools.partial(gather_kernel, chips, index),
        out_shape=(near(width, D, kind=F32), near(width, BLOCK, kind=F32)),
        in_specs=[VM] * (chips + 1 + len(so_far)),
        out_specs=(VM, VM),
        scratch_shapes=[pltpu.VMEM((chips * PIECE, D), BF)],
        input_output_aliases={chips + 1 + k: k for k in range(len(so_far))},
        compiler_params=limit(8),
        cost_estimate=SMALL,
    )(*[resident(p) for p in parts], resident(turned), *[resident(a) for a in so_far])


def other_kernel(chips, *refs):
    parts = refs[:chips]
    xt_ref, acc_ref, gram_in_ref, gram_ref, _, _, out_ref, every = refs[chips:]
    own = D // chips // 2
    rows = pl.ds(pl.multiple_of((1 - lax.rem(lax.axis_index("dp"), 2)) * own, 16), own)
    for k, part in enumerate(parts):
        every[k * PIECE : (k + 1) * PIECE, :] = part[...]
    add_gram(chips, every, gram_ref, False)
    out_ref[:, D : D + BLOCK] = gram_ref[rows, :].astype(BF)
    out_ref[:, D + SIDE : D + SIDE + BLOCK] = gram_in_ref[rows, :].astype(BF)

    @pl.loop(0, D // LOAD)
    def _(step):
        columns = pl.ds(pl.multiple_of(step * LOAD, LOAD), LOAD)
        term = jnp.dot(xt_ref[PIECES - 1, rows, :], every[:, columns], preferred_element_type=F32)
        out_ref[:, columns] = (term + acc_ref[rows, columns]).astype(BF)


def other_half(chips, parts, turned, acc, gram_in, gram_out):
    width = D // chips
    return pl.pallas_call(
        functools.partial(other_kernel, chips),
        out_shape=(
            near(width, D, kind=F32),
            near(width, BLOCK, kind=F32),
            near(width // 2, D + 2 * SIDE),
        ),
        in_specs=[VM] * (chips + 4),
        out_specs=(VM, VM, VM),
        scratch_shapes=[pltpu.VMEM((chips * PIECE, D), BF)],
        input_output_aliases={chips + 1: 0, chips + 3: 1},
        compiler_params=limit(8),
        cost_estimate=SMALL,
    )(
        *[resident(p) for p in parts],
        resident(turned),
        resident(acc),
        resident(gram_in),
        resident(gram_out),
    )


def own_kernel(chips, *refs):
    parts = refs[:chips]
    xt_ref, acc_ref, out_ref, every = refs[chips:]
    own = D // chips // 2
    rows = pl.ds(pl.multiple_of(lax.rem(lax.axis_index("dp"), 2) * own, 16), own)
    for k, part in enumerate(parts):
        every[k * PIECE : (k + 1) * PIECE, :] = part[...]

    @pl.loop(0, D // LOAD)
    def _(step):
        columns = pl.ds(pl.multiple_of(step * LOAD, LOAD), LOAD)
        term = jnp.dot(xt_ref[PIECES - 1, rows, :], every[:, columns], preferred_element_type=F32)
        out_ref[:, columns] = term + acc_ref[rows, columns]


def own_half(chips, parts, turned, acc):
    width = D // chips
    return pl.pallas_call(
        functools.partial(own_kernel, chips),
        out_shape=near(width // 2, D, kind=F32),
        in_specs=[VM] * (chips + 2),
        out_specs=VM,
        scratch_shapes=[pltpu.VMEM((chips * PIECE, D), BF)],
        compiler_params=limit(8),
        cost_estimate=SMALL,
    )(*[resident(p) for p in parts], resident(turned), resident(acc))


def finish_kernel(blocks, total, own_ref, other_ref, left_ref, right_ref, *refs):
    gram_in_ref, gram_out_ref, update_ref, factor_in_ref, factor_out_ref, ready, sems = refs
    step_width = 2 * PAIR
    copies = []
    core = lax.rem(lax.axis_index("dp"), 2)
    for step in range(D // step_width):
        columns = slice(step * step_width, (step + 1) * step_width)
        grad = (own_ref[:, columns] + other_ref[:, columns].astype(F32)).astype(BF)
        for block in range(blocks):
            rows = slice(block * BLOCK, (block + 1) * BLOCK)
            left = jnp.dot(left_ref[block], grad[rows], preferred_element_type=F32).astype(BF)
            for side in range(2):
                right = jnp.dot(
                    left[:, side * PAIR : (side + 1) * PAIR],
                    right_ref[2 * step + side],
                    preferred_element_type=F32,
                )
                ready[step, rows, side * PAIR : (side + 1) * PAIR] = (
                    right * (1.0 / math.sqrt(total))
                ).astype(BF)
        copy = pltpu.make_async_copy(ready.at[step], update_ref.at[:, columns], sems.at[step])
        copy.start()
        copies.append(copy)
    for block in range(blocks):
        rows = slice(block * BLOCK, (block + 1) * BLOCK)
        start = pl.multiple_of((core * blocks + block) * BLOCK, BLOCK)
        mine = pl.ds(start, BLOCK)
        factor_out_ref[block] = (
            gram_out_ref[mine, :] + other_ref[rows, D : D + BLOCK].astype(F32)
        ) * (1.0 / total)
        factor_in_ref[block] = (
            gram_in_ref[mine, :] + other_ref[rows, D + SIDE : D + SIDE + BLOCK].astype(F32)
        ) * (1.0 / total)
    for copy in copies:
        copy.wait()


def finish(blocks, total, own, other, left, right, gram_in, gram_out):
    factor = shape(blocks, BLOCK, BLOCK, kind=F32)
    steps = D // (2 * PAIR)
    return pl.pallas_call(
        functools.partial(finish_kernel, blocks, total),
        out_shape=(shape(blocks * BLOCK, D), factor, factor),
        in_specs=[VM] * 6,
        out_specs=(HB, VM, VM),
        scratch_shapes=[
            pltpu.VMEM((steps, blocks * BLOCK, 2 * PAIR), BF),
            pltpu.SemaphoreType.DMA((steps,)),
        ],
        compiler_params=limit(8),
        cost_estimate=SMALL,
    )(
        resident(own),
        resident(other),
        resident(left),
        resident(right),
        resident(gram_in),
        resident(gram_out),
    )


def shards(sections, ranks, tokens, cotangent, live_counts, weight, inverse_in, inverse_out):
    total = float(TOK_DEV * ranks)
    chips = ranks // 2
    begun = begin(sections, chips, live_counts, tokens, cotangent, weight[0])
    matrix, ahead, packed_tokens, packed_cot, slopes = begun[:5]
    stores = list(begun[5 : 5 + chips])
    kept = list(begun[5 + chips :])
    behind = None
    parts = []
    last_turn = 2 * (sections - 1)
    crossed = None
    acc = []
    for tick in range(PIECES + last_turn):
        done = tick - last_turn
        arrived_ahead = arrived_behind = None
        if 0 < tick < PIECES + sections - 1:
            pairs = [(s - 1, s) for s in range(1, sections) if 0 <= tick - s < PIECES]
            arrived_ahead = lax.ppermute(ahead, "section", pairs)
            ahead, matrix, slopes, stores = forward(
                tick, arrived_ahead, packed_tokens, matrix, slopes, stores
            )
        if tick > sections - 1:
            pairs = [(s + 1, s) for s in range(sections - 1) if 0 <= tick - last_turn + s < PIECES]
            arrived_behind = lax.ppermute(behind, "section", pairs)
        if tick >= sections - 1:
            after = []
            if tick == PIECES + sections - 1:
                after = crossed[1:]
            if done >= 1:
                after = after + [parts[done - 1][1 << b] for b in range(chips.bit_length() - 1)]
            if done >= 2:
                acc = gather(chips, done - 2, parts[done - 2], rows_turned, acc)
                after = after + [acc[1]]
            behind, matrix, kept = backward(
                tick, sections, arrived_behind, matrix, slopes, packed_cot, kept, after
            )
        if tick == PIECES + sections - 2:
            crossed = [stores[0]] + [swap(stores[o], ranks, 2 * o) for o in range(1, chips)]
            rows_turned, gram_in, left, right = prepare(crossed, inverse_in[0], inverse_out[0])
        if 0 <= done < PIECES:
            piece = [kept[done]]
            for offset in range(1, chips):
                bit = offset & -offset if done % 2 else 1 << (offset.bit_length() - 1)
                piece.append(swap(piece[offset ^ bit], ranks, 2 * bit))
            parts.append(piece)
    acc = gather(chips, PIECES - 2, parts[PIECES - 2], rows_turned, acc)
    acc, gram_out, other = other_half(chips, parts[-1], rows_turned, acc[0], gram_in, acc[1])
    other = swap(other, ranks, 1)
    own = own_half(chips, parts[-1], rows_turned, acc)
    update, factor_in, factor_out = finish(
        inverse_in.shape[1], total, own, other, left, right, gram_in, gram_out
    )
    return (update[None], factor_in[None], factor_out[None])


def solution(mesh):
    in_specs = (
        P("dp", None),
        P("dp", None),
        P("dp", None),
        P("section", None, None),
        P("section", "dp", None, None),
        P("section", None, None, None),
    )
    out_specs = (
        P("section", "dp", None),
        P("section", "dp", None, None),
        P("section", "dp", None, None),
    )
    body = functools.partial(shards, mesh.shape["section"], mesh.shape["dp"])
    return jax.shard_map(body, mesh=mesh, in_specs=in_specs, out_specs=out_specs, check_vma=False)
```

```python
import functools
import math

import jax
import jax.numpy as jnp
from jax import lax
from jax.experimental import pallas as pl
from jax.experimental.pallas import tpu as pltpu
from jax.sharding import PartitionSpec as P

D = 3072
BLOCK = 192
MICRO = 4
ROWS = 80
TOK_DEV = 320
LIVE = 240
NBLK = 16

PIECE = 80
PIECES = LIVE // PIECE
WIDE = 1024
LOAD = 512
PAIR = 2 * BLOCK
SIDE = 256
FLIGHT = 4

C_ZERO = 0.7978845608028654
C_ONE = 0.044715

BF = jnp.bfloat16
F32 = jnp.float32
VM = pl.BlockSpec(memory_space=pltpu.VMEM)
SM = pl.BlockSpec(memory_space=pltpu.SMEM)
HB = pl.BlockSpec(memory_space=pl.ANY)
MIB = 1 << 20


def resident(x):
    return pltpu.with_memory_space_constraint(x, pltpu.VMEM)


def distant(x):
    return pltpu.with_memory_space_constraint(x, pltpu.HBM)


SMALL = pl.CostEstimate(flops=1000, bytes_accessed=1000, transcendentals=0)


def shape(*sizes, kind=BF):
    return jax.ShapeDtypeStruct(sizes, kind)


def near(*sizes, kind=BF):
    return pltpu.VMEM(sizes, kind)


def limit(size):
    return pltpu.CompilerParams(vmem_limit_bytes=size * MIB)


def swap(x, ranks, flip):
    return lax.ppermute(x, "dp", [(r, r ^ flip) for r in range(ranks)])


def contract_last(a, b):
    return lax.dot_general(a, b, (((1,), (1,)), ((), ())), preferred_element_type=F32)


def forward_columns(columns, held, w_ref, next_ref, slope_ref, piece):
    pre = jnp.dot(held[...], w_ref[:, columns], preferred_element_type=F32)
    square = pre * pre
    hyper = jnp.tanh(C_ZERO * (pre + C_ONE * pre * square))
    half = 0.5 * (1.0 + hyper)
    next_ref[:, columns] = (held[:, columns].astype(F32) + pre * half).astype(BF)
    slope_ref[piece, :, columns] = half + 0.5 * pre * (1.0 - hyper * hyper) * C_ZERO * (
        1.0 + 3.0 * C_ONE * square
    )


def keep_columns(piece, span, held, stores):
    chips = len(stores) // len(span)
    width = D // chips
    chip = lax.div(lax.axis_index("dp"), 2)
    for k, index in enumerate(span):

        @pl.when(piece == index)
        def _():
            for offset in range(chips):
                columns = pl.ds(pl.multiple_of((chip ^ offset) * width, 128), width)
                stores[k * chips + offset][...] = held[:, columns]


def begin_kernel(sections, chips, counts_ref, tokens_ref, cot_ref, weight_ref, *refs):
    w_ref, next_ref, tok_out, cot_out, slope_ref = refs[:5]
    stores = refs[5 : 5 + chips]
    held, raw, raw_sem, sems = refs[-4:]
    here = lax.axis_index("section")
    loads = [
        pltpu.make_async_copy(
            weight_ref.at[:, pl.ds(k * LOAD, LOAD)], w_ref.at[:, pl.ds(k * LOAD, LOAD)], sems.at[k]
        )
        for k in range(D // LOAD)
    ]
    copy_tokens = pltpu.make_async_copy(tokens_ref, raw, raw_sem)
    copy_cot = pltpu.make_async_copy(cot_ref, raw, raw_sem)

    def pack(copy, target):
        row = lax.broadcasted_iota(jnp.int32, (LIVE, TOK_DEV), 0)
        column = lax.broadcasted_iota(jnp.int32, (LIVE, TOK_DEV), 1)
        origin = row
        edge = jnp.int32(0)
        for micro in range(MICRO):
            count = counts_ref[0, micro]
            edge = edge + count
            origin = origin + jnp.where(row >= edge, ROWS - count, 0)
        pick = (column == origin).astype(F32).astype(BF)
        copy.wait()
        for start in range(0, D, WIDE):
            part = jnp.dot(
                pick, raw[:, start : start + WIDE], preferred_element_type=F32
            ).astype(BF)
            for piece in range(PIECES):
                target[piece, :, start : start + WIDE] = part[piece * PIECE : (piece + 1) * PIECE]

    @pl.when(here == 0)
    def _():
        copy_tokens.start()

    for load in loads[:FLIGHT]:
        load.start()

    @pl.when(here == 0)
    def _():
        pack(copy_tokens, tok_out)
        held[...] = tok_out[0]

    for k, load in enumerate(loads):
        load.wait()
        if k + FLIGHT < len(loads):
            loads[k + FLIGHT].start()

        @pl.when(here == 0)
        def _():
            forward_columns(pl.ds(k * LOAD, LOAD), held, w_ref, next_ref, slope_ref, 0)

    @pl.when(here == 0)
    def _():
        keep_columns(0, [0], held, stores)

    @pl.when(jnp.logical_and(here == sections - 1, sections > 1))
    def _():
        copy_cot.start()
        pack(copy_cot, cot_out)


def begin(sections, chips, counts, tokens, cotangent, matrix):
    packed = near(PIECES, PIECE, D)
    return pl.pallas_call(
        functools.partial(begin_kernel, sections, chips),
        out_shape=(
            near(D, D),
            near(PIECE, D),
            packed,
            packed,
            near(PIECES, PIECE, D, kind=F32),
            *[near(PIECE, D // chips)] * (chips * PIECES),
            *[near(PIECE, D)] * PIECES,
        ),
        in_specs=[SM, HB, HB, HB],
        out_specs=[VM] * (5 + chips) + [HB] * (chips * (PIECES - 1) + PIECES),
        scratch_shapes=[
            pltpu.VMEM((PIECE, D), BF),
            pltpu.VMEM((TOK_DEV, D), BF),
            pltpu.SemaphoreType.DMA,
            pltpu.SemaphoreType.DMA((D // LOAD,)),
        ],
        compiler_params=limit(8),
        cost_estimate=SMALL,
    )(counts, distant(tokens), distant(cotangent), distant(matrix))


def forward_kernel(tick, span, count, from_ref, tok_ref, w_ref, *refs):
    next_ref, _, slope_ref = refs[1 + count : 4 + count]
    stores = refs[4 + count : 4 + 2 * count]
    (held,) = refs[4 + 2 * count :]
    here = lax.axis_index("section")
    piece = tick - here

    @pl.when(jnp.logical_and(piece >= 0, piece < PIECES))
    def _():
        if tick < PIECES:

            @pl.when(here == 0)
            def _():
                held[...] = tok_ref[tick]

        @pl.when(here > 0)
        def _():
            held[...] = from_ref[...]

        @pl.loop(0, D // WIDE)
        def _(step):
            columns = pl.ds(pl.multiple_of(step * WIDE, WIDE), WIDE)
            forward_columns(columns, held, w_ref, next_ref, slope_ref, piece)

        keep_columns(piece, span, held, stores)


def forward(tick, sections, arrived, tokens, matrix, slopes, stores):
    span = list(range(max(0, tick - sections + 1), min(PIECES - 1, tick) + 1))
    flat = [s for k in span for s in stores[k]]
    count = len(flat)
    outs = pl.pallas_call(
        functools.partial(forward_kernel, tick, span, count),
        out_shape=(
            near(PIECE, D),
            near(*matrix.shape),
            near(*slopes.shape, kind=F32),
            *[near(*s.shape) for s in flat],
        ),
        in_specs=[VM] * (4 + count),
        out_specs=[VM] * (3 + count),
        scratch_shapes=[pltpu.VMEM((PIECE, D), BF)],
        input_output_aliases={2 + k: 1 + k for k in range(2 + count)},
        compiler_params=limit(6),
        cost_estimate=SMALL,
    )(
        resident(arrived),
        resident(tokens),
        resident(matrix),
        resident(slopes),
        *[resident(s) for s in flat],
    )
    stores = list(stores)
    chips = count // len(span)
    for k, index in enumerate(span):
        stores[index] = list(outs[3 + k * chips : 3 + (k + 1) * chips])
    return outs[0], outs[1], outs[2], stores


def backward_kernel(tick, sections, span, late, *refs):
    keeps = len(span)
    lead = 4 if tick > sections - 1 else 3
    w_ref, slope_ref, cot_ref = refs[:3]
    from_ref = refs[3] if lead == 4 else None
    outs = refs[lead + keeps + late :]
    next_ref, kept = outs[0], outs[2 : 2 + keeps]
    flow, scaled = outs[2 + keeps :]
    here = lax.axis_index("section")
    piece = tick - 2 * (sections - 1) + here

    @pl.when(jnp.logical_and(piece >= 0, piece < PIECES))
    def _():
        if 0 <= tick - (sections - 1) < PIECES:

            @pl.when(here == sections - 1)
            def _():
                flow[...] = cot_ref[tick - (sections - 1)]

        if from_ref is not None:

            @pl.when(here < sections - 1)
            def _():
                flow[...] = from_ref[...]

        scaled[...] = (flow[...].astype(F32) * slope_ref[piece]).astype(BF)
        for out, index in zip(kept, span):

            @pl.when(piece == index)
            def _():
                out[...] = scaled[...]

        @pl.when(here > 0)
        def _():
            @pl.loop(0, D // WIDE)
            def _(step):
                part = pl.ds(pl.multiple_of(step * WIDE, WIDE), WIDE)
                back = contract_last(scaled[...], w_ref[part, :])
                next_ref[:, part] = (flow[:, part].astype(F32) + back).astype(BF)


def backward(tick, sections, arrived, matrix, slopes, cotangent, kept, after):
    low = max(0, tick - 2 * (sections - 1))
    high = min(PIECES - 1, tick - (sections - 1))
    span = list(range(low, high + 1))
    first = [] if arrived is None else [resident(arrived)]
    base = 3 + len(first)
    out = pl.pallas_call(
        functools.partial(backward_kernel, tick, sections, span, len(after)),
        out_shape=(near(PIECE, D), near(D, D), *[near(PIECE, D) for _ in span]),
        in_specs=[VM] * (base + len(span)) + [HB] * len(after),
        out_specs=[VM] * (2 + len(span)),
        scratch_shapes=[pltpu.VMEM((PIECE, D), BF), pltpu.VMEM((PIECE, D), BF)],
        input_output_aliases={0: 1, **{base + k: 2 + k for k in range(len(span))}},
        compiler_params=limit(6),
        cost_estimate=SMALL,
    )(
        resident(matrix),
        resident(slopes),
        resident(cotangent),
        *first,
        *[resident(kept[k]) for k in span],
        *after,
    )
    kept = list(kept)
    for k, index in enumerate(span):
        kept[index] = out[2 + k]
    return out[0], out[1], kept


def prepare_kernel(chips, blocks, *refs):
    parts = refs[: chips * PIECES]
    pin_ref, pout_ref, xt_ref, gram_ref, left_ref, right_ref = refs[chips * PIECES :]
    for piece in range(PIECES):
        both = jnp.concatenate(
            [part[...] for part in parts[piece * chips : (piece + 1) * chips]], axis=0
        )
        xt_ref[piece] = both.T
    for block in range(2 * blocks):
        rows = slice(block * BLOCK, (block + 1) * BLOCK)
        gram = jnp.zeros((BLOCK, BLOCK), F32)
        for piece in range(PIECES):
            some = xt_ref[piece, rows, :]
            gram = gram + contract_last(some, some)
        gram_ref[rows, :] = gram
    for block in range(blocks):
        left_ref[block] = pin_ref[block].astype(BF)
    row = lax.broadcasted_iota(jnp.int32, (BLOCK, PAIR), 0)
    column = lax.broadcasted_iota(jnp.int32, (BLOCK, PAIR), 1)

    @pl.loop(0, NBLK // 2)
    def _(pair):
        for side in range(2):
            place = (column == row + side * BLOCK).astype(F32).astype(BF)
            wide = jnp.dot(pout_ref[2 * pair + side].astype(BF), place, preferred_element_type=F32)
            right_ref[pair, side * BLOCK : (side + 1) * BLOCK, :] = wide.astype(BF)


def prepare(parts, inverse_in, inverse_out):
    chips = len(parts[0])
    width = D // chips
    blocks = inverse_in.shape[0]
    flat = [p for piece in parts for p in piece]
    return pl.pallas_call(
        functools.partial(prepare_kernel, chips, blocks),
        out_shape=(
            near(PIECES, width, chips * PIECE),
            near(width, BLOCK, kind=F32),
            near(blocks, BLOCK, BLOCK),
            near(NBLK // 2, PAIR, PAIR),
        ),
        in_specs=[VM] * (len(flat) + 2),
        out_specs=(VM, VM, VM, VM),
        compiler_params=limit(8),
        cost_estimate=SMALL,
    )(*[resident(p) for p in flat], inverse_in, inverse_out)


def add_gram(chips, every, gram_ref, begins):
    width = D // chips
    chip = lax.div(lax.axis_index("dp"), 2)
    columns = pl.ds(pl.multiple_of(chip * width, 128), width)
    turned = every[:, columns].T
    for block in range(width // BLOCK):
        rows = slice(block * BLOCK, (block + 1) * BLOCK)
        gram = contract_last(turned[rows], turned[rows])
        gram_ref[rows, :] = gram if begins else gram + gram_ref[rows, :]


def fill(parts, every):
    for k, part in enumerate(parts):
        every[k * PIECE : (k + 1) * PIECE, :] = part[...]


def half_rows(mine, own):
    core = lax.rem(lax.axis_index("dp"), 2)
    return pl.ds(pl.multiple_of((core if mine else 1 - core) * own, 16), own)


def gather_kernel(chips, index, *refs):
    parts = refs[:chips]
    xt_ref = refs[chips]
    own_ref, other_ref, gram_ref, every = refs[-4:]
    fill(parts, every)
    add_gram(chips, every, gram_ref, index == 0)
    for mine, acc_ref in ((True, own_ref), (False, other_ref)):
        rows = half_rows(mine, acc_ref.shape[0])

        @pl.loop(0, D // LOAD)
        def _(step):
            columns = pl.ds(pl.multiple_of(step * LOAD, LOAD), LOAD)
            term = jnp.dot(xt_ref[index, rows, :], every[:, columns], preferred_element_type=F32)
            acc_ref[:, columns] = term if index == 0 else acc_ref[:, columns] + term


def gather(chips, index, parts, turned, so_far):
    width = D // chips
    half = near(width // 2, D, kind=F32)
    return pl.pallas_call(
        functools.partial(gather_kernel, chips, index),
        out_shape=(half, half, near(width, BLOCK, kind=F32)),
        in_specs=[VM] * (chips + 1 + len(so_far)),
        out_specs=(VM, VM, VM),
        scratch_shapes=[pltpu.VMEM((chips * PIECE, D), BF)],
        input_output_aliases={chips + 1 + k: k for k in range(len(so_far))},
        compiler_params=limit(8),
        cost_estimate=SMALL,
    )(*[resident(p) for p in parts], resident(turned), *[resident(a) for a in so_far])


def other_kernel(chips, *refs):
    parts = refs[:chips]
    xt_ref, acc_ref, gram_in_ref, gram_ref, _, out_ref, every = refs[chips:]
    rows = half_rows(False, acc_ref.shape[0])
    fill(parts, every)
    add_gram(chips, every, gram_ref, False)
    out_ref[:, D : D + BLOCK] = gram_ref[rows, :].astype(BF)
    out_ref[:, D + SIDE : D + SIDE + BLOCK] = gram_in_ref[rows, :].astype(BF)

    @pl.loop(0, D // LOAD)
    def _(step):
        columns = pl.ds(pl.multiple_of(step * LOAD, LOAD), LOAD)
        term = jnp.dot(xt_ref[PIECES - 1, rows, :], every[:, columns], preferred_element_type=F32)
        out_ref[:, columns] = (term + acc_ref[:, columns]).astype(BF)


def other_half(chips, parts, turned, acc, gram_in, gram_out):
    width = D // chips
    return pl.pallas_call(
        functools.partial(other_kernel, chips),
        out_shape=(near(width, BLOCK, kind=F32), near(width // 2, D + 2 * SIDE)),
        in_specs=[VM] * (chips + 4),
        out_specs=(VM, VM),
        scratch_shapes=[pltpu.VMEM((chips * PIECE, D), BF)],
        input_output_aliases={chips + 3: 0},
        compiler_params=limit(8),
        cost_estimate=SMALL,
    )(
        *[resident(p) for p in parts],
        resident(turned),
        resident(acc),
        resident(gram_in),
        resident(gram_out),
    )


def own_kernel(chips, *refs):
    parts = refs[:chips]
    xt_ref, acc_ref, out_ref, every = refs[chips:]
    rows = half_rows(True, acc_ref.shape[0])
    fill(parts, every)

    @pl.loop(0, D // LOAD)
    def _(step):
        columns = pl.ds(pl.multiple_of(step * LOAD, LOAD), LOAD)
        term = jnp.dot(xt_ref[PIECES - 1, rows, :], every[:, columns], preferred_element_type=F32)
        out_ref[:, columns] = term + acc_ref[:, columns]


def own_half(chips, parts, turned, acc):
    return pl.pallas_call(
        functools.partial(own_kernel, chips),
        out_shape=near(*acc.shape, kind=F32),
        in_specs=[VM] * (chips + 2),
        out_specs=VM,
        scratch_shapes=[pltpu.VMEM((chips * PIECE, D), BF)],
        input_output_aliases={chips + 1: 0},
        compiler_params=limit(8),
        cost_estimate=SMALL,
    )(*[resident(p) for p in parts], resident(turned), resident(acc))


def finish_kernel(blocks, total, own_ref, other_ref, left_ref, right_ref, *refs):
    gram_in_ref, gram_out_ref, update_ref, factor_in_ref, factor_out_ref, ready, sems = refs
    step_width = 2 * PAIR
    copies = []
    core = lax.rem(lax.axis_index("dp"), 2)
    for step in range(D // step_width):
        columns = slice(step * step_width, (step + 1) * step_width)
        grad = (own_ref[:, columns] + other_ref[:, columns].astype(F32)).astype(BF)
        for block in range(blocks):
            rows = slice(block * BLOCK, (block + 1) * BLOCK)
            left = jnp.dot(left_ref[block], grad[rows], preferred_element_type=F32).astype(BF)
            for side in range(2):
                right = jnp.dot(
                    left[:, side * PAIR : (side + 1) * PAIR],
                    right_ref[2 * step + side],
                    preferred_element_type=F32,
                )
                ready[step, rows, side * PAIR : (side + 1) * PAIR] = (
                    right * (1.0 / math.sqrt(total))
                ).astype(BF)
        copy = pltpu.make_async_copy(ready.at[step], update_ref.at[:, columns], sems.at[step])
        copy.start()
        copies.append(copy)
    for block in range(blocks):
        rows = slice(block * BLOCK, (block + 1) * BLOCK)
        start = pl.multiple_of((core * blocks + block) * BLOCK, BLOCK)
        mine = pl.ds(start, BLOCK)
        factor_out_ref[block] = (
            gram_out_ref[mine, :] + other_ref[rows, D : D + BLOCK].astype(F32)
        ) * (1.0 / total)
        factor_in_ref[block] = (
            gram_in_ref[mine, :] + other_ref[rows, D + SIDE : D + SIDE + BLOCK].astype(F32)
        ) * (1.0 / total)
    for copy in copies:
        copy.wait()


def finish(blocks, total, own, other, left, right, gram_in, gram_out):
    factor = shape(blocks, BLOCK, BLOCK, kind=F32)
    steps = D // (2 * PAIR)
    return pl.pallas_call(
        functools.partial(finish_kernel, blocks, total),
        out_shape=(shape(blocks * BLOCK, D), factor, factor),
        in_specs=[VM] * 6,
        out_specs=(HB, VM, VM),
        scratch_shapes=[
            pltpu.VMEM((steps, blocks * BLOCK, 2 * PAIR), BF),
            pltpu.SemaphoreType.DMA((steps,)),
        ],
        compiler_params=limit(8),
        cost_estimate=SMALL,
    )(
        resident(own),
        resident(other),
        resident(left),
        resident(right),
        resident(gram_in),
        resident(gram_out),
    )


def shards(sections, ranks, tokens, cotangent, live_counts, weight, inverse_in, inverse_out):
    total = float(TOK_DEV * ranks)
    chips = ranks // 2
    begun = begin(sections, chips, live_counts, tokens, cotangent, weight[0])
    matrix, ahead, packed_tokens, packed_cot, slopes = begun[:5]
    stores = [list(begun[5 + k * chips : 5 + (k + 1) * chips]) for k in range(PIECES)]
    kept = list(begun[5 + chips * PIECES :])
    behind = None
    parts = []
    crossed = []
    last_turn = 2 * (sections - 1)
    single = [1 << b for b in range(chips.bit_length() - 1)]
    acc = []
    for tick in range(PIECES + last_turn):
        done = tick - last_turn
        known = tick - (sections - 1)
        arrived_ahead = arrived_behind = None
        if 0 < tick < PIECES + sections - 1:
            pairs = [(s - 1, s) for s in range(1, sections) if 0 <= tick - s < PIECES]
            arrived_ahead = lax.ppermute(ahead, "section", pairs)
            ahead, matrix, slopes, stores = forward(
                tick, sections, arrived_ahead, packed_tokens, matrix, slopes, stores
            )
        if tick > sections - 1:
            pairs = [(s + 1, s) for s in range(sections - 1) if 0 <= tick - last_turn + s < PIECES]
            arrived_behind = lax.ppermute(behind, "section", pairs)
        if tick >= sections - 1:
            after = []
            if 1 <= known <= PIECES:
                after = crossed[known - 1][1:]
            if known == PIECES:
                rows_turned, gram_in, left, right = prepare(crossed, inverse_in[0], inverse_out[0])
            if done >= 1:
                after = after + [parts[done - 1][o] for o in single]
            if done >= 2:
                acc = gather(chips, done - 2, parts[done - 2], rows_turned, acc)
                after = after + [acc[2]]
            behind, matrix, kept = backward(
                tick, sections, arrived_behind, matrix, slopes, packed_cot, kept, after
            )
        if 0 <= known < PIECES:
            swapped = [swap(stores[known][o], ranks, 2 * o) for o in range(1, chips)]
            crossed.append([stores[known][0]] + swapped)
        if 0 <= done < PIECES:
            piece = [kept[done]]
            for offset in range(1, chips):
                bit = offset & -offset if done % 2 else 1 << (offset.bit_length() - 1)
                piece.append(swap(piece[offset ^ bit], ranks, 2 * bit))
            parts.append(piece)
    acc = gather(chips, PIECES - 2, parts[PIECES - 2], rows_turned, acc)
    gram_out, other = other_half(chips, parts[-1], rows_turned, acc[1], gram_in, acc[2])
    other = swap(other, ranks, 1)
    own = own_half(chips, parts[-1], rows_turned, acc[0])
    update, factor_in, factor_out = finish(
        inverse_in.shape[1], total, own, other, left, right, gram_in, gram_out
    )
    return (update[None], factor_in[None], factor_out[None])


def solution(mesh):
    in_specs = (
        P("dp", None),
        P("dp", None),
        P("dp", None),
        P("section", None, None),
        P("section", "dp", None, None),
        P("section", None, None, None),
    )
    out_specs = (
        P("section", "dp", None),
        P("section", "dp", None, None),
        P("section", "dp", None, None),
    )
    body = functools.partial(shards, mesh.shape["section"], mesh.shape["dp"])
    return jax.shard_map(body, mesh=mesh, in_specs=in_specs, out_specs=out_specs, check_vma=False)
```

```python
import functools
import math

import jax
import jax.numpy as jnp
from jax import lax
from jax.experimental import pallas as pl
from jax.experimental.pallas import tpu as pltpu
from jax.sharding import PartitionSpec as P

D = 3072
BLOCK = 192
MICRO = 4
ROWS = 80
TOK_DEV = 320
LIVE = 240
NBLK = 16

PIECE = 80
PIECES = LIVE // PIECE
WIDE = 1024
LOAD = 512
PAIR = 2 * BLOCK
SIDE = 256
FLIGHT = 4

C_ZERO = 0.7978845608028654
C_ONE = 0.044715

BF = jnp.bfloat16
F32 = jnp.float32
VM = pl.BlockSpec(memory_space=pltpu.VMEM)
SM = pl.BlockSpec(memory_space=pltpu.SMEM)
HB = pl.BlockSpec(memory_space=pl.ANY)
MIB = 1 << 20


def resident(x):
    return pltpu.with_memory_space_constraint(x, pltpu.VMEM)


def distant(x):
    return pltpu.with_memory_space_constraint(x, pltpu.HBM)


SMALL = pl.CostEstimate(flops=1000, bytes_accessed=1000, transcendentals=0)


def shape(*sizes, kind=BF):
    return jax.ShapeDtypeStruct(sizes, kind)


def near(*sizes, kind=BF):
    return pltpu.VMEM(sizes, kind)


def limit(size):
    return pltpu.CompilerParams(vmem_limit_bytes=size * MIB)


def swap(x, ranks, flip):
    return lax.ppermute(x, "dp", [(r, r ^ flip) for r in range(ranks)])


def contract_last(a, b):
    return lax.dot_general(a, b, (((1,), (1,)), ((), ())), preferred_element_type=F32)


def forward_columns(columns, held, w_ref, next_ref, slope_ref, piece):
    pre = jnp.dot(held[...], w_ref[:, columns], preferred_element_type=F32)
    square = pre * pre
    hyper = jnp.tanh(C_ZERO * (pre + C_ONE * pre * square))
    half = 0.5 * (1.0 + hyper)
    next_ref[:, columns] = (held[:, columns].astype(F32) + pre * half).astype(BF)
    slope = half + 0.5 * pre * (1.0 - hyper * hyper) * C_ZERO * (1.0 + 3.0 * C_ONE * square)
    slope_ref[piece, :, columns] = slope.astype(BF)


def keep_columns(piece, span, held, stores):
    chips = len(stores) // len(span)
    width = D // chips
    chip = lax.div(lax.axis_index("dp"), 2)
    for k, index in enumerate(span):

        @pl.when(piece == index)
        def _():
            for offset in range(chips):
                columns = pl.ds(pl.multiple_of((chip ^ offset) * width, 128), width)
                stores[k * chips + offset][...] = held[:, columns]


def begin_kernel(sections, chips, counts_ref, tokens_ref, cot_ref, weight_ref, *refs):
    w_ref, next_ref, tok_out, cot_out, slope_ref = refs[:5]
    stores = refs[5 : 5 + chips]
    held, raw, raw_sem, sems = refs[-4:]
    here = lax.axis_index("section")
    loads = [
        pltpu.make_async_copy(
            weight_ref.at[:, pl.ds(k * LOAD, LOAD)], w_ref.at[:, pl.ds(k * LOAD, LOAD)], sems.at[k]
        )
        for k in range(D // LOAD)
    ]
    copy_tokens = pltpu.make_async_copy(tokens_ref, raw, raw_sem)
    copy_cot = pltpu.make_async_copy(cot_ref, raw, raw_sem)

    def pack(target):
        row = lax.broadcasted_iota(jnp.int32, (LIVE, TOK_DEV), 0)
        column = lax.broadcasted_iota(jnp.int32, (LIVE, TOK_DEV), 1)
        origin = row
        edge = jnp.int32(0)
        for micro in range(MICRO):
            count = counts_ref[0, micro]
            edge = edge + count
            origin = origin + jnp.where(row >= edge, ROWS - count, 0)
        pick = (column == origin).astype(F32).astype(BF)
        for start in range(0, D, WIDE):
            part = jnp.dot(
                pick, raw[:, start : start + WIDE], preferred_element_type=F32
            ).astype(BF)
            for piece in range(PIECES):
                target[piece, :, start : start + WIDE] = part[piece * PIECE : (piece + 1) * PIECE]

    @pl.when(here == 0)
    def _():
        copy_tokens.start()
        copy_tokens.wait()

    for load in loads[:FLIGHT]:
        load.start()

    @pl.when(here == 0)
    def _():
        pack(tok_out)
        held[...] = tok_out[0]

    for k, load in enumerate(loads):
        load.wait()
        if k + FLIGHT < len(loads):
            loads[k + FLIGHT].start()

        @pl.when(here == 0)
        def _():
            forward_columns(pl.ds(k * LOAD, LOAD), held, w_ref, next_ref, slope_ref, 0)

    @pl.when(here == 0)
    def _():
        keep_columns(0, [0], held, stores)

    @pl.when(jnp.logical_and(here == sections - 1, sections > 1))
    def _():
        copy_cot.start()
        copy_cot.wait()
        pack(cot_out)


def begin(sections, chips, counts, tokens, cotangent, matrix):
    packed = near(PIECES, PIECE, D)
    return pl.pallas_call(
        functools.partial(begin_kernel, sections, chips),
        out_shape=(
            near(D, D),
            near(PIECE, D),
            packed,
            packed,
            near(PIECES, PIECE, D),
            *[near(PIECE, D // chips)] * (chips * PIECES),
            *[near(PIECE, D)] * PIECES,
        ),
        in_specs=[SM, HB, HB, HB],
        out_specs=[VM] * (5 + chips) + [HB] * (chips * (PIECES - 1) + PIECES),
        scratch_shapes=[
            pltpu.VMEM((PIECE, D), BF),
            pltpu.VMEM((TOK_DEV, D), BF),
            pltpu.SemaphoreType.DMA,
            pltpu.SemaphoreType.DMA((D // LOAD,)),
        ],
        compiler_params=limit(8),
        cost_estimate=SMALL,
    )(counts, distant(tokens), distant(cotangent), distant(matrix))


def forward_kernel(tick, span, count, from_ref, tok_ref, w_ref, *refs):
    next_ref, _, slope_ref = refs[1 + count : 4 + count]
    stores = refs[4 + count : 4 + 2 * count]
    (held,) = refs[4 + 2 * count :]
    here = lax.axis_index("section")
    piece = tick - here

    @pl.when(jnp.logical_and(piece >= 0, piece < PIECES))
    def _():
        if tick < PIECES:

            @pl.when(here == 0)
            def _():
                held[...] = tok_ref[tick]

        @pl.when(here > 0)
        def _():
            held[...] = from_ref[...]

        @pl.loop(0, D // WIDE)
        def _(step):
            columns = pl.ds(pl.multiple_of(step * WIDE, WIDE), WIDE)
            forward_columns(columns, held, w_ref, next_ref, slope_ref, piece)

        keep_columns(piece, span, held, stores)


def forward(tick, sections, arrived, tokens, matrix, slopes, stores):
    span = list(range(max(0, tick - sections + 1), min(PIECES - 1, tick) + 1))
    flat = [s for k in span for s in stores[k]]
    count = len(flat)
    outs = pl.pallas_call(
        functools.partial(forward_kernel, tick, span, count),
        out_shape=(
            near(PIECE, D),
            near(*matrix.shape),
            near(*slopes.shape),
            *[near(*s.shape) for s in flat],
        ),
        in_specs=[VM] * (4 + count),
        out_specs=[VM] * (3 + count),
        scratch_shapes=[pltpu.VMEM((PIECE, D), BF)],
        input_output_aliases={2 + k: 1 + k for k in range(2 + count)},
        compiler_params=limit(4),
        cost_estimate=SMALL,
    )(
        resident(arrived),
        resident(tokens),
        resident(matrix),
        resident(slopes),
        *[resident(s) for s in flat],
    )
    stores = list(stores)
    chips = count // len(span)
    for k, index in enumerate(span):
        stores[index] = list(outs[3 + k * chips : 3 + (k + 1) * chips])
    return outs[0], outs[1], outs[2], stores


def turn_kernel(w_ref, _, out_ref):
    @pl.when(lax.axis_index("section") > 0)
    def _():
        @pl.loop(0, D // LOAD)
        def _(step):
            rows = pl.ds(pl.multiple_of(step * LOAD, LOAD), LOAD)

            @pl.loop(0, D // LOAD)
            def _(other):
                columns = pl.ds(pl.multiple_of(other * LOAD, LOAD), LOAD)
                out_ref[columns, rows] = w_ref[rows, columns].T


def turn(matrix):
    return pl.pallas_call(
        turn_kernel,
        out_shape=(near(*matrix.shape), near(*matrix.shape)),
        in_specs=[VM],
        out_specs=(VM, VM),
        input_output_aliases={0: 0},
        compiler_params=limit(3),
        cost_estimate=SMALL,
    )(resident(matrix))


def backward_kernel(tick, sections, span, late, *refs):
    keeps = len(span)
    lead = 4 if tick > sections - 1 else 3
    w_ref, slope_ref, cot_ref = refs[:3]
    from_ref = refs[3] if lead == 4 else None
    outs = refs[lead + keeps + late :]
    next_ref, kept = outs[0], outs[2 : 2 + keeps]
    flow, scaled = outs[2 + keeps :]
    here = lax.axis_index("section")
    piece = tick - 2 * (sections - 1) + here

    @pl.when(jnp.logical_and(piece >= 0, piece < PIECES))
    def _():
        if 0 <= tick - (sections - 1) < PIECES:

            @pl.when(here == sections - 1)
            def _():
                flow[...] = cot_ref[tick - (sections - 1)]

        if from_ref is not None:

            @pl.when(here < sections - 1)
            def _():
                flow[...] = from_ref[...]

        scaled[...] = (flow[...].astype(F32) * slope_ref[piece].astype(F32)).astype(BF)
        for out, index in zip(kept, span):

            @pl.when(piece == index)
            def _():
                out[...] = scaled[...]

        @pl.when(here > 0)
        def _():
            @pl.loop(0, D // WIDE)
            def _(step):
                part = pl.ds(pl.multiple_of(step * WIDE, WIDE), WIDE)
                back = jnp.dot(scaled[...], w_ref[:, part], preferred_element_type=F32)
                next_ref[:, part] = (flow[:, part].astype(F32) + back).astype(BF)


def backward(tick, sections, arrived, matrix, slopes, cotangent, kept, after):
    low = max(0, tick - 2 * (sections - 1))
    high = min(PIECES - 1, tick - (sections - 1))
    span = list(range(low, high + 1))
    first = [] if arrived is None else [resident(arrived)]
    base = 3 + len(first)
    out = pl.pallas_call(
        functools.partial(backward_kernel, tick, sections, span, len(after)),
        out_shape=(near(PIECE, D), near(D, D), *[near(PIECE, D) for _ in span]),
        in_specs=[VM] * (base + len(span)) + [HB] * len(after),
        out_specs=[VM] * (2 + len(span)),
        scratch_shapes=[pltpu.VMEM((PIECE, D), BF), pltpu.VMEM((PIECE, D), BF)],
        input_output_aliases={0: 1, **{base + k: 2 + k for k in range(len(span))}},
        compiler_params=limit(4),
        cost_estimate=SMALL,
    )(
        resident(matrix),
        resident(slopes),
        resident(cotangent),
        *first,
        *[resident(kept[k]) for k in span],
        *after,
    )
    kept = list(kept)
    for k, index in enumerate(span):
        kept[index] = out[2 + k]
    return out[0], out[1], kept


def prepare_kernel(chips, blocks, *refs):
    parts = refs[: chips * PIECES]
    pin_ref, pout_ref, xt_ref, gram_ref, left_ref, right_ref = refs[chips * PIECES :]
    for piece in range(PIECES):
        both = jnp.concatenate(
            [part[...] for part in parts[piece * chips : (piece + 1) * chips]], axis=0
        )
        xt_ref[piece] = both.T
    for block in range(2 * blocks):
        rows = slice(block * BLOCK, (block + 1) * BLOCK)
        gram = jnp.zeros((BLOCK, BLOCK), F32)
        for piece in range(PIECES):
            some = xt_ref[piece, rows, :]
            gram = gram + contract_last(some, some)
        gram_ref[rows, :] = gram
    for block in range(blocks):
        left_ref[block] = pin_ref[block].astype(BF)
    row = lax.broadcasted_iota(jnp.int32, (BLOCK, PAIR), 0)
    column = lax.broadcasted_iota(jnp.int32, (BLOCK, PAIR), 1)

    @pl.loop(0, NBLK // 2)
    def _(pair):
        for side in range(2):
            place = (column == row + side * BLOCK).astype(F32).astype(BF)
            wide = jnp.dot(pout_ref[2 * pair + side].astype(BF), place, preferred_element_type=F32)
            right_ref[pair, side * BLOCK : (side + 1) * BLOCK, :] = wide.astype(BF)


def prepare(parts, inverse_in, inverse_out):
    chips = len(parts[0])
    width = D // chips
    blocks = inverse_in.shape[0]
    flat = [p for piece in parts for p in piece]
    return pl.pallas_call(
        functools.partial(prepare_kernel, chips, blocks),
        out_shape=(
            near(PIECES, width, chips * PIECE),
            near(width, BLOCK, kind=F32),
            near(blocks, BLOCK, BLOCK),
            near(NBLK // 2, PAIR, PAIR),
        ),
        in_specs=[VM] * (len(flat) + 2),
        out_specs=(VM, VM, VM, VM),
        compiler_params=limit(8),
        cost_estimate=SMALL,
    )(*[resident(p) for p in flat], inverse_in, inverse_out)


def add_gram(chips, every, gram_ref, begins):
    width = D // chips
    chip = lax.div(lax.axis_index("dp"), 2)
    columns = pl.ds(pl.multiple_of(chip * width, 128), width)
    turned = every[:, columns].T
    for block in range(width // BLOCK):
        rows = slice(block * BLOCK, (block + 1) * BLOCK)
        gram = contract_last(turned[rows], turned[rows])
        gram_ref[rows, :] = gram if begins else gram + gram_ref[rows, :]


def fill(parts, every):
    for k, part in enumerate(parts):
        every[k * PIECE : (k + 1) * PIECE, :] = part[...]


def half_rows(mine, own):
    core = lax.rem(lax.axis_index("dp"), 2)
    return pl.ds(pl.multiple_of((core if mine else 1 - core) * own, 16), own)


def gather_kernel(chips, index, *refs):
    parts = refs[:chips]
    xt_ref = refs[chips]
    own_ref, other_ref, gram_ref, every = refs[-4:]
    fill(parts, every)
    add_gram(chips, every, gram_ref, index == 0)
    for mine, acc_ref in ((True, own_ref), (False, other_ref)):
        rows = half_rows(mine, acc_ref.shape[0])

        @pl.loop(0, D // LOAD)
        def _(step):
            columns = pl.ds(pl.multiple_of(step * LOAD, LOAD), LOAD)
            term = jnp.dot(xt_ref[index, rows, :], every[:, columns], preferred_element_type=F32)
            acc_ref[:, columns] = term if index == 0 else acc_ref[:, columns] + term


def gather(chips, index, parts, turned, so_far):
    width = D // chips
    half = near(width // 2, D, kind=F32)
    return pl.pallas_call(
        functools.partial(gather_kernel, chips, index),
        out_shape=(half, half, near(width, BLOCK, kind=F32)),
        in_specs=[VM] * (chips + 1 + len(so_far)),
        out_specs=(VM, VM, VM),
        scratch_shapes=[pltpu.VMEM((chips * PIECE, D), BF)],
        input_output_aliases={chips + 1 + k: k for k in range(len(so_far))},
        compiler_params=limit(8),
        cost_estimate=SMALL,
    )(*[resident(p) for p in parts], resident(turned), *[resident(a) for a in so_far])


def other_kernel(chips, *refs):
    parts = refs[:chips]
    xt_ref, acc_ref, gram_in_ref, gram_ref, _, out_ref, every = refs[chips:]
    rows = half_rows(False, acc_ref.shape[0])
    fill(parts, every)
    add_gram(chips, every, gram_ref, False)
    out_ref[:, D : D + BLOCK] = gram_ref[rows, :].astype(BF)
    out_ref[:, D + SIDE : D + SIDE + BLOCK] = gram_in_ref[rows, :].astype(BF)

    @pl.loop(0, D // LOAD)
    def _(step):
        columns = pl.ds(pl.multiple_of(step * LOAD, LOAD), LOAD)
        term = jnp.dot(xt_ref[PIECES - 1, rows, :], every[:, columns], preferred_element_type=F32)
        out_ref[:, columns] = (term + acc_ref[:, columns]).astype(BF)


def other_half(chips, parts, turned, acc, gram_in, gram_out):
    width = D // chips
    return pl.pallas_call(
        functools.partial(other_kernel, chips),
        out_shape=(near(width, BLOCK, kind=F32), near(width // 2, D + 2 * SIDE)),
        in_specs=[VM] * (chips + 4),
        out_specs=(VM, VM),
        scratch_shapes=[pltpu.VMEM((chips * PIECE, D), BF)],
        input_output_aliases={chips + 3: 0},
        compiler_params=limit(8),
        cost_estimate=SMALL,
    )(
        *[resident(p) for p in parts],
        resident(turned),
        resident(acc),
        resident(gram_in),
        resident(gram_out),
    )


def own_kernel(chips, *refs):
    parts = refs[:chips]
    xt_ref, acc_ref, out_ref, every = refs[chips:]
    rows = half_rows(True, acc_ref.shape[0])
    fill(parts, every)

    @pl.loop(0, D // LOAD)
    def _(step):
        columns = pl.ds(pl.multiple_of(step * LOAD, LOAD), LOAD)
        term = jnp.dot(xt_ref[PIECES - 1, rows, :], every[:, columns], preferred_element_type=F32)
        out_ref[:, columns] = term + acc_ref[:, columns]


def own_half(chips, parts, turned, acc):
    return pl.pallas_call(
        functools.partial(own_kernel, chips),
        out_shape=near(*acc.shape, kind=F32),
        in_specs=[VM] * (chips + 2),
        out_specs=VM,
        scratch_shapes=[pltpu.VMEM((chips * PIECE, D), BF)],
        input_output_aliases={chips + 1: 0},
        compiler_params=limit(8),
        cost_estimate=SMALL,
    )(*[resident(p) for p in parts], resident(turned), resident(acc))


def finish_kernel(blocks, total, own_ref, other_ref, left_ref, right_ref, *refs):
    gram_in_ref, gram_out_ref, update_ref, factor_in_ref, factor_out_ref, ready, sems = refs
    step_width = 2 * PAIR
    copies = []
    core = lax.rem(lax.axis_index("dp"), 2)
    for step in range(D // step_width):
        columns = slice(step * step_width, (step + 1) * step_width)
        grad = (own_ref[:, columns] + other_ref[:, columns].astype(F32)).astype(BF)
        for block in range(blocks):
            rows = slice(block * BLOCK, (block + 1) * BLOCK)
            left = jnp.dot(left_ref[block], grad[rows], preferred_element_type=F32).astype(BF)
            for side in range(2):
                right = jnp.dot(
                    left[:, side * PAIR : (side + 1) * PAIR],
                    right_ref[2 * step + side],
                    preferred_element_type=F32,
                )
                ready[step, rows, side * PAIR : (side + 1) * PAIR] = (
                    right * (1.0 / math.sqrt(total))
                ).astype(BF)
        copy = pltpu.make_async_copy(ready.at[step], update_ref.at[:, columns], sems.at[step])
        copy.start()
        copies.append(copy)
    for block in range(blocks):
        rows = slice(block * BLOCK, (block + 1) * BLOCK)
        start = pl.multiple_of((core * blocks + block) * BLOCK, BLOCK)
        mine = pl.ds(start, BLOCK)
        factor_out_ref[block] = (
            gram_out_ref[mine, :] + other_ref[rows, D : D + BLOCK].astype(F32)
        ) * (1.0 / total)
        factor_in_ref[block] = (
            gram_in_ref[mine, :] + other_ref[rows, D + SIDE : D + SIDE + BLOCK].astype(F32)
        ) * (1.0 / total)
    for copy in copies:
        copy.wait()


def finish(blocks, total, own, other, left, right, gram_in, gram_out):
    factor = shape(blocks, BLOCK, BLOCK, kind=F32)
    steps = D // (2 * PAIR)
    return pl.pallas_call(
        functools.partial(finish_kernel, blocks, total),
        out_shape=(shape(blocks * BLOCK, D), factor, factor),
        in_specs=[VM] * 6,
        out_specs=(HB, VM, VM),
        scratch_shapes=[
            pltpu.VMEM((steps, blocks * BLOCK, 2 * PAIR), BF),
            pltpu.SemaphoreType.DMA((steps,)),
        ],
        compiler_params=limit(8),
        cost_estimate=SMALL,
    )(
        resident(own),
        resident(other),
        resident(left),
        resident(right),
        resident(gram_in),
        resident(gram_out),
    )


def shards(sections, ranks, tokens, cotangent, live_counts, weight, inverse_in, inverse_out):
    total = float(TOK_DEV * ranks)
    chips = ranks // 2
    begun = begin(sections, chips, live_counts, tokens, cotangent, weight[0])
    matrix, ahead, packed_tokens, packed_cot, slopes = begun[:5]
    stores = [list(begun[5 + k * chips : 5 + (k + 1) * chips]) for k in range(PIECES)]
    kept = list(begun[5 + chips * PIECES :])
    behind = None
    parts = []
    crossed = []
    last_turn = 2 * (sections - 1)
    single = [1 << b for b in range(chips.bit_length() - 1)]
    acc = []
    for tick in range(PIECES + last_turn):
        done = tick - last_turn
        known = tick - (sections - 1)
        arrived_ahead = arrived_behind = None
        if 0 < tick < PIECES + sections - 1:
            pairs = [(s - 1, s) for s in range(1, sections) if 0 <= tick - s < PIECES]
            arrived_ahead = lax.ppermute(ahead, "section", pairs)
            ahead, matrix, slopes, stores = forward(
                tick, sections, arrived_ahead, packed_tokens, matrix, slopes, stores
            )
        if tick == sections - 2:
            matrix, turned = turn(matrix)
        if tick > sections - 1:
            pairs = [(s + 1, s) for s in range(sections - 1) if 0 <= tick - last_turn + s < PIECES]
            arrived_behind = lax.ppermute(behind, "section", pairs)
        if tick >= sections - 1:
            after = []
            if 1 <= known <= PIECES:
                after = crossed[known - 1][1:]
            if known == PIECES:
                rows_turned, gram_in, left, right = prepare(crossed, inverse_in[0], inverse_out[0])
            if done >= 1:
                after = after + [parts[done - 1][o] for o in single]
            if done >= 2:
                acc = gather(chips, done - 2, parts[done - 2], rows_turned, acc)
                after = after + [acc[2]]
            behind, turned, kept = backward(
                tick, sections, arrived_behind, turned, slopes, packed_cot, kept, after
            )
        if 0 <= known < PIECES:
            swapped = [swap(stores[known][o], ranks, 2 * o) for o in range(1, chips)]
            crossed.append([stores[known][0]] + swapped)
        if 0 <= done < PIECES:
            piece = [kept[done]]
            for offset in range(1, chips):
                bit = offset & -offset if done % 2 else 1 << (offset.bit_length() - 1)
                piece.append(swap(piece[offset ^ bit], ranks, 2 * bit))
            parts.append(piece)
    acc = gather(chips, PIECES - 2, parts[PIECES - 2], rows_turned, acc)
    gram_out, other = other_half(chips, parts[-1], rows_turned, acc[1], gram_in, acc[2])
    other = swap(other, ranks, 1)
    own = own_half(chips, parts[-1], rows_turned, acc[0])
    update, factor_in, factor_out = finish(
        inverse_in.shape[1], total, own, other, left, right, gram_in, gram_out
    )
    return (update[None], factor_in[None], factor_out[None])


def solution(mesh):
    in_specs = (
        P("dp", None),
        P("dp", None),
        P("dp", None),
        P("section", None, None),
        P("section", "dp", None, None),
        P("section", None, None, None),
    )
    out_specs = (
        P("section", "dp", None),
        P("section", "dp", None, None),
        P("section", "dp", None, None),
    )
    body = functools.partial(shards, mesh.shape["section"], mesh.shape["dp"])
    return jax.shard_map(body, mesh=mesh, in_specs=in_specs, out_specs=out_specs, check_vma=False)
```

```python
import functools
import math

import jax
import jax.numpy as jnp
from jax import lax
from jax.experimental import pallas as pl
from jax.experimental.pallas import tpu as pltpu
from jax.sharding import PartitionSpec as P

D = 3072
BLOCK = 192
MICRO = 4
ROWS = 80
TOK_DEV = 320
LIVE = 240
NBLK = 16

PIECE = 80
PIECES = LIVE // PIECE
WIDE = 1024
LOAD = 512
PAIR = 2 * BLOCK
SIDE = 256
FLIGHT = 4

C_ZERO = 0.7978845608028654
C_ONE = 0.044715

BF = jnp.bfloat16
F32 = jnp.float32
VM = pl.BlockSpec(memory_space=pltpu.VMEM)
SM = pl.BlockSpec(memory_space=pltpu.SMEM)
HB = pl.BlockSpec(memory_space=pl.ANY)
MIB = 1 << 20


def resident(x):
    return pltpu.with_memory_space_constraint(x, pltpu.VMEM)


def distant(x):
    return pltpu.with_memory_space_constraint(x, pltpu.HBM)


SMALL = pl.CostEstimate(flops=1000, bytes_accessed=1000, transcendentals=0)


def shape(*sizes, kind=BF):
    return jax.ShapeDtypeStruct(sizes, kind)


def near(*sizes, kind=BF):
    return pltpu.VMEM(sizes, kind)


def limit(size):
    return pltpu.CompilerParams(vmem_limit_bytes=size * MIB)


def swap(x, ranks, flip):
    return lax.ppermute(x, "dp", [(r, r ^ flip) for r in range(ranks)])


def contract_last(a, b):
    return lax.dot_general(a, b, (((1,), (1,)), ((), ())), preferred_element_type=F32)


def forward_columns(columns, held, w_ref, next_ref, slope_ref, piece):
    pre = jnp.dot(held[...], w_ref[:, columns], preferred_element_type=F32)
    square = pre * pre
    hyper = jnp.tanh(C_ZERO * (pre + C_ONE * pre * square))
    half = 0.5 * (1.0 + hyper)
    next_ref[:, columns] = (held[:, columns].astype(F32) + pre * half).astype(BF)
    slope = half + 0.5 * pre * (1.0 - hyper * hyper) * C_ZERO * (1.0 + 3.0 * C_ONE * square)
    slope_ref[piece, :, columns] = slope.astype(BF)


def keep_columns(piece, span, held, stores):
    chips = len(stores) // len(span)
    width = D // chips
    chip = lax.div(lax.axis_index("dp"), 2)
    for k, index in enumerate(span):

        @pl.when(piece == index)
        def _():
            for offset in range(chips):
                columns = pl.ds(pl.multiple_of((chip ^ offset) * width, 128), width)
                stores[k * chips + offset][...] = held[:, columns]


def begin_kernel(sections, chips, counts_ref, tokens_ref, cot_ref, weight_ref, *refs):
    w_ref, next_ref, tok_out, cot_out, slope_ref = refs[:5]
    stores = refs[5 : 5 + chips]
    held, raw, raw_sem, sems = refs[-4:]
    here = lax.axis_index("section")
    loads = [
        pltpu.make_async_copy(
            weight_ref.at[:, pl.ds(k * LOAD, LOAD)], w_ref.at[:, pl.ds(k * LOAD, LOAD)], sems.at[k]
        )
        for k in range(D // LOAD)
    ]
    copy_tokens = pltpu.make_async_copy(tokens_ref, raw, raw_sem)
    copy_cot = pltpu.make_async_copy(cot_ref, raw, raw_sem)

    def pack(target):
        row = lax.broadcasted_iota(jnp.int32, (LIVE, TOK_DEV), 0)
        column = lax.broadcasted_iota(jnp.int32, (LIVE, TOK_DEV), 1)
        origin = row
        edge = jnp.int32(0)
        for micro in range(MICRO):
            count = counts_ref[0, micro]
            edge = edge + count
            origin = origin + jnp.where(row >= edge, ROWS - count, 0)
        pick = (column == origin).astype(F32).astype(BF)
        for start in range(0, D, WIDE):
            part = jnp.dot(
                pick, raw[:, start : start + WIDE], preferred_element_type=F32
            ).astype(BF)
            for piece in range(PIECES):
                target[piece, :, start : start + WIDE] = part[piece * PIECE : (piece + 1) * PIECE]

    @pl.when(here == 0)
    def _():
        copy_tokens.start()
        copy_tokens.wait()

    for load in loads[:FLIGHT]:
        load.start()

    @pl.when(here == 0)
    def _():
        pack(tok_out)
        held[...] = tok_out[0]

    for k, load in enumerate(loads):
        load.wait()
        if k + FLIGHT < len(loads):
            loads[k + FLIGHT].start()

        @pl.when(here == 0)
        def _():
            forward_columns(pl.ds(k * LOAD, LOAD), held, w_ref, next_ref, slope_ref, 0)

    @pl.when(here == 0)
    def _():
        keep_columns(0, [0], held, stores)

    @pl.when(jnp.logical_and(here == sections - 1, sections > 1))
    def _():
        copy_cot.start()
        copy_cot.wait()
        pack(cot_out)


def begin(sections, chips, counts, tokens, cotangent, matrix):
    packed = near(PIECES, PIECE, D)
    return pl.pallas_call(
        functools.partial(begin_kernel, sections, chips),
        out_shape=(
            near(D, D),
            near(PIECE, D),
            packed,
            packed,
            near(PIECES, PIECE, D),
            *[near(PIECE, D // chips)] * (chips * PIECES),
            *[near(PIECE, D)] * PIECES,
        ),
        in_specs=[SM, HB, HB, HB],
        out_specs=[VM] * (5 + chips) + [HB] * (chips * (PIECES - 1) + PIECES),
        scratch_shapes=[
            pltpu.VMEM((PIECE, D), BF),
            pltpu.VMEM((TOK_DEV, D), BF),
            pltpu.SemaphoreType.DMA,
            pltpu.SemaphoreType.DMA((D // LOAD,)),
        ],
        compiler_params=limit(8),
        cost_estimate=SMALL,
    )(counts, distant(tokens), distant(cotangent), distant(matrix))


def forward_kernel(tick, span, count, from_ref, tok_ref, w_ref, *refs):
    next_ref, _, slope_ref = refs[1 + count : 4 + count]
    stores = refs[4 + count : 4 + 2 * count]
    (held,) = refs[4 + 2 * count :]
    here = lax.axis_index("section")
    piece = tick - here

    @pl.when(jnp.logical_and(piece >= 0, piece < PIECES))
    def _():
        if tick < PIECES:

            @pl.when(here == 0)
            def _():
                held[...] = tok_ref[tick]

        @pl.when(here > 0)
        def _():
            held[...] = from_ref[...]

        @pl.loop(0, D // WIDE)
        def _(step):
            columns = pl.ds(pl.multiple_of(step * WIDE, WIDE), WIDE)
            forward_columns(columns, held, w_ref, next_ref, slope_ref, piece)

        keep_columns(piece, span, held, stores)


def forward(tick, sections, arrived, tokens, matrix, slopes, stores):
    span = list(range(max(0, tick - sections + 1), min(PIECES - 1, tick) + 1))
    flat = [s for k in span for s in stores[k]]
    count = len(flat)
    outs = pl.pallas_call(
        functools.partial(forward_kernel, tick, span, count),
        out_shape=(
            near(PIECE, D),
            near(*matrix.shape),
            near(*slopes.shape),
            *[near(*s.shape) for s in flat],
        ),
        in_specs=[VM] * (4 + count),
        out_specs=[VM] * (3 + count),
        scratch_shapes=[pltpu.VMEM((PIECE, D), BF)],
        input_output_aliases={2 + k: 1 + k for k in range(2 + count)},
        compiler_params=limit(4),
        cost_estimate=SMALL,
    )(
        resident(arrived),
        resident(tokens),
        resident(matrix),
        resident(slopes),
        *[resident(s) for s in flat],
    )
    stores = list(stores)
    chips = count // len(span)
    for k, index in enumerate(span):
        stores[index] = list(outs[3 + k * chips : 3 + (k + 1) * chips])
    return outs[0], outs[1], outs[2], stores


def turn_kernel(w_ref, _, out_ref):
    @pl.when(lax.axis_index("section") > 0)
    def _():
        @pl.loop(0, D // LOAD)
        def _(step):
            rows = pl.ds(pl.multiple_of(step * LOAD, LOAD), LOAD)

            @pl.loop(0, D // LOAD)
            def _(other):
                columns = pl.ds(pl.multiple_of(other * LOAD, LOAD), LOAD)
                out_ref[columns, rows] = w_ref[rows, columns].T


def turn(matrix):
    return pl.pallas_call(
        turn_kernel,
        out_shape=(near(*matrix.shape), near(*matrix.shape)),
        in_specs=[VM],
        out_specs=(VM, VM),
        input_output_aliases={0: 0},
        compiler_params=limit(3),
        cost_estimate=SMALL,
    )(resident(matrix))


def backward_kernel(tick, sections, span, late, *refs):
    keeps = len(span)
    refs = refs[late:]
    w_ref, slope_ref = refs[:2]
    chained = tick > sections - 1
    opens = tick - (sections - 1) < PIECES
    cot_ref = refs[2] if opens else None
    from_ref = refs[2 + opens + keeps] if chained else None
    outs = refs[2 + opens + keeps + chained :]
    next_ref, kept = outs[0], outs[2 : 2 + keeps]
    flow, scaled = outs[2 + keeps :]
    here = lax.axis_index("section")
    piece = tick - 2 * (sections - 1) + here

    @pl.when(jnp.logical_and(piece >= 0, piece < PIECES))
    def _():
        if opens:

            @pl.when(here == sections - 1)
            def _():
                flow[...] = cot_ref[tick - (sections - 1)]

        if from_ref is not None:

            @pl.when(here < sections - 1)
            def _():
                flow[...] = from_ref[...]

        scaled[...] = (flow[...].astype(F32) * slope_ref[piece].astype(F32)).astype(BF)
        for out, index in zip(kept, span):

            @pl.when(piece == index)
            def _():
                out[...] = scaled[...]

        @pl.when(here > 0)
        def _():
            @pl.loop(0, D // WIDE)
            def _(step):
                part = pl.ds(pl.multiple_of(step * WIDE, WIDE), WIDE)
                back = jnp.dot(scaled[...], w_ref[:, part], preferred_element_type=F32)
                next_ref[:, part] = (flow[:, part].astype(F32) + back).astype(BF)


def backward(tick, sections, arrived, matrix, slopes, cotangent, kept, after):
    low = max(0, tick - 2 * (sections - 1))
    high = min(PIECES - 1, tick - (sections - 1))
    span = list(range(low, high + 1))
    first = [] if arrived is None else [resident(arrived)]
    opens = [resident(cotangent)] if tick - (sections - 1) < PIECES else []
    base = 2 + len(after) + len(opens)
    out = pl.pallas_call(
        functools.partial(backward_kernel, tick, sections, span, len(after)),
        out_shape=(near(PIECE, D), near(D, D), *[near(PIECE, D) for _ in span]),
        in_specs=[HB] * len(after) + [VM] * (2 + len(opens) + len(span) + len(first)),
        out_specs=[VM] * (2 + len(span)),
        scratch_shapes=[pltpu.VMEM((PIECE, D), BF), pltpu.VMEM((PIECE, D), BF)],
        input_output_aliases={
            len(after): 1,
            **{base + k: 2 + k for k in range(len(span))},
        },
        compiler_params=limit(4),
        cost_estimate=SMALL,
    )(
        *after,
        resident(matrix),
        resident(slopes),
        *opens,
        *[resident(kept[k]) for k in span],
        *first,
    )
    kept = list(kept)
    for k, index in enumerate(span):
        kept[index] = out[2 + k]
    return out[0], out[1], kept


def prepare_kernel(chips, blocks, *refs):
    parts = refs[: chips * PIECES]
    pin_ref, pout_ref, gram_ref, left_ref, right_ref = refs[chips * PIECES : chips * PIECES + 5]
    turned = refs[chips * PIECES + 5 :]
    for piece in range(PIECES):
        some = [part[...] for part in parts[piece * chips : (piece + 1) * chips]]
        if piece < PIECES - 1:
            turned[piece][...] = jnp.concatenate(some, axis=0).T
        else:
            turned[piece][...] = jnp.concatenate(some[:-1], axis=0).T
            turned[piece + 1][...] = some[-1].T
    for block in range(2 * blocks):
        rows = slice(block * BLOCK, (block + 1) * BLOCK)
        gram = jnp.zeros((BLOCK, BLOCK), F32)
        for ref in turned:
            some = ref[rows, :]
            gram = gram + contract_last(some, some)
        gram_ref[rows, :] = gram
    for block in range(blocks):
        left_ref[block] = pin_ref[block].astype(BF)
    row = lax.broadcasted_iota(jnp.int32, (BLOCK, PAIR), 0)
    column = lax.broadcasted_iota(jnp.int32, (BLOCK, PAIR), 1)

    @pl.loop(0, NBLK // 2)
    def _(pair):
        for side in range(2):
            place = (column == row + side * BLOCK).astype(F32).astype(BF)
            wide = jnp.dot(pout_ref[2 * pair + side].astype(BF), place, preferred_element_type=F32)
            right_ref[pair, side * BLOCK : (side + 1) * BLOCK, :] = wide.astype(BF)


def prepare(parts, inverse_in, inverse_out):
    chips = len(parts[0])
    width = D // chips
    blocks = inverse_in.shape[0]
    flat = [p for piece in parts for p in piece]
    return pl.pallas_call(
        functools.partial(prepare_kernel, chips, blocks),
        out_shape=(
            near(width, BLOCK, kind=F32),
            near(blocks, BLOCK, BLOCK),
            near(NBLK // 2, PAIR, PAIR),
            *[near(width, chips * PIECE)] * (PIECES - 1),
            near(width, (chips - 1) * PIECE),
            near(width, PIECE),
        ),
        in_specs=[VM] * (len(flat) + 2),
        out_specs=[VM] * (4 + PIECES),
        compiler_params=limit(8),
        cost_estimate=SMALL,
    )(*[resident(p) for p in flat], inverse_in, inverse_out)


def add_gram(every, gram_ref, begins):
    width = gram_ref.shape[0]
    chip = lax.div(lax.axis_index("dp"), 2)
    columns = pl.ds(pl.multiple_of(chip * width, 128), width)
    turned = every[:, columns].T
    for block in range(width // BLOCK):
        rows = slice(block * BLOCK, (block + 1) * BLOCK)
        gram = contract_last(turned[rows], turned[rows])
        gram_ref[rows, :] = gram if begins else gram + gram_ref[rows, :]


def fill(parts, every):
    for k, part in enumerate(parts):
        every[k * PIECE : (k + 1) * PIECE, :] = part[...]


def half_rows(mine, own):
    core = lax.rem(lax.axis_index("dp"), 2)
    return pl.ds(pl.multiple_of((core if mine else 1 - core) * own, 16), own)


def gather_kernel(count, begins, *refs):
    parts = refs[:count]
    xt_ref = refs[count]
    own_ref, other_ref, gram_ref, every = refs[-4:]
    fill(parts, every)
    add_gram(every, gram_ref, begins)
    for mine, acc_ref in ((True, own_ref), (False, other_ref)):
        rows = half_rows(mine, acc_ref.shape[0])

        @pl.loop(0, D // LOAD)
        def _(step):
            columns = pl.ds(pl.multiple_of(step * LOAD, LOAD), LOAD)
            term = jnp.dot(xt_ref[rows, :], every[:, columns], preferred_element_type=F32)
            acc_ref[:, columns] = term if begins else acc_ref[:, columns] + term


def gather(parts, turned, so_far):
    count = len(parts)
    width = turned.shape[0]
    half = near(width // 2, D, kind=F32)
    return pl.pallas_call(
        functools.partial(gather_kernel, count, not so_far),
        out_shape=(half, half, near(width, BLOCK, kind=F32)),
        in_specs=[VM] * (count + 1 + len(so_far)),
        out_specs=(VM, VM, VM),
        scratch_shapes=[pltpu.VMEM((count * PIECE, D), BF)],
        input_output_aliases={count + 1 + k: k for k in range(len(so_far))},
        compiler_params=limit(8),
        cost_estimate=SMALL,
    )(*[resident(p) for p in parts], resident(turned), *[resident(a) for a in so_far])


def other_kernel(part, xt_ref, acc_ref, gram_in_ref, gram_ref, _, out_ref):
    rows = half_rows(False, acc_ref.shape[0])
    add_gram(part, gram_ref, False)
    out_ref[:, D : D + BLOCK] = gram_ref[rows, :].astype(BF)
    out_ref[:, D + SIDE : D + SIDE + BLOCK] = gram_in_ref[rows, :].astype(BF)

    @pl.loop(0, D // LOAD)
    def _(step):
        columns = pl.ds(pl.multiple_of(step * LOAD, LOAD), LOAD)
        term = jnp.dot(xt_ref[rows, :], part[:, columns], preferred_element_type=F32)
        out_ref[:, columns] = (term + acc_ref[:, columns]).astype(BF)


def other_half(part, turned, acc, gram_in, gram_out):
    width = turned.shape[0]
    return pl.pallas_call(
        other_kernel,
        out_shape=(near(width, BLOCK, kind=F32), near(width // 2, D + 2 * SIDE)),
        in_specs=[VM] * 5,
        out_specs=(VM, VM),
        input_output_aliases={4: 0},
        compiler_params=limit(8),
        cost_estimate=SMALL,
    )(resident(part), resident(turned), resident(acc), resident(gram_in), resident(gram_out))


def own_kernel(part, xt_ref, acc_ref, out_ref):
    rows = half_rows(True, acc_ref.shape[0])

    @pl.loop(0, D // LOAD)
    def _(step):
        columns = pl.ds(pl.multiple_of(step * LOAD, LOAD), LOAD)
        term = jnp.dot(xt_ref[rows, :], part[:, columns], preferred_element_type=F32)
        out_ref[:, columns] = term + acc_ref[:, columns]


def own_half(part, turned, acc):
    return pl.pallas_call(
        own_kernel,
        out_shape=near(*acc.shape, kind=F32),
        in_specs=[VM] * 3,
        out_specs=VM,
        input_output_aliases={2: 0},
        compiler_params=limit(8),
        cost_estimate=SMALL,
    )(resident(part), resident(turned), resident(acc))


def finish_kernel(blocks, total, own_ref, other_ref, left_ref, right_ref, *refs):
    gram_in_ref, gram_out_ref, update_ref, factor_in_ref, factor_out_ref, ready, sems = refs
    core = lax.rem(lax.axis_index("dp"), 2)
    scale = 1.0 / math.sqrt(total)
    pairs = D // PAIR
    for step in range(D // (2 * PAIR)):
        columns = slice(step * 2 * PAIR, (step + 1) * 2 * PAIR)
        grad = (own_ref[:, columns] + other_ref[:, columns].astype(F32)).astype(BF)
        for block in range(blocks):
            rows = slice(block * BLOCK, (block + 1) * BLOCK)
            ready[rows, columns] = jnp.dot(
                left_ref[block], grad[rows], preferred_element_type=F32
            ).astype(BF)
    copies = []
    for pair in range(pairs):
        columns = slice(pair * PAIR, (pair + 1) * PAIR)
        right = jnp.dot(ready[:, columns], right_ref[pair], preferred_element_type=F32)
        ready[:, columns] = (right * scale).astype(BF)
        if pair % 2:
            columns = slice((pair - 1) * PAIR, (pair + 1) * PAIR)
            copy = pltpu.make_async_copy(
                ready.at[:, columns], update_ref.at[:, columns], sems.at[pair // 2]
            )
            copy.start()
            copies.append(copy)
    for block in range(blocks):
        rows = slice(block * BLOCK, (block + 1) * BLOCK)
        start = pl.multiple_of((core * blocks + block) * BLOCK, BLOCK)
        mine = pl.ds(start, BLOCK)
        factor_out_ref[block] = (
            gram_out_ref[mine, :] + other_ref[rows, D : D + BLOCK].astype(F32)
        ) * (1.0 / total)
        factor_in_ref[block] = (
            gram_in_ref[mine, :] + other_ref[rows, D + SIDE : D + SIDE + BLOCK].astype(F32)
        ) * (1.0 / total)
    for copy in copies:
        copy.wait()


def finish(blocks, total, own, other, left, right, gram_in, gram_out):
    factor = shape(blocks, BLOCK, BLOCK, kind=F32)
    steps = D // (2 * PAIR)
    return pl.pallas_call(
        functools.partial(finish_kernel, blocks, total),
        out_shape=(shape(blocks * BLOCK, D), factor, factor),
        in_specs=[VM] * 6,
        out_specs=(HB, VM, VM),
        scratch_shapes=[
            pltpu.VMEM((blocks * BLOCK, D), BF),
            pltpu.SemaphoreType.DMA((steps,)),
        ],
        compiler_params=limit(8),
        cost_estimate=SMALL,
    )(
        resident(own),
        resident(other),
        resident(left),
        resident(right),
        resident(gram_in),
        resident(gram_out),
    )


def shards(sections, ranks, tokens, cotangent, live_counts, weight, inverse_in, inverse_out):
    total = float(TOK_DEV * ranks)
    chips = ranks // 2
    begun = begin(sections, chips, live_counts, tokens, cotangent, weight[0])
    matrix, ahead, packed_tokens, packed_cot, slopes = begun[:5]
    stores = [list(begun[5 + k * chips : 5 + (k + 1) * chips]) for k in range(PIECES)]
    kept = list(begun[5 + chips * PIECES :])
    behind = None
    parts = []
    crossed = []
    last_turn = 2 * (sections - 1)
    single = [1 << b for b in range(chips.bit_length() - 1)]
    acc = []
    for tick in range(PIECES + last_turn):
        done = tick - last_turn
        known = tick - (sections - 1)
        arrived_ahead = arrived_behind = None
        if 0 < tick < PIECES + sections - 1:
            pairs = [(s - 1, s) for s in range(1, sections) if 0 <= tick - s < PIECES]
            arrived_ahead = lax.ppermute(ahead, "section", pairs)
            ahead, matrix, slopes, stores = forward(
                tick, sections, arrived_ahead, packed_tokens, matrix, slopes, stores
            )
        if tick == sections - 2:
            matrix, turned = turn(matrix)
        if tick > sections - 1:
            pairs = [(s + 1, s) for s in range(sections - 1) if 0 <= tick - last_turn + s < PIECES]
            arrived_behind = lax.ppermute(behind, "section", pairs)
        if tick >= sections - 1:
            after = []
            if 1 <= known <= PIECES:
                after = crossed[known - 1][1:]
            if known == PIECES:
                gram_in, left, right, *rows_turned = prepare(
                    crossed, inverse_in[0], inverse_out[0]
                )
            if 1 <= done == PIECES - 1:
                after = after + [parts[done - 1][o] for o in single]
            if done >= 2:
                acc = gather(parts[done - 2], rows_turned[done - 2], acc)
                after = after + [acc[2]]
            behind, turned, kept = backward(
                tick, sections, arrived_behind, turned, slopes, packed_cot, kept, after
            )
        if 0 <= known < PIECES:
            swapped = [swap(stores[known][o], ranks, 2 * o) for o in range(1, chips)]
            crossed.append([stores[known][0]] + swapped)
        if 0 <= done < PIECES:
            piece = [kept[done]]
            for offset in range(1, chips):
                bit = offset & -offset if done % 2 else 1 << (offset.bit_length() - 1)
                piece.append(swap(piece[offset ^ bit], ranks, 2 * bit))
            parts.append(piece)
    acc = gather(parts[-1][:-1], rows_turned[-2], acc)
    acc = gather(parts[-2], rows_turned[-3], acc)
    gram_out, other = other_half(parts[-1][-1], rows_turned[-1], acc[1], gram_in, acc[2])
    other = swap(other, ranks, 1)
    own = own_half(parts[-1][-1], rows_turned[-1], acc[0])
    update, factor_in, factor_out = finish(
        inverse_in.shape[1], total, own, other, left, right, gram_in, gram_out
    )
    return (update[None], factor_in[None], factor_out[None])


def solution(mesh):
    in_specs = (
        P("dp", None),
        P("dp", None),
        P("dp", None),
        P("section", None, None),
        P("section", "dp", None, None),
        P("section", None, None, None),
    )
    out_specs = (
        P("section", "dp", None),
        P("section", "dp", None, None),
        P("section", "dp", None, None),
    )
    body = functools.partial(shards, mesh.shape["section"], mesh.shape["dp"])
    return jax.shard_map(body, mesh=mesh, in_specs=in_specs, out_specs=out_specs, check_vma=False)
```

```python
import functools
import math

import jax
import jax.numpy as jnp
from jax import lax
from jax.experimental import pallas as pl
from jax.experimental.pallas import tpu as pltpu
from jax.sharding import PartitionSpec as P

D = 3072
BLOCK = 192
MICRO = 4
ROWS = 80
TOK_DEV = 320
LIVE = 240
NBLK = 16

PIECE = 80
PIECES = LIVE // PIECE
WIDE = 1024
LOAD = 512
PAIR = 2 * BLOCK
SIDE = 256
FLIGHT = 4

C_ZERO = 0.7978845608028654
C_ONE = 0.044715

BF = jnp.bfloat16
F32 = jnp.float32
VM = pl.BlockSpec(memory_space=pltpu.VMEM)
HB = pl.BlockSpec(memory_space=pl.ANY)
MIB = 1 << 20


def resident(x):
    return pltpu.with_memory_space_constraint(x, pltpu.VMEM)


def distant(x):
    return pltpu.with_memory_space_constraint(x, pltpu.HBM)


SMALL = pl.CostEstimate(flops=1000, bytes_accessed=1000, transcendentals=0)


def shape(*sizes, kind=BF):
    return jax.ShapeDtypeStruct(sizes, kind)


def near(*sizes, kind=BF):
    return pltpu.VMEM(sizes, kind)


def limit(size):
    return pltpu.CompilerParams(vmem_limit_bytes=size * MIB)


def swap(x, ranks, flip):
    return lax.ppermute(x, "dp", [(r, r ^ flip) for r in range(ranks)])


def contract_last(a, b):
    return lax.dot_general(a, b, (((1,), (1,)), ((), ())), preferred_element_type=F32)


def forward_columns(columns, held, w_ref, next_ref, slope_ref, piece):
    pre = jnp.dot(held[...], w_ref[:, columns], preferred_element_type=F32)
    square = pre * pre
    hyper = jnp.tanh(C_ZERO * (pre + C_ONE * pre * square))
    half = 0.5 * (1.0 + hyper)
    if next_ref is not None:
        next_ref[:, columns] = (held[:, columns].astype(F32) + pre * half).astype(BF)
    slope = half + 0.5 * pre * (1.0 - hyper * hyper) * C_ZERO * (1.0 + 3.0 * C_ONE * square)
    slope_ref[piece, :, columns] = slope.astype(BF)


def keep_columns(piece, span, held, stores):
    chips = len(stores) // len(span)
    width = D // chips
    chip = lax.div(lax.axis_index("dp"), 2)
    for k, index in enumerate(span):

        @pl.when(piece == index)
        def _():
            for offset in range(chips):
                columns = pl.ds(pl.multiple_of((chip ^ offset) * width, 128), width)
                stores[k * chips + offset][...] = held[:, columns]


def begin_kernel(sections, chips, counts_ref, tokens_ref, cot_ref, weight_ref, *refs):
    w_ref, next_ref, tok_out, cot_out, slope_ref = refs[:5]
    stores = refs[5 : 5 + chips]
    held, raw, counts, raw_sem, counts_sem, sems = refs[-6:]
    here = lax.axis_index("section")
    loads = [
        pltpu.make_async_copy(
            weight_ref.at[:, pl.ds(k * LOAD, LOAD)], w_ref.at[:, pl.ds(k * LOAD, LOAD)], sems.at[k]
        )
        for k in range(D // LOAD)
    ]
    copy_tokens = pltpu.make_async_copy(tokens_ref, raw, raw_sem)
    copy_cot = pltpu.make_async_copy(cot_ref, raw, raw_sem)
    copy_counts = pltpu.make_async_copy(counts_ref, counts, counts_sem)

    def pack(target):
        row = lax.broadcasted_iota(jnp.int32, (LIVE, TOK_DEV), 0)
        column = lax.broadcasted_iota(jnp.int32, (LIVE, TOK_DEV), 1)
        origin = row
        edge = jnp.int32(0)
        for micro in range(MICRO):
            count = counts[0, micro]
            edge = edge + count
            origin = origin + jnp.where(row >= edge, ROWS - count, 0)
        pick = (column == origin).astype(F32).astype(BF)
        for start in range(0, D, WIDE):
            part = jnp.dot(
                pick, raw[:, start : start + WIDE], preferred_element_type=F32
            ).astype(BF)
            for piece in range(PIECES):
                target[piece, :, start : start + WIDE] = part[piece * PIECE : (piece + 1) * PIECE]

    @pl.when(here == 0)
    def _():
        copy_counts.start()
        copy_tokens.start()
        copy_counts.wait()
        copy_tokens.wait()

    for load in loads[:FLIGHT]:
        load.start()

    @pl.when(here == 0)
    def _():
        pack(tok_out)
        held[...] = tok_out[0]

    for k, load in enumerate(loads):
        load.wait()
        if k + FLIGHT < len(loads):
            loads[k + FLIGHT].start()

        @pl.when(here == 0)
        def _():
            forward_columns(pl.ds(k * LOAD, LOAD), held, w_ref, next_ref, slope_ref, 0)

    @pl.when(here == 0)
    def _():
        keep_columns(0, [0], held, stores)

    @pl.when(jnp.logical_and(here == sections - 1, sections > 1))
    def _():
        copy_counts.start()
        copy_cot.start()
        copy_counts.wait()
        copy_cot.wait()
        pack(cot_out)


def begin(sections, chips, counts, tokens, cotangent, matrix):
    packed = near(PIECES, PIECE, D)
    return pl.pallas_call(
        functools.partial(begin_kernel, sections, chips),
        out_shape=(
            near(D, D),
            near(PIECE, D),
            packed,
            packed,
            near(PIECES, PIECE, D),
            *[near(PIECE, D // chips)] * (chips * PIECES),
            *[near(PIECE, D)] * PIECES,
        ),
        in_specs=[HB] * 4,
        out_specs=[VM] * (5 + chips) + [HB] * (chips * (PIECES - 1) + PIECES),
        scratch_shapes=[
            pltpu.VMEM((PIECE, D), BF),
            pltpu.VMEM((TOK_DEV, D), BF),
            pltpu.SMEM((1, MICRO), jnp.int32),
            pltpu.SemaphoreType.DMA,
            pltpu.SemaphoreType.DMA,
            pltpu.SemaphoreType.DMA((D // LOAD,)),
        ],
        compiler_params=limit(8),
        cost_estimate=SMALL,
    )(distant(counts), distant(tokens), distant(cotangent), distant(matrix))


def forward_kernel(tick, span, count, sends, from_ref, tok_ref, w_ref, *refs):
    outs = refs[1 + count :]
    slope_ref = outs[1]
    stores = outs[2 : 2 + count]
    next_ref = outs[2 + count] if sends else None
    held = outs[-1]
    here = lax.axis_index("section")
    piece = tick - here

    @pl.when(jnp.logical_and(piece >= 0, piece < PIECES))
    def _():
        if tick < PIECES:

            @pl.when(here == 0)
            def _():
                held[...] = tok_ref[tick]

        @pl.when(here > 0)
        def _():
            held[...] = from_ref[...]

        @pl.loop(0, D // WIDE)
        def _(step):
            columns = pl.ds(pl.multiple_of(step * WIDE, WIDE), WIDE)
            forward_columns(columns, held, w_ref, next_ref, slope_ref, piece)

        keep_columns(piece, span, held, stores)


def forward(tick, sections, arrived, tokens, matrix, slopes, stores):
    span = list(range(max(0, tick - sections + 1), min(PIECES - 1, tick) + 1))
    flat = [s for k in span for s in stores[k]]
    count = len(flat)
    sends = tick < PIECES + sections - 2
    outs = pl.pallas_call(
        functools.partial(forward_kernel, tick, span, count, sends),
        out_shape=(
            near(*matrix.shape),
            near(*slopes.shape),
            *[near(*s.shape) for s in flat],
            *[near(PIECE, D)] * sends,
        ),
        in_specs=[VM] * (4 + count),
        out_specs=[VM] * (2 + count + sends),
        scratch_shapes=[pltpu.VMEM((PIECE, D), BF)],
        input_output_aliases={2 + k: k for k in range(2 + count)},
        compiler_params=limit(4),
        cost_estimate=SMALL,
    )(
        resident(arrived),
        resident(tokens),
        resident(matrix),
        resident(slopes),
        *[resident(s) for s in flat],
    )
    stores = list(stores)
    chips = count // len(span)
    for k, index in enumerate(span):
        stores[index] = list(outs[2 + k * chips : 2 + (k + 1) * chips])
    return outs[-1], outs[0], outs[1], stores


def turn_kernel(w_ref, _, out_ref):
    @pl.when(lax.axis_index("section") > 0)
    def _():
        @pl.loop(0, D // LOAD)
        def _(step):
            rows = pl.ds(pl.multiple_of(step * LOAD, LOAD), LOAD)

            @pl.loop(0, D // LOAD)
            def _(other):
                columns = pl.ds(pl.multiple_of(other * LOAD, LOAD), LOAD)
                out_ref[columns, rows] = w_ref[rows, columns].T


def turn(matrix):
    return pl.pallas_call(
        turn_kernel,
        out_shape=(near(*matrix.shape), near(*matrix.shape)),
        in_specs=[VM],
        out_specs=(VM, VM),
        input_output_aliases={0: 0},
        compiler_params=limit(3),
        cost_estimate=SMALL,
    )(resident(matrix))


def backward_kernel(tick, sections, span, late, *refs):
    keeps = len(span)
    refs = refs[late:]
    w_ref, slope_ref = refs[:2]
    chained = tick > sections - 1
    opens = tick - (sections - 1) < PIECES
    cot_ref = refs[2] if opens else None
    from_ref = refs[2 + opens + keeps] if chained else None
    outs = refs[2 + opens + keeps + chained :]
    sends = tick < 2 * (sections - 1) + PIECES - 1
    kept = outs[1 : 1 + keeps]
    next_ref = outs[1 + keeps] if sends else None
    flow, scaled = outs[-2:]
    here = lax.axis_index("section")
    piece = tick - 2 * (sections - 1) + here

    @pl.when(jnp.logical_and(piece >= 0, piece < PIECES))
    def _():
        if opens:

            @pl.when(here == sections - 1)
            def _():
                flow[...] = cot_ref[tick - (sections - 1)]

        if from_ref is not None:

            @pl.when(here < sections - 1)
            def _():
                flow[...] = from_ref[...]

        scaled[...] = (flow[...].astype(F32) * slope_ref[piece].astype(F32)).astype(BF)
        for out, index in zip(kept, span):

            @pl.when(piece == index)
            def _():
                out[...] = scaled[...]

        @pl.when(jnp.logical_and(here > 0, sends))
        def _():
            @pl.loop(0, D // WIDE)
            def _(step):
                part = pl.ds(pl.multiple_of(step * WIDE, WIDE), WIDE)
                back = jnp.dot(scaled[...], w_ref[:, part], preferred_element_type=F32)
                if sends:
                    next_ref[:, part] = (flow[:, part].astype(F32) + back).astype(BF)


def backward(tick, sections, arrived, matrix, slopes, cotangent, kept, after):
    low = max(0, tick - 2 * (sections - 1))
    high = min(PIECES - 1, tick - (sections - 1))
    span = list(range(low, high + 1))
    first = [] if arrived is None else [resident(arrived)]
    sends = tick < 2 * (sections - 1) + PIECES - 1
    opens = [resident(cotangent)] if tick - (sections - 1) < PIECES else []
    base = 2 + len(after) + len(opens)
    out = pl.pallas_call(
        functools.partial(backward_kernel, tick, sections, span, len(after)),
        out_shape=(near(D, D), *[near(PIECE, D)] * (len(span) + sends)),
        in_specs=[HB] * len(after) + [VM] * (2 + len(opens) + len(span) + len(first)),
        out_specs=[VM] * (1 + len(span) + sends),
        scratch_shapes=[pltpu.VMEM((PIECE, D), BF), pltpu.VMEM((PIECE, D), BF)],
        input_output_aliases={
            len(after): 0,
            **{base + k: 1 + k for k in range(len(span))},
        },
        compiler_params=limit(4),
        cost_estimate=SMALL,
    )(
        *after,
        resident(matrix),
        resident(slopes),
        *opens,
        *[resident(kept[k]) for k in span],
        *first,
    )
    kept = list(kept)
    for k, index in enumerate(span):
        kept[index] = out[1 + k]
    return out[-1], out[0], kept


def prepare_kernel(chips, blocks, *refs):
    parts = refs[: chips * PIECES]
    pin_ref, pout_ref, gram_ref, left_ref, right_ref = refs[chips * PIECES : chips * PIECES + 5]
    turned = refs[chips * PIECES + 5 :]
    final = []
    for piece in range(PIECES):
        some = [part[...] for part in parts[piece * chips : (piece + 1) * chips]]
        if piece < PIECES - 2:
            turned[piece][...] = jnp.concatenate(some, axis=0).T
        else:
            turned[piece][...] = jnp.concatenate(some[:-1], axis=0).T
            final.append(some[-1])
    turned[PIECES][...] = jnp.concatenate(final, axis=0).T
    for block in range(2 * blocks):
        rows = slice(block * BLOCK, (block + 1) * BLOCK)
        gram = jnp.zeros((BLOCK, BLOCK), F32)
        for ref in turned:
            some = ref[rows, :]
            gram = gram + contract_last(some, some)
        gram_ref[rows, :] = gram
    for block in range(blocks):
        left_ref[block] = pin_ref[block].astype(BF)
    for block in range(NBLK):
        right_ref[block] = pout_ref[block].astype(BF)


def prepare(parts, inverse_in, inverse_out):
    chips = len(parts[0])
    width = D // chips
    blocks = inverse_in.shape[0]
    flat = [p for piece in parts for p in piece]
    return pl.pallas_call(
        functools.partial(prepare_kernel, chips, blocks),
        out_shape=(
            near(width, BLOCK, kind=F32),
            near(blocks, BLOCK, BLOCK),
            near(NBLK, BLOCK, BLOCK),
            *[near(width, chips * PIECE)] * (PIECES - 2),
            *[near(width, (chips - 1) * PIECE)] * 2,
            near(width, 2 * PIECE),
        ),
        in_specs=[VM] * (len(flat) + 2),
        out_specs=[VM] * (4 + PIECES),
        compiler_params=limit(8),
        cost_estimate=SMALL,
    )(*[resident(p) for p in flat], inverse_in, inverse_out)


def add_gram(every, gram_ref, begins):
    width = gram_ref.shape[0]
    chip = lax.div(lax.axis_index("dp"), 2)
    columns = pl.ds(pl.multiple_of(chip * width, 128), width)
    turned = every[:, columns].T
    for block in range(width // BLOCK):
        rows = slice(block * BLOCK, (block + 1) * BLOCK)
        gram = contract_last(turned[rows], turned[rows])
        gram_ref[rows, :] = gram if begins else gram + gram_ref[rows, :]


def fill(parts, every):
    for k, part in enumerate(parts):
        every[k * PIECE : (k + 1) * PIECE, :] = part[...]


def half_rows(mine, own):
    core = lax.rem(lax.axis_index("dp"), 2)
    return pl.ds(pl.multiple_of((core if mine else 1 - core) * own, 16), own)


def gather_kernel(count, begins, *refs):
    parts = refs[:count]
    xt_ref = refs[count]
    own_ref, other_ref, gram_ref, every = refs[-4:]
    fill(parts, every)
    add_gram(every, gram_ref, begins)
    for mine, acc_ref in ((True, own_ref), (False, other_ref)):
        rows = half_rows(mine, acc_ref.shape[0])

        @pl.loop(0, D // LOAD)
        def _(step):
            columns = pl.ds(pl.multiple_of(step * LOAD, LOAD), LOAD)
            term = jnp.dot(xt_ref[rows, :], every[:, columns], preferred_element_type=F32)
            acc_ref[:, columns] = term if begins else acc_ref[:, columns] + term


def gather(parts, turned, so_far):
    count = len(parts)
    width = turned.shape[0]
    half = near(width // 2, D, kind=F32)
    return pl.pallas_call(
        functools.partial(gather_kernel, count, not so_far),
        out_shape=(half, half, near(width, BLOCK, kind=F32)),
        in_specs=[VM] * (count + 1 + len(so_far)),
        out_specs=(VM, VM, VM),
        scratch_shapes=[pltpu.VMEM((count * PIECE, D), BF)],
        input_output_aliases={count + 1 + k: k for k in range(len(so_far))},
        compiler_params=limit(8),
        cost_estimate=SMALL,
    )(*[resident(p) for p in parts], resident(turned), *[resident(a) for a in so_far])


def other_kernel(first, second, xt_ref, acc_ref, gram_in_ref, gram_ref, _, out_ref, part):
    rows = half_rows(False, acc_ref.shape[0])
    fill((first, second), part)
    add_gram(part, gram_ref, False)
    out_ref[:, D : D + BLOCK] = gram_ref[rows, :].astype(BF)
    out_ref[:, D + SIDE : D + SIDE + BLOCK] = gram_in_ref[rows, :].astype(BF)

    @pl.loop(0, D // LOAD)
    def _(step):
        columns = pl.ds(pl.multiple_of(step * LOAD, LOAD), LOAD)
        term = jnp.dot(xt_ref[rows, :], part[:, columns], preferred_element_type=F32)
        out_ref[:, columns] = (term + acc_ref[:, columns]).astype(BF)


def other_half(parts, turned, acc, gram_in, gram_out):
    width = turned.shape[0]
    return pl.pallas_call(
        other_kernel,
        out_shape=(near(width, BLOCK, kind=F32), near(width // 2, D + 2 * SIDE)),
        in_specs=[VM] * 6,
        out_specs=(VM, VM),
        scratch_shapes=[pltpu.VMEM((2 * PIECE, D), BF)],
        input_output_aliases={5: 0},
        compiler_params=limit(8),
        cost_estimate=SMALL,
    )(
        *[resident(p) for p in parts],
        resident(turned),
        resident(acc),
        resident(gram_in),
        resident(gram_out),
    )


def own_kernel(first, second, xt_ref, acc_ref, out_ref, part):
    rows = half_rows(True, acc_ref.shape[0])
    fill((first, second), part)

    @pl.loop(0, D // LOAD)
    def _(step):
        columns = pl.ds(pl.multiple_of(step * LOAD, LOAD), LOAD)
        term = jnp.dot(xt_ref[rows, :], part[:, columns], preferred_element_type=F32)
        out_ref[:, columns] = term + acc_ref[:, columns]


def own_half(parts, turned, acc):
    return pl.pallas_call(
        own_kernel,
        out_shape=near(*acc.shape, kind=F32),
        in_specs=[VM] * 4,
        out_specs=VM,
        scratch_shapes=[pltpu.VMEM((2 * PIECE, D), BF)],
        input_output_aliases={3: 0},
        compiler_params=limit(8),
        cost_estimate=SMALL,
    )(*[resident(p) for p in parts], resident(turned), resident(acc))


def finish_kernel(blocks, total, own_ref, other_ref, left_ref, right_ref, *refs):
    gram_in_ref, gram_out_ref, update_ref, factor_in_ref, factor_out_ref, ready, sems = refs
    core = lax.rem(lax.axis_index("dp"), 2)
    scale = 1.0 / math.sqrt(total)
    pairs = D // PAIR
    for step in range(D // (2 * PAIR)):
        columns = slice(step * 2 * PAIR, (step + 1) * 2 * PAIR)
        grad = (own_ref[:, columns] + other_ref[:, columns].astype(F32)).astype(BF)
        for block in range(blocks):
            rows = slice(block * BLOCK, (block + 1) * BLOCK)
            ready[rows, columns] = jnp.dot(
                left_ref[block], grad[rows], preferred_element_type=F32
            ).astype(BF)
    copies = []
    for pair in range(pairs):
        for block in (2 * pair, 2 * pair + 1):
            columns = slice(block * BLOCK, (block + 1) * BLOCK)
            right = jnp.dot(ready[:, columns], right_ref[block], preferred_element_type=F32)
            ready[:, columns] = (right * scale).astype(BF)
        if pair % 2:
            columns = slice((pair - 1) * PAIR, (pair + 1) * PAIR)
            copy = pltpu.make_async_copy(
                ready.at[:, columns], update_ref.at[:, columns], sems.at[pair // 2]
            )
            copy.start()
            copies.append(copy)
    for block in range(blocks):
        rows = slice(block * BLOCK, (block + 1) * BLOCK)
        start = pl.multiple_of((core * blocks + block) * BLOCK, BLOCK)
        mine = pl.ds(start, BLOCK)
        factor_out_ref[block] = (
            gram_out_ref[mine, :] + other_ref[rows, D : D + BLOCK].astype(F32)
        ) * (1.0 / total)
        factor_in_ref[block] = (
            gram_in_ref[mine, :] + other_ref[rows, D + SIDE : D + SIDE + BLOCK].astype(F32)
        ) * (1.0 / total)
    for copy in copies:
        copy.wait()


def finish(blocks, total, own, other, left, right, gram_in, gram_out):
    factor = shape(blocks, BLOCK, BLOCK, kind=F32)
    steps = D // (2 * PAIR)
    return pl.pallas_call(
        functools.partial(finish_kernel, blocks, total),
        out_shape=(shape(blocks * BLOCK, D), factor, factor),
        in_specs=[VM] * 6,
        out_specs=(HB, VM, VM),
        scratch_shapes=[
            pltpu.VMEM((blocks * BLOCK, D), BF),
            pltpu.SemaphoreType.DMA((steps,)),
        ],
        compiler_params=limit(8),
        cost_estimate=SMALL,
    )(
        resident(own),
        resident(other),
        resident(left),
        resident(right),
        resident(gram_in),
        resident(gram_out),
    )


def shards(sections, ranks, tokens, cotangent, live_counts, weight, inverse_in, inverse_out):
    total = float(TOK_DEV * ranks)
    chips = ranks // 2
    begun = begin(sections, chips, live_counts, tokens, cotangent, weight[0])
    matrix, ahead, packed_tokens, packed_cot, slopes = begun[:5]
    stores = [list(begun[5 + k * chips : 5 + (k + 1) * chips]) for k in range(PIECES)]
    kept = list(begun[5 + chips * PIECES :])
    behind = None
    parts = []
    crossed = []
    last_turn = 2 * (sections - 1)
    single = [1 << b for b in range(chips.bit_length() - 1)]
    acc = []
    for tick in range(PIECES + last_turn):
        done = tick - last_turn
        known = tick - (sections - 1)
        arrived_ahead = arrived_behind = None
        if 0 < tick < PIECES + sections - 1:
            pairs = [(s - 1, s) for s in range(1, sections) if 0 <= tick - s < PIECES]
            arrived_ahead = lax.ppermute(ahead, "section", pairs)
            ahead, matrix, slopes, stores = forward(
                tick, sections, arrived_ahead, packed_tokens, matrix, slopes, stores
            )
        if tick == sections - 2:
            matrix, turned = turn(matrix)
        if tick > sections - 1:
            pairs = [(s + 1, s) for s in range(sections - 1) if 0 <= tick - last_turn + s < PIECES]
            arrived_behind = lax.ppermute(behind, "section", pairs)
        if tick >= sections - 1:
            after = []
            if 1 <= known <= PIECES:
                after = crossed[known - 1][1:]
            if known == PIECES:
                gram_in, left, right, *rows_turned = prepare(
                    crossed, inverse_in[0], inverse_out[0]
                )
            if 1 <= done == PIECES - 1:
                after = after + [parts[done - 1][o] for o in single]
            if done >= 2:
                acc = gather(parts[done - 2], rows_turned[done - 2], acc)
                after = after + [acc[2]]
            behind, turned, kept = backward(
                tick, sections, arrived_behind, turned, slopes, packed_cot, kept, after
            )
        if 0 <= known < PIECES:
            swapped = [swap(stores[known][o], ranks, 2 * o) for o in range(1, chips)]
            crossed.append([stores[known][0]] + swapped)
        if 0 <= done < PIECES:
            piece = [kept[done]]
            for offset in range(1, chips):
                bit = offset & -offset if done % 2 else 1 << (offset.bit_length() - 1)
                piece.append(swap(piece[offset ^ bit], ranks, 2 * bit))
            parts.append(piece)
    for index in range(PIECES - 2, PIECES):
        acc = gather(parts[index][:-1], rows_turned[index], acc)
    final = [parts[-2][-1], parts[-1][-1]]
    gram_out, other = other_half(final, rows_turned[-1], acc[1], gram_in, acc[2])
    other = swap(other, ranks, 1)
    own = own_half(final, rows_turned[-1], acc[0])
    update, factor_in, factor_out = finish(
        inverse_in.shape[1], total, own, other, left, right, gram_in, gram_out
    )
    return (update[None], factor_in[None], factor_out[None])


def solution(mesh):
    in_specs = (
        P("dp", None),
        P("dp", None),
        P("dp", None),
        P("section", None, None),
        P("section", "dp", None, None),
        P("section", None, None, None),
    )
    out_specs = (
        P("section", "dp", None),
        P("section", "dp", None, None),
        P("section", "dp", None, None),
    )
    body = functools.partial(shards, mesh.shape["section"], mesh.shape["dp"])
    return jax.shard_map(body, mesh=mesh, in_specs=in_specs, out_specs=out_specs, check_vma=False)
```

```python
import functools
import math

import jax
import jax.numpy as jnp
from jax import lax
from jax.experimental import pallas as pl
from jax.experimental.pallas import tpu as pltpu
from jax.sharding import PartitionSpec as P

D = 3072
BLOCK = 192
MICRO = 4
ROWS = 80
TOK_DEV = 320
LIVE = 240
NBLK = 16

PIECE = 80
PIECES = LIVE // PIECE
WIDE = 1024
LOAD = 512
PAIR = 2 * BLOCK
SIDE = 256
FLIGHT = 4

C_ZERO = 0.7978845608028654
C_ONE = 0.044715

BF = jnp.bfloat16
F32 = jnp.float32
VM = pl.BlockSpec(memory_space=pltpu.VMEM)
HB = pl.BlockSpec(memory_space=pl.ANY)
MIB = 1 << 20


def resident(x):
    return pltpu.with_memory_space_constraint(x, pltpu.VMEM)


def distant(x):
    return pltpu.with_memory_space_constraint(x, pltpu.HBM)


SMALL = pl.CostEstimate(flops=1000, bytes_accessed=1000, transcendentals=0)


def shape(*sizes, kind=BF):
    return jax.ShapeDtypeStruct(sizes, kind)


def near(*sizes, kind=BF):
    return pltpu.VMEM(sizes, kind)


def limit(size):
    return pltpu.CompilerParams(vmem_limit_bytes=size * MIB)


def swap(x, ranks, flip):
    return lax.ppermute(x, "dp", [(r, r ^ flip) for r in range(ranks)])


def contract_last(a, b):
    return lax.dot_general(a, b, (((1,), (1,)), ((), ())), preferred_element_type=F32)


def forward_columns(columns, held, w_ref, next_ref, slope_ref, piece):
    pre = jnp.dot(held[...], w_ref[:, columns], preferred_element_type=F32)
    square = pre * pre
    hyper = jnp.tanh(C_ZERO * (pre + C_ONE * pre * square))
    half = 0.5 * (1.0 + hyper)
    if next_ref is not None:
        next_ref[:, columns] = (held[:, columns].astype(F32) + pre * half).astype(BF)
    slope = half + 0.5 * pre * (1.0 - hyper * hyper) * C_ZERO * (1.0 + 3.0 * C_ONE * square)
    slope_ref[piece, :, columns] = slope.astype(BF)


def keep_columns(piece, span, held, stores):
    chips = len(stores) // len(span)
    width = D // chips
    chip = lax.div(lax.axis_index("dp"), 2)
    for k, index in enumerate(span):

        @pl.when(piece == index)
        def _():
            for offset in range(chips):
                columns = pl.ds(pl.multiple_of((chip ^ offset) * width, 128), width)
                stores[k * chips + offset][...] = held[:, columns]


def begin_kernel(sections, chips, counts_ref, tokens_ref, cot_ref, weight_ref, *refs):
    w_ref, next_ref, tok_out, cot_out, slope_ref = refs[:5]
    stores = refs[5 : 5 + chips]
    held, raw, counts, raw_sem, counts_sem, sems = refs[-6:]
    here = lax.axis_index("section")
    loads = [
        pltpu.make_async_copy(
            weight_ref.at[:, pl.ds(k * LOAD, LOAD)], w_ref.at[:, pl.ds(k * LOAD, LOAD)], sems.at[k]
        )
        for k in range(D // LOAD)
    ]
    copy_tokens = pltpu.make_async_copy(tokens_ref, raw, raw_sem)
    copy_cot = pltpu.make_async_copy(cot_ref, raw, raw_sem)
    copy_counts = pltpu.make_async_copy(counts_ref, counts, counts_sem)

    def pack(target):
        row = lax.broadcasted_iota(jnp.int32, (LIVE, TOK_DEV), 0)
        column = lax.broadcasted_iota(jnp.int32, (LIVE, TOK_DEV), 1)
        origin = row
        edge = jnp.int32(0)
        for micro in range(MICRO):
            count = counts[0, micro]
            edge = edge + count
            origin = origin + jnp.where(row >= edge, ROWS - count, 0)
        pick = (column == origin).astype(F32).astype(BF)
        for start in range(0, D, WIDE):
            part = jnp.dot(
                pick, raw[:, start : start + WIDE], preferred_element_type=F32
            ).astype(BF)
            for piece in range(PIECES):
                target[piece, :, start : start + WIDE] = part[piece * PIECE : (piece + 1) * PIECE]

    @pl.when(here == 0)
    def _():
        copy_counts.start()
        copy_tokens.start()
        for load in loads[:2]:
            load.start()
        copy_counts.wait()
        copy_tokens.wait()

    @pl.when(here > 0)
    def _():
        for load in loads[:2]:
            load.start()

    for load in loads[2:FLIGHT]:
        load.start()

    @pl.when(here == 0)
    def _():
        pack(tok_out)
        held[...] = tok_out[0]

    for k, load in enumerate(loads):
        load.wait()
        if k + FLIGHT < len(loads):
            loads[k + FLIGHT].start()

        @pl.when(here == 0)
        def _():
            forward_columns(pl.ds(k * LOAD, LOAD), held, w_ref, next_ref, slope_ref, 0)

    @pl.when(here == 0)
    def _():
        keep_columns(0, [0], held, stores)

    @pl.when(jnp.logical_and(here == sections - 1, sections > 1))
    def _():
        copy_counts.start()
        copy_cot.start()
        copy_counts.wait()
        copy_cot.wait()
        pack(cot_out)


def begin(sections, chips, counts, tokens, cotangent, matrix):
    packed = near(PIECES, PIECE, D)
    return pl.pallas_call(
        functools.partial(begin_kernel, sections, chips),
        out_shape=(
            near(D, D),
            near(PIECE, D),
            packed,
            packed,
            near(PIECES, PIECE, D),
            *[near(PIECE, D // chips)] * (chips * PIECES),
            *[near(PIECE, D)] * PIECES,
        ),
        in_specs=[HB] * 4,
        out_specs=[VM] * (5 + chips) + [HB] * (chips * (PIECES - 1) + PIECES),
        scratch_shapes=[
            pltpu.VMEM((PIECE, D), BF),
            pltpu.VMEM((TOK_DEV, D), BF),
            pltpu.SMEM((1, MICRO), jnp.int32),
            pltpu.SemaphoreType.DMA,
            pltpu.SemaphoreType.DMA,
            pltpu.SemaphoreType.DMA((D // LOAD,)),
        ],
        compiler_params=limit(8),
        cost_estimate=SMALL,
    )(distant(counts), distant(tokens), distant(cotangent), distant(matrix))


def forward_kernel(tick, span, count, sends, from_ref, tok_ref, w_ref, *refs):
    outs = refs[1 + count :]
    slope_ref = outs[1]
    stores = outs[2 : 2 + count]
    next_ref = outs[2 + count] if sends else None
    held = outs[-1]
    here = lax.axis_index("section")
    piece = tick - here

    @pl.when(jnp.logical_and(piece >= 0, piece < PIECES))
    def _():
        if tick < PIECES:

            @pl.when(here == 0)
            def _():
                held[...] = tok_ref[tick]

        @pl.when(here > 0)
        def _():
            held[...] = from_ref[...]

        @pl.loop(0, D // WIDE)
        def _(step):
            columns = pl.ds(pl.multiple_of(step * WIDE, WIDE), WIDE)
            forward_columns(columns, held, w_ref, next_ref, slope_ref, piece)

        keep_columns(piece, span, held, stores)


def forward(tick, sections, arrived, tokens, matrix, slopes, stores):
    span = list(range(max(0, tick - sections + 1), min(PIECES - 1, tick) + 1))
    flat = [s for k in span for s in stores[k]]
    count = len(flat)
    sends = tick < PIECES + sections - 2
    outs = pl.pallas_call(
        functools.partial(forward_kernel, tick, span, count, sends),
        out_shape=(
            near(*matrix.shape),
            near(*slopes.shape),
            *[near(*s.shape) for s in flat],
            *[near(PIECE, D)] * sends,
        ),
        in_specs=[VM] * (4 + count),
        out_specs=[VM] * (2 + count + sends),
        scratch_shapes=[pltpu.VMEM((PIECE, D), BF)],
        input_output_aliases={2 + k: k for k in range(2 + count)},
        compiler_params=limit(4),
        cost_estimate=SMALL,
    )(
        resident(arrived),
        resident(tokens),
        resident(matrix),
        resident(slopes),
        *[resident(s) for s in flat],
    )
    stores = list(stores)
    chips = count // len(span)
    for k, index in enumerate(span):
        stores[index] = list(outs[2 + k * chips : 2 + (k + 1) * chips])
    return outs[-1], outs[0], outs[1], stores


def turn_kernel(w_ref, _, out_ref):
    @pl.when(lax.axis_index("section") > 0)
    def _():
        @pl.loop(0, D // LOAD)
        def _(step):
            rows = pl.ds(pl.multiple_of(step * LOAD, LOAD), LOAD)

            @pl.loop(0, D // LOAD)
            def _(other):
                columns = pl.ds(pl.multiple_of(other * LOAD, LOAD), LOAD)
                out_ref[columns, rows] = w_ref[rows, columns].T


def turn(matrix):
    return pl.pallas_call(
        turn_kernel,
        out_shape=(near(*matrix.shape), near(*matrix.shape)),
        in_specs=[VM],
        out_specs=(VM, VM),
        input_output_aliases={0: 0},
        compiler_params=limit(3),
        cost_estimate=SMALL,
    )(resident(matrix))


def backward_kernel(tick, sections, span, late, *refs):
    keeps = len(span)
    refs = refs[late:]
    w_ref, slope_ref = refs[:2]
    chained = tick > sections - 1
    opens = tick - (sections - 1) < PIECES
    cot_ref = refs[2] if opens else None
    from_ref = refs[2 + opens + keeps] if chained else None
    outs = refs[2 + opens + keeps + chained :]
    sends = tick < 2 * (sections - 1) + PIECES - 1
    kept = outs[1 : 1 + keeps]
    next_ref = outs[1 + keeps] if sends else None
    flow, scaled = outs[-2:]
    here = lax.axis_index("section")
    piece = tick - 2 * (sections - 1) + here

    @pl.when(jnp.logical_and(piece >= 0, piece < PIECES))
    def _():
        if opens:

            @pl.when(here == sections - 1)
            def _():
                flow[...] = cot_ref[tick - (sections - 1)]

        if from_ref is not None:

            @pl.when(here < sections - 1)
            def _():
                flow[...] = from_ref[...]

        scaled[...] = (flow[...].astype(F32) * slope_ref[piece].astype(F32)).astype(BF)
        for out, index in zip(kept, span):

            @pl.when(piece == index)
            def _():
                out[...] = scaled[...]

        @pl.when(jnp.logical_and(here > 0, sends))
        def _():
            @pl.loop(0, D // WIDE)
            def _(step):
                part = pl.ds(pl.multiple_of(step * WIDE, WIDE), WIDE)
                back = jnp.dot(scaled[...], w_ref[:, part], preferred_element_type=F32)
                if sends:
                    next_ref[:, part] = (flow[:, part].astype(F32) + back).astype(BF)


def backward(tick, sections, arrived, matrix, slopes, cotangent, kept, after):
    low = max(0, tick - 2 * (sections - 1))
    high = min(PIECES - 1, tick - (sections - 1))
    span = list(range(low, high + 1))
    first = [] if arrived is None else [resident(arrived)]
    sends = tick < 2 * (sections - 1) + PIECES - 1
    opens = [resident(cotangent)] if tick - (sections - 1) < PIECES else []
    base = 2 + len(after) + len(opens)
    out = pl.pallas_call(
        functools.partial(backward_kernel, tick, sections, span, len(after)),
        out_shape=(near(D, D), *[near(PIECE, D)] * (len(span) + sends)),
        in_specs=[HB] * len(after) + [VM] * (2 + len(opens) + len(span) + len(first)),
        out_specs=[VM] * (1 + len(span) + sends),
        scratch_shapes=[pltpu.VMEM((PIECE, D), BF), pltpu.VMEM((PIECE, D), BF)],
        input_output_aliases={
            len(after): 0,
            **{base + k: 1 + k for k in range(len(span))},
        },
        compiler_params=limit(4),
        cost_estimate=SMALL,
    )(
        *after,
        resident(matrix),
        resident(slopes),
        *opens,
        *[resident(kept[k]) for k in span],
        *first,
    )
    kept = list(kept)
    for k, index in enumerate(span):
        kept[index] = out[1 + k]
    return out[-1], out[0], kept


def prepare_kernel(chips, blocks, *refs):
    parts = refs[: chips * PIECES]
    pin_ref, pout_ref, gram_ref, left_ref, right_ref = refs[chips * PIECES : chips * PIECES + 5]
    turned = refs[chips * PIECES + 5 :]
    final = []
    for piece in range(PIECES):
        some = [part[...] for part in parts[piece * chips : (piece + 1) * chips]]
        if piece < PIECES - 2:
            turned[piece][...] = jnp.concatenate(some, axis=0).T
        else:
            turned[piece][...] = jnp.concatenate(some[:-1], axis=0).T
            final.append(some[-1])
    turned[PIECES][...] = jnp.concatenate(final, axis=0).T
    for block in range(2 * blocks):
        rows = slice(block * BLOCK, (block + 1) * BLOCK)
        gram = jnp.zeros((BLOCK, BLOCK), F32)
        for ref in turned:
            some = ref[rows, :]
            gram = gram + contract_last(some, some)
        gram_ref[rows, :] = gram
    for block in range(blocks):
        left_ref[block] = pin_ref[block].astype(BF)
    row = lax.broadcasted_iota(jnp.int32, (BLOCK, PAIR), 0)
    column = lax.broadcasted_iota(jnp.int32, (BLOCK, PAIR), 1)

    @pl.loop(0, NBLK // 2)
    def _(pair):
        for side in range(2):
            place = (column == row + side * BLOCK).astype(F32).astype(BF)
            wide = jnp.dot(pout_ref[2 * pair + side].astype(BF), place, preferred_element_type=F32)
            right_ref[pair, side * BLOCK : (side + 1) * BLOCK, :] = wide.astype(BF)


def prepare(parts, inverse_in, inverse_out):
    chips = len(parts[0])
    width = D // chips
    blocks = inverse_in.shape[0]
    flat = [p for piece in parts for p in piece]
    return pl.pallas_call(
        functools.partial(prepare_kernel, chips, blocks),
        out_shape=(
            near(width, BLOCK, kind=F32),
            near(blocks, BLOCK, BLOCK),
            near(NBLK // 2, PAIR, PAIR),
            *[near(width, chips * PIECE)] * (PIECES - 2),
            *[near(width, (chips - 1) * PIECE)] * 2,
            near(width, 2 * PIECE),
        ),
        in_specs=[VM] * (len(flat) + 2),
        out_specs=[VM] * (4 + PIECES),
        compiler_params=limit(8),
        cost_estimate=SMALL,
    )(*[resident(p) for p in flat], inverse_in, inverse_out)


def add_gram(every, gram_ref, begins):
    width = gram_ref.shape[0]
    chip = lax.div(lax.axis_index("dp"), 2)
    columns = pl.ds(pl.multiple_of(chip * width, 128), width)
    turned = every[:, columns].T
    for block in range(width // BLOCK):
        rows = slice(block * BLOCK, (block + 1) * BLOCK)
        gram = contract_last(turned[rows], turned[rows])
        gram_ref[rows, :] = gram if begins else gram + gram_ref[rows, :]


def fill(parts, every):
    for k, part in enumerate(parts):
        every[k * PIECE : (k + 1) * PIECE, :] = part[...]


def half_rows(mine, own):
    core = lax.rem(lax.axis_index("dp"), 2)
    return pl.ds(pl.multiple_of((core if mine else 1 - core) * own, 16), own)


def gather_kernel(count, begins, *refs):
    parts = refs[:count]
    xt_ref = refs[count]
    own_ref, other_ref, gram_ref, every = refs[-4:]
    fill(parts, every)
    add_gram(every, gram_ref, begins)
    for mine, acc_ref in ((True, own_ref), (False, other_ref)):
        rows = half_rows(mine, acc_ref.shape[0])

        @pl.loop(0, D // LOAD)
        def _(step):
            columns = pl.ds(pl.multiple_of(step * LOAD, LOAD), LOAD)
            term = jnp.dot(xt_ref[rows, :], every[:, columns], preferred_element_type=F32)
            acc_ref[:, columns] = term if begins else acc_ref[:, columns] + term


def gather(parts, turned, so_far):
    count = len(parts)
    width = turned.shape[0]
    half = near(width // 2, D, kind=F32)
    return pl.pallas_call(
        functools.partial(gather_kernel, count, not so_far),
        out_shape=(half, half, near(width, BLOCK, kind=F32)),
        in_specs=[VM] * (count + 1 + len(so_far)),
        out_specs=(VM, VM, VM),
        scratch_shapes=[pltpu.VMEM((count * PIECE, D), BF)],
        input_output_aliases={count + 1 + k: k for k in range(len(so_far))},
        compiler_params=limit(8),
        cost_estimate=SMALL,
    )(*[resident(p) for p in parts], resident(turned), *[resident(a) for a in so_far])


def other_kernel(first, second, xt_ref, acc_ref, gram_in_ref, gram_ref, _, out_ref, part):
    rows = half_rows(False, acc_ref.shape[0])
    fill((first, second), part)
    add_gram(part, gram_ref, False)
    out_ref[:, D : D + BLOCK] = gram_ref[rows, :].astype(BF)
    out_ref[:, D + SIDE : D + SIDE + BLOCK] = gram_in_ref[rows, :].astype(BF)

    @pl.loop(0, D // LOAD)
    def _(step):
        columns = pl.ds(pl.multiple_of(step * LOAD, LOAD), LOAD)
        term = jnp.dot(xt_ref[rows, :], part[:, columns], preferred_element_type=F32)
        out_ref[:, columns] = (term + acc_ref[:, columns]).astype(BF)


def other_half(parts, turned, acc, gram_in, gram_out):
    width = turned.shape[0]
    return pl.pallas_call(
        other_kernel,
        out_shape=(near(width, BLOCK, kind=F32), near(width // 2, D + 2 * SIDE)),
        in_specs=[VM] * 6,
        out_specs=(VM, VM),
        scratch_shapes=[pltpu.VMEM((2 * PIECE, D), BF)],
        input_output_aliases={5: 0},
        compiler_params=limit(8),
        cost_estimate=SMALL,
    )(
        *[resident(p) for p in parts],
        resident(turned),
        resident(acc),
        resident(gram_in),
        resident(gram_out),
    )


def own_kernel(first, second, xt_ref, acc_ref, out_ref, part):
    rows = half_rows(True, acc_ref.shape[0])
    fill((first, second), part)

    @pl.loop(0, D // LOAD)
    def _(step):
        columns = pl.ds(pl.multiple_of(step * LOAD, LOAD), LOAD)
        term = jnp.dot(xt_ref[rows, :], part[:, columns], preferred_element_type=F32)
        out_ref[:, columns] = term + acc_ref[:, columns]


def own_half(parts, turned, acc):
    return pl.pallas_call(
        own_kernel,
        out_shape=near(*acc.shape, kind=F32),
        in_specs=[VM] * 4,
        out_specs=VM,
        scratch_shapes=[pltpu.VMEM((2 * PIECE, D), BF)],
        input_output_aliases={3: 0},
        compiler_params=limit(8),
        cost_estimate=SMALL,
    )(*[resident(p) for p in parts], resident(turned), resident(acc))


def finish_kernel(blocks, total, own_ref, other_ref, left_ref, right_ref, *refs):
    gram_in_ref, gram_out_ref, update_ref, factor_in_ref, factor_out_ref, ready, grams, sems = refs
    core = lax.rem(lax.axis_index("dp"), 2)
    scale = 1.0 / math.sqrt(total)
    pairs = D // PAIR
    copies = []
    for block in range(blocks):
        rows = slice(block * BLOCK, (block + 1) * BLOCK)
        start = pl.multiple_of((core * blocks + block) * BLOCK, BLOCK)
        mine = pl.ds(start, BLOCK)
        grams[1, block] = (
            gram_out_ref[mine, :] + other_ref[rows, D : D + BLOCK].astype(F32)
        ) * (1.0 / total)
        grams[0, block] = (
            gram_in_ref[mine, :] + other_ref[rows, D + SIDE : D + SIDE + BLOCK].astype(F32)
        ) * (1.0 / total)
    for k, ref in enumerate((factor_in_ref, factor_out_ref)):
        copy = pltpu.make_async_copy(grams.at[k], ref, sems.at[pairs + k])
        copy.start()
        copies.append(copy)
    for step in range(D // (2 * PAIR)):
        columns = slice(step * 2 * PAIR, (step + 1) * 2 * PAIR)
        grad = (own_ref[:, columns] + other_ref[:, columns].astype(F32)).astype(BF)
        for block in range(blocks):
            rows = slice(block * BLOCK, (block + 1) * BLOCK)
            ready[rows, columns] = jnp.dot(
                left_ref[block], grad[rows], preferred_element_type=F32
            ).astype(BF)
    for pair in range(pairs):
        columns = slice(pair * PAIR, (pair + 1) * PAIR)
        right = jnp.dot(ready[:, columns], right_ref[pair], preferred_element_type=F32)
        ready[:, columns] = (right * scale).astype(BF)
        copy = pltpu.make_async_copy(
            ready.at[:, columns], update_ref.at[:, columns], sems.at[pair]
        )
        copy.start()
        copies.append(copy)
    for copy in copies:
        copy.wait()


def finish(blocks, total, own, other, left, right, gram_in, gram_out):
    factor = shape(blocks, BLOCK, BLOCK, kind=F32)
    return pl.pallas_call(
        functools.partial(finish_kernel, blocks, total),
        out_shape=(shape(blocks * BLOCK, D), factor, factor),
        in_specs=[VM] * 6,
        out_specs=(HB, HB, HB),
        scratch_shapes=[
            pltpu.VMEM((blocks * BLOCK, D), BF),
            pltpu.VMEM((2, blocks, BLOCK, BLOCK), F32),
            pltpu.SemaphoreType.DMA((D // PAIR + 2,)),
        ],
        compiler_params=limit(8),
        cost_estimate=SMALL,
    )(
        resident(own),
        resident(other),
        resident(left),
        resident(right),
        resident(gram_in),
        resident(gram_out),
    )


def shards(sections, ranks, tokens, cotangent, live_counts, weight, inverse_in, inverse_out):
    total = float(TOK_DEV * ranks)
    chips = ranks // 2
    begun = begin(sections, chips, live_counts, tokens, cotangent, weight[0])
    matrix, ahead, packed_tokens, packed_cot, slopes = begun[:5]
    stores = [list(begun[5 + k * chips : 5 + (k + 1) * chips]) for k in range(PIECES)]
    kept = list(begun[5 + chips * PIECES :])
    behind = None
    parts = []
    crossed = []
    last_turn = 2 * (sections - 1)
    single = [1 << b for b in range(chips.bit_length() - 1)]
    acc = []
    for tick in range(PIECES + last_turn):
        done = tick - last_turn
        known = tick - (sections - 1)
        arrived_ahead = arrived_behind = None
        if 0 < tick < PIECES + sections - 1:
            pairs = [(s - 1, s) for s in range(1, sections) if 0 <= tick - s < PIECES]
            arrived_ahead = lax.ppermute(ahead, "section", pairs)
            ahead, matrix, slopes, stores = forward(
                tick, sections, arrived_ahead, packed_tokens, matrix, slopes, stores
            )
        if tick == sections - 2:
            matrix, turned = turn(matrix)
        if tick > sections - 1:
            pairs = [(s + 1, s) for s in range(sections - 1) if 0 <= tick - last_turn + s < PIECES]
            arrived_behind = lax.ppermute(behind, "section", pairs)
        if tick >= sections - 1:
            after = []
            if 1 <= known <= PIECES:
                after = crossed[known - 1][1:]
            if known == PIECES:
                gram_in, left, right, *rows_turned = prepare(
                    crossed, inverse_in[0], inverse_out[0]
                )
            if 1 <= done == PIECES - 1:
                after = after + [parts[done - 1][o] for o in single]
            if done >= 2:
                acc = gather(parts[done - 2], rows_turned[done - 2], acc)
                after = after + [acc[2]]
            behind, turned, kept = backward(
                tick, sections, arrived_behind, turned, slopes, packed_cot, kept, after
            )
        if 0 <= known < PIECES:
            swapped = [swap(stores[known][o], ranks, 2 * o) for o in range(1, chips)]
            crossed.append([stores[known][0]] + swapped)
        if 0 <= done < PIECES:
            piece = [kept[done]]
            for offset in range(1, chips):
                bit = offset & -offset if done % 2 else 1 << (offset.bit_length() - 1)
                piece.append(swap(piece[offset ^ bit], ranks, 2 * bit))
            parts.append(piece)
    for index in range(PIECES - 2, PIECES):
        acc = gather(parts[index][:-1], rows_turned[index], acc)
    final = [parts[-2][-1], parts[-1][-1]]
    gram_out, other = other_half(final, rows_turned[-1], acc[1], gram_in, acc[2])
    other = swap(other, ranks, 1)
    own = own_half(final, rows_turned[-1], acc[0])
    update, factor_in, factor_out = finish(
        inverse_in.shape[1], total, own, other, left, right, gram_in, gram_out
    )
    return (update[None], factor_in[None], factor_out[None])


def solution(mesh):
    in_specs = (
        P("dp", None),
        P("dp", None),
        P("dp", None),
        P("section", None, None),
        P("section", "dp", None, None),
        P("section", None, None, None),
    )
    out_specs = (
        P("section", "dp", None),
        P("section", "dp", None, None),
        P("section", "dp", None, None),
    )
    body = functools.partial(shards, mesh.shape["section"], mesh.shape["dp"])
    return jax.shard_map(body, mesh=mesh, in_specs=in_specs, out_specs=out_specs, check_vma=False)
```

```python
import functools
import math

import jax
import jax.numpy as jnp
from jax import lax
from jax.experimental import pallas as pl
from jax.experimental.pallas import tpu as pltpu
from jax.sharding import PartitionSpec as P

D = 3072
BLOCK = 192
MICRO = 4
ROWS = 80
TOK_DEV = 320
LIVE = 240
NBLK = 16

PIECE = 80
PIECES = LIVE // PIECE
WIDE = 1024
LOAD = 512
PAIR = 2 * BLOCK
SIDE = 256
FLIGHT = 4

C_ZERO = 0.7978845608028654
C_ONE = 0.044715

BF = jnp.bfloat16
F32 = jnp.float32
VM = pl.BlockSpec(memory_space=pltpu.VMEM)
HB = pl.BlockSpec(memory_space=pl.ANY)
MIB = 1 << 20


def resident(x):
    return pltpu.with_memory_space_constraint(x, pltpu.VMEM)


def distant(x):
    return pltpu.with_memory_space_constraint(x, pltpu.HBM)


SMALL = pl.CostEstimate(flops=1000, bytes_accessed=1000, transcendentals=0)


def shape(*sizes, kind=BF):
    return jax.ShapeDtypeStruct(sizes, kind)


def near(*sizes, kind=BF):
    return pltpu.VMEM(sizes, kind)


def limit(size):
    return pltpu.CompilerParams(vmem_limit_bytes=size * MIB)


def swap(x, ranks, flip):
    return lax.ppermute(x, "dp", [(r, r ^ flip) for r in range(ranks)])


def contract_last(a, b):
    return lax.dot_general(a, b, (((1,), (1,)), ((), ())), preferred_element_type=F32)


def forward_columns(columns, held, w_ref, next_ref, slope_ref, piece):
    pre = jnp.dot(held[...], w_ref[:, columns], preferred_element_type=F32)
    square = pre * pre
    hyper = jnp.tanh(C_ZERO * (pre + C_ONE * pre * square))
    half = 0.5 * (1.0 + hyper)
    if next_ref is not None:
        next_ref[:, columns] = (held[:, columns].astype(F32) + pre * half).astype(BF)
    slope = half + 0.5 * pre * (1.0 - hyper * hyper) * C_ZERO * (1.0 + 3.0 * C_ONE * square)
    slope_ref[piece, :, columns] = slope.astype(BF)


def keep_columns(piece, span, held, stores):
    chips = len(stores) // len(span)
    width = D // chips
    chip = lax.div(lax.axis_index("dp"), 2)
    for k, index in enumerate(span):

        @pl.when(piece == index)
        def _():
            for offset in range(chips):
                columns = pl.ds(pl.multiple_of((chip ^ offset) * width, 128), width)
                stores[k * chips + offset][...] = held[:, columns]


def begin_kernel(sections, chips, counts_ref, tokens_ref, cot_ref, weight_ref, *refs):
    w_ref, next_ref, tok_out, cot_out, slope_ref = refs[:5]
    stores = refs[5 : 5 + chips]
    held, raw, counts, raw_sem, counts_sem, sems = refs[-6:]
    here = lax.axis_index("section")
    loads = [
        pltpu.make_async_copy(
            weight_ref.at[:, pl.ds(k * LOAD, LOAD)], w_ref.at[:, pl.ds(k * LOAD, LOAD)], sems.at[k]
        )
        for k in range(D // LOAD)
    ]
    copy_tokens = pltpu.make_async_copy(tokens_ref, raw, raw_sem)
    copy_cot = pltpu.make_async_copy(cot_ref, raw, raw_sem)
    copy_counts = pltpu.make_async_copy(counts_ref, counts, counts_sem)

    def pack(target):
        row = lax.broadcasted_iota(jnp.int32, (LIVE, TOK_DEV), 0)
        column = lax.broadcasted_iota(jnp.int32, (LIVE, TOK_DEV), 1)
        origin = row
        edge = jnp.int32(0)
        for micro in range(MICRO):
            count = counts[0, micro]
            edge = edge + count
            origin = origin + jnp.where(row >= edge, ROWS - count, 0)
        pick = (column == origin).astype(F32).astype(BF)
        for start in range(0, D, WIDE):
            part = jnp.dot(
                pick, raw[:, start : start + WIDE], preferred_element_type=F32
            ).astype(BF)
            for piece in range(PIECES):
                target[piece, :, start : start + WIDE] = part[piece * PIECE : (piece + 1) * PIECE]

    @pl.when(here == 0)
    def _():
        copy_counts.start()
        copy_tokens.start()
        for load in loads[:2]:
            load.start()
        copy_counts.wait()
        copy_tokens.wait()
        for load in loads[2:FLIGHT]:
            load.start()
        pack(tok_out)
        held[...] = tok_out[0]
        for k, load in enumerate(loads):
            load.wait()
            if k + FLIGHT < len(loads):
                loads[k + FLIGHT].start()
            forward_columns(pl.ds(k * LOAD, LOAD), held, w_ref, next_ref, slope_ref, 0)
        keep_columns(0, [0], held, stores)

    @pl.when(here > 0)
    def _():
        blocks = [
            pltpu.make_async_copy(
                weight_ref.at[pl.ds(k * LOAD, LOAD)], w_ref.at[pl.ds(k * LOAD, LOAD)], sems.at[k]
            )
            for k in range(D // LOAD)
        ]
        for block in blocks:
            block.start()
        for block in blocks:
            block.wait()

    @pl.when(jnp.logical_and(here == sections - 1, sections > 1))
    def _():
        copy_counts.start()
        copy_cot.start()
        copy_counts.wait()
        copy_cot.wait()
        pack(cot_out)


def begin(sections, chips, counts, tokens, cotangent, matrix):
    packed = near(PIECES, PIECE, D)
    return pl.pallas_call(
        functools.partial(begin_kernel, sections, chips),
        out_shape=(
            near(D, D),
            near(PIECE, D),
            packed,
            packed,
            near(PIECES, PIECE, D),
            *[near(PIECE, D // chips)] * (chips * PIECES),
            *[near(PIECE, D)] * PIECES,
        ),
        in_specs=[HB] * 4,
        out_specs=[VM] * (5 + chips) + [HB] * (chips * (PIECES - 1) + PIECES),
        scratch_shapes=[
            pltpu.VMEM((PIECE, D), BF),
            pltpu.VMEM((TOK_DEV, D), BF),
            pltpu.SMEM((1, MICRO), jnp.int32),
            pltpu.SemaphoreType.DMA,
            pltpu.SemaphoreType.DMA,
            pltpu.SemaphoreType.DMA((D // LOAD,)),
        ],
        compiler_params=limit(8),
        cost_estimate=SMALL,
    )(distant(counts), distant(tokens), distant(cotangent), distant(matrix))


def forward_kernel(tick, span, count, sends, from_ref, tok_ref, w_ref, *refs):
    outs = refs[1 + count :]
    slope_ref = outs[1]
    stores = outs[2 : 2 + count]
    next_ref = outs[2 + count] if sends else None
    held = outs[-1]
    here = lax.axis_index("section")
    piece = tick - here

    @pl.when(jnp.logical_and(piece >= 0, piece < PIECES))
    def _():
        if tick < PIECES:

            @pl.when(here == 0)
            def _():
                held[...] = tok_ref[tick]

        @pl.when(here > 0)
        def _():
            held[...] = from_ref[...]

        @pl.loop(0, D // WIDE)
        def _(step):
            columns = pl.ds(pl.multiple_of(step * WIDE, WIDE), WIDE)
            forward_columns(columns, held, w_ref, next_ref, slope_ref, piece)

        keep_columns(piece, span, held, stores)


def forward(tick, sections, arrived, tokens, matrix, slopes, stores):
    span = list(range(max(0, tick - sections + 1), min(PIECES - 1, tick) + 1))
    flat = [s for k in span for s in stores[k]]
    count = len(flat)
    sends = tick < PIECES + sections - 2
    outs = pl.pallas_call(
        functools.partial(forward_kernel, tick, span, count, sends),
        out_shape=(
            near(*matrix.shape),
            near(*slopes.shape),
            *[near(*s.shape) for s in flat],
            *[near(PIECE, D)] * sends,
        ),
        in_specs=[VM] * (4 + count),
        out_specs=[VM] * (2 + count + sends),
        scratch_shapes=[pltpu.VMEM((PIECE, D), BF)],
        input_output_aliases={2 + k: k for k in range(2 + count)},
        compiler_params=limit(4),
        cost_estimate=SMALL,
    )(
        resident(arrived),
        resident(tokens),
        resident(matrix),
        resident(slopes),
        *[resident(s) for s in flat],
    )
    stores = list(stores)
    chips = count // len(span)
    for k, index in enumerate(span):
        stores[index] = list(outs[2 + k * chips : 2 + (k + 1) * chips])
    return outs[-1], outs[0], outs[1], stores


def turn_kernel(w_ref, _, out_ref):
    @pl.when(lax.axis_index("section") > 0)
    def _():
        @pl.loop(0, D // LOAD)
        def _(step):
            rows = pl.ds(pl.multiple_of(step * LOAD, LOAD), LOAD)

            @pl.loop(0, D // LOAD)
            def _(other):
                columns = pl.ds(pl.multiple_of(other * LOAD, LOAD), LOAD)
                out_ref[columns, rows] = w_ref[rows, columns].T


def turn(matrix):
    return pl.pallas_call(
        turn_kernel,
        out_shape=(near(*matrix.shape), near(*matrix.shape)),
        in_specs=[VM],
        out_specs=(VM, VM),
        input_output_aliases={0: 0},
        compiler_params=limit(3),
        cost_estimate=SMALL,
    )(resident(matrix))


def backward_kernel(tick, sections, span, late, *refs):
    keeps = len(span)
    refs = refs[late:]
    w_ref, slope_ref = refs[:2]
    chained = tick > sections - 1
    opens = tick - (sections - 1) < PIECES
    cot_ref = refs[2] if opens else None
    from_ref = refs[2 + opens + keeps] if chained else None
    outs = refs[2 + opens + keeps + chained :]
    sends = tick < 2 * (sections - 1) + PIECES - 1
    kept = outs[1 : 1 + keeps]
    next_ref = outs[1 + keeps] if sends else None
    flow, scaled = outs[-2:]
    here = lax.axis_index("section")
    piece = tick - 2 * (sections - 1) + here

    @pl.when(jnp.logical_and(piece >= 0, piece < PIECES))
    def _():
        if opens:

            @pl.when(here == sections - 1)
            def _():
                flow[...] = cot_ref[tick - (sections - 1)]

        if from_ref is not None:

            @pl.when(here < sections - 1)
            def _():
                flow[...] = from_ref[...]

        scaled[...] = (flow[...].astype(F32) * slope_ref[piece].astype(F32)).astype(BF)
        for out, index in zip(kept, span):

            @pl.when(piece == index)
            def _():
                out[...] = scaled[...]

        @pl.when(jnp.logical_and(here > 0, sends))
        def _():
            @pl.loop(0, D // WIDE)
            def _(step):
                part = pl.ds(pl.multiple_of(step * WIDE, WIDE), WIDE)
                back = jnp.dot(scaled[...], w_ref[:, part], preferred_element_type=F32)
                if sends:
                    next_ref[:, part] = (flow[:, part].astype(F32) + back).astype(BF)


def backward(tick, sections, arrived, matrix, slopes, cotangent, kept, after):
    low = max(0, tick - 2 * (sections - 1))
    high = min(PIECES - 1, tick - (sections - 1))
    span = list(range(low, high + 1))
    first = [] if arrived is None else [resident(arrived)]
    sends = tick < 2 * (sections - 1) + PIECES - 1
    opens = [resident(cotangent)] if tick - (sections - 1) < PIECES else []
    base = 2 + len(after) + len(opens)
    out = pl.pallas_call(
        functools.partial(backward_kernel, tick, sections, span, len(after)),
        out_shape=(near(D, D), *[near(PIECE, D)] * (len(span) + sends)),
        in_specs=[HB] * len(after) + [VM] * (2 + len(opens) + len(span) + len(first)),
        out_specs=[VM] * (1 + len(span) + sends),
        scratch_shapes=[pltpu.VMEM((PIECE, D), BF), pltpu.VMEM((PIECE, D), BF)],
        input_output_aliases={
            len(after): 0,
            **{base + k: 1 + k for k in range(len(span))},
        },
        compiler_params=limit(4),
        cost_estimate=SMALL,
    )(
        *after,
        resident(matrix),
        resident(slopes),
        *opens,
        *[resident(kept[k]) for k in span],
        *first,
    )
    kept = list(kept)
    for k, index in enumerate(span):
        kept[index] = out[1 + k]
    return out[-1], out[0], kept


def prepare_kernel(chips, blocks, *refs):
    parts = refs[: chips * PIECES]
    pin_ref, pout_ref, gram_ref, left_ref, right_ref = refs[chips * PIECES : chips * PIECES + 5]
    turned = refs[chips * PIECES + 5 :]
    final = []
    width = gram_ref.shape[0]

    def keep(ref, some):
        columns = jnp.concatenate(some, axis=0).T
        for block in range(width // BLOCK):
            rows = slice(block * BLOCK, (block + 1) * BLOCK)
            ref[own_first(block * BLOCK, width // 2), :] = columns[rows]

    for piece in range(PIECES):
        some = [part[...] for part in parts[piece * chips : (piece + 1) * chips]]
        if piece < PIECES - 2:
            keep(turned[piece], some)
        else:
            keep(turned[piece], some[:-1])
            final.append(some[-1])
    keep(turned[PIECES], final)
    for block in range(2 * blocks):
        rows = slice(block * BLOCK, (block + 1) * BLOCK)
        gram = jnp.zeros((BLOCK, BLOCK), F32)
        for ref in turned:
            some = ref[rows, :]
            gram = gram + contract_last(some, some)
        gram_ref[rows, :] = gram
    for block in range(blocks):
        left_ref[block] = pin_ref[block].astype(BF)
    row = lax.broadcasted_iota(jnp.int32, (BLOCK, PAIR), 0)
    column = lax.broadcasted_iota(jnp.int32, (BLOCK, PAIR), 1)

    @pl.loop(0, NBLK // 2)
    def _(pair):
        for side in range(2):
            place = (column == row + side * BLOCK).astype(F32).astype(BF)
            wide = jnp.dot(pout_ref[2 * pair + side].astype(BF), place, preferred_element_type=F32)
            right_ref[pair, side * BLOCK : (side + 1) * BLOCK, :] = wide.astype(BF)


def prepare(parts, inverse_in, inverse_out):
    chips = len(parts[0])
    width = D // chips
    blocks = inverse_in.shape[0]
    flat = [p for piece in parts for p in piece]
    return pl.pallas_call(
        functools.partial(prepare_kernel, chips, blocks),
        out_shape=(
            near(width, BLOCK, kind=F32),
            near(blocks, BLOCK, BLOCK),
            near(NBLK // 2, PAIR, PAIR),
            *[near(width, chips * PIECE)] * (PIECES - 2),
            *[near(width, (chips - 1) * PIECE)] * 2,
            near(width, 2 * PIECE),
        ),
        in_specs=[VM] * (len(flat) + 2),
        out_specs=[VM] * (4 + PIECES),
        compiler_params=limit(8),
        cost_estimate=SMALL,
    )(*[resident(p) for p in flat], inverse_in, inverse_out)


def own_first(chunk, own):
    core = lax.rem(lax.axis_index("dp"), 2)
    first = lax.rem(chunk // own + core, 2) * own + chunk % own
    return pl.ds(pl.multiple_of(first, 16), min(own, BLOCK))


def add_gram(every, gram_ref, begins):
    width = gram_ref.shape[0]
    chip = lax.div(lax.axis_index("dp"), 2)
    columns = pl.ds(pl.multiple_of(chip * width, 128), width)
    turned = every[:, columns].T
    for block in range(width // BLOCK):
        rows = slice(block * BLOCK, (block + 1) * BLOCK)
        place = own_first(block * BLOCK, width // 2)
        gram = contract_last(turned[rows], turned[rows])
        gram_ref[place, :] = gram if begins else gram + gram_ref[place, :]


def fill(parts, every):
    for k, part in enumerate(parts):
        every[k * PIECE : (k + 1) * PIECE, :] = part[...]


def gather_kernel(count, begins, *refs):
    parts = refs[:count]
    xt_ref = refs[count]
    own_ref, other_ref, gram_ref, every = refs[-4:]
    fill(parts, every)
    add_gram(every, gram_ref, begins)
    own = own_ref.shape[0]

    @pl.loop(0, D // LOAD)
    def _(step):
        columns = pl.ds(pl.multiple_of(step * LOAD, LOAD), LOAD)
        term = jnp.dot(xt_ref[...], every[:, columns], preferred_element_type=F32)
        for acc_ref, some in ((own_ref, term[:own]), (other_ref, term[own:])):
            acc_ref[:, columns] = some if begins else acc_ref[:, columns] + some


def gather(parts, turned, so_far):
    count = len(parts)
    width = turned.shape[0]
    half = near(width // 2, D, kind=F32)
    return pl.pallas_call(
        functools.partial(gather_kernel, count, not so_far),
        out_shape=(half, half, near(width, BLOCK, kind=F32)),
        in_specs=[VM] * (count + 1 + len(so_far)),
        out_specs=(VM, VM, VM),
        scratch_shapes=[pltpu.VMEM((count * PIECE, D), BF)],
        input_output_aliases={count + 1 + k: k for k in range(len(so_far))},
        compiler_params=limit(8),
        cost_estimate=SMALL,
    )(*[resident(p) for p in parts], resident(turned), *[resident(a) for a in so_far])


def other_kernel(first, second, xt_ref, acc_ref, gram_in_ref, gram_ref, _, out_ref, part):
    rows = slice(acc_ref.shape[0], 2 * acc_ref.shape[0])
    fill((first, second), part)
    add_gram(part, gram_ref, False)
    out_ref[:, D : D + BLOCK] = gram_ref[rows, :].astype(BF)
    out_ref[:, D + SIDE : D + SIDE + BLOCK] = gram_in_ref[rows, :].astype(BF)

    @pl.loop(0, D // LOAD)
    def _(step):
        columns = pl.ds(pl.multiple_of(step * LOAD, LOAD), LOAD)
        term = jnp.dot(xt_ref[rows, :], part[:, columns], preferred_element_type=F32)
        out_ref[:, columns] = (term + acc_ref[:, columns]).astype(BF)


def other_half(parts, turned, acc, gram_in, gram_out):
    width = turned.shape[0]
    return pl.pallas_call(
        other_kernel,
        out_shape=(near(width, BLOCK, kind=F32), near(width // 2, D + 2 * SIDE)),
        in_specs=[VM] * 6,
        out_specs=(VM, VM),
        scratch_shapes=[pltpu.VMEM((2 * PIECE, D), BF)],
        input_output_aliases={5: 0},
        compiler_params=limit(8),
        cost_estimate=SMALL,
    )(
        *[resident(p) for p in parts],
        resident(turned),
        resident(acc),
        resident(gram_in),
        resident(gram_out),
    )


def own_kernel(first, second, xt_ref, acc_ref, out_ref, part):
    rows = slice(0, acc_ref.shape[0])
    fill((first, second), part)

    @pl.loop(0, D // LOAD)
    def _(step):
        columns = pl.ds(pl.multiple_of(step * LOAD, LOAD), LOAD)
        term = jnp.dot(xt_ref[rows, :], part[:, columns], preferred_element_type=F32)
        out_ref[:, columns] = term + acc_ref[:, columns]


def own_half(parts, turned, acc):
    return pl.pallas_call(
        own_kernel,
        out_shape=near(*acc.shape, kind=F32),
        in_specs=[VM] * 4,
        out_specs=VM,
        scratch_shapes=[pltpu.VMEM((2 * PIECE, D), BF)],
        input_output_aliases={3: 0},
        compiler_params=limit(8),
        cost_estimate=SMALL,
    )(*[resident(p) for p in parts], resident(turned), resident(acc))


def finish_kernel(blocks, total, own_ref, other_ref, left_ref, right_ref, *refs):
    gram_in_ref, gram_out_ref, update_ref, factor_in_ref, factor_out_ref, ready, grams, sems = refs
    scale = 1.0 / math.sqrt(total)
    pairs = D // PAIR
    copies = []
    for block in range(blocks):
        rows = slice(block * BLOCK, (block + 1) * BLOCK)
        mine = rows
        grams[1, block] = (
            gram_out_ref[mine, :] + other_ref[rows, D : D + BLOCK].astype(F32)
        ) * (1.0 / total)
        grams[0, block] = (
            gram_in_ref[mine, :] + other_ref[rows, D + SIDE : D + SIDE + BLOCK].astype(F32)
        ) * (1.0 / total)
    for k, ref in enumerate((factor_in_ref, factor_out_ref)):
        copy = pltpu.make_async_copy(grams.at[k], ref, sems.at[pairs + k])
        copy.start()
        copies.append(copy)
    for step in range(D // (2 * PAIR)):
        columns = slice(step * 2 * PAIR, (step + 1) * 2 * PAIR)
        grad = (own_ref[:, columns] + other_ref[:, columns].astype(F32)).astype(BF)
        for block in range(blocks):
            rows = slice(block * BLOCK, (block + 1) * BLOCK)
            ready[rows, columns] = jnp.dot(
                left_ref[block], grad[rows], preferred_element_type=F32
            ).astype(BF)
    for pair in range(pairs):
        columns = slice(pair * PAIR, (pair + 1) * PAIR)
        right = jnp.dot(ready[:, columns], right_ref[pair], preferred_element_type=F32)
        ready[:, columns] = (right * scale).astype(BF)
        copy = pltpu.make_async_copy(
            ready.at[:, columns], update_ref.at[:, columns], sems.at[pair]
        )
        copy.start()
        copies.append(copy)
    for copy in copies:
        copy.wait()


def finish(blocks, total, own, other, left, right, gram_in, gram_out):
    factor = shape(blocks, BLOCK, BLOCK, kind=F32)
    return pl.pallas_call(
        functools.partial(finish_kernel, blocks, total),
        out_shape=(shape(blocks * BLOCK, D), factor, factor),
        in_specs=[VM] * 6,
        out_specs=(HB, HB, HB),
        scratch_shapes=[
            pltpu.VMEM((blocks * BLOCK, D), BF),
            pltpu.VMEM((2, blocks, BLOCK, BLOCK), F32),
            pltpu.SemaphoreType.DMA((D // PAIR + 2,)),
        ],
        compiler_params=limit(8),
        cost_estimate=SMALL,
    )(
        resident(own),
        resident(other),
        resident(left),
        resident(right),
        resident(gram_in),
        resident(gram_out),
    )


def shards(sections, ranks, tokens, cotangent, live_counts, weight, inverse_in, inverse_out):
    total = float(TOK_DEV * ranks)
    chips = ranks // 2
    begun = begin(sections, chips, live_counts, tokens, cotangent, weight[0])
    matrix, ahead, packed_tokens, packed_cot, slopes = begun[:5]
    stores = [list(begun[5 + k * chips : 5 + (k + 1) * chips]) for k in range(PIECES)]
    kept = list(begun[5 + chips * PIECES :])
    behind = None
    parts = []
    crossed = []
    last_turn = 2 * (sections - 1)
    single = [1 << b for b in range(chips.bit_length() - 1)]
    acc = []
    for tick in range(PIECES + last_turn):
        done = tick - last_turn
        known = tick - (sections - 1)
        arrived_ahead = arrived_behind = None
        if 0 < tick < PIECES + sections - 1:
            pairs = [(s - 1, s) for s in range(1, sections) if 0 <= tick - s < PIECES]
            arrived_ahead = lax.ppermute(ahead, "section", pairs)
            ahead, matrix, slopes, stores = forward(
                tick, sections, arrived_ahead, packed_tokens, matrix, slopes, stores
            )
        if tick == sections - 2:
            matrix, turned = turn(matrix)
        if tick > sections - 1:
            pairs = [(s + 1, s) for s in range(sections - 1) if 0 <= tick - last_turn + s < PIECES]
            arrived_behind = lax.ppermute(behind, "section", pairs)
        if tick >= sections - 1:
            after = []
            if 1 <= known <= PIECES:
                after = crossed[known - 1][1:]
            if known == PIECES:
                gram_in, left, right, *rows_turned = prepare(
                    crossed, inverse_in[0], inverse_out[0]
                )
            if 1 <= done == PIECES - 1:
                after = after + [parts[done - 1][o] for o in single]
            if done >= 2:
                acc = gather(parts[done - 2], rows_turned[done - 2], acc)
                after = after + [acc[2]]
            behind, turned, kept = backward(
                tick, sections, arrived_behind, turned, slopes, packed_cot, kept, after
            )
        if 0 <= known < PIECES:
            swapped = [swap(stores[known][o], ranks, 2 * o) for o in range(1, chips)]
            crossed.append([stores[known][0]] + swapped)
        if 0 <= done < PIECES:
            piece = [kept[done]]
            for offset in range(1, chips):
                bit = offset & -offset if done % 2 else 1 << (offset.bit_length() - 1)
                piece.append(swap(piece[offset ^ bit], ranks, 2 * bit))
            parts.append(piece)
    for index in range(PIECES - 2, PIECES):
        acc = gather(parts[index][:-1], rows_turned[index], acc)
    final = [parts[-2][-1], parts[-1][-1]]
    gram_out, other = other_half(final, rows_turned[-1], acc[1], gram_in, acc[2])
    other = swap(other, ranks, 1)
    own = own_half(final, rows_turned[-1], acc[0])
    update, factor_in, factor_out = finish(
        inverse_in.shape[1], total, own, other, left, right, gram_in, gram_out
    )
    return (update[None], factor_in[None], factor_out[None])


def solution(mesh):
    in_specs = (
        P("dp", None),
        P("dp", None),
        P("dp", None),
        P("section", None, None),
        P("section", "dp", None, None),
        P("section", None, None, None),
    )
    out_specs = (
        P("section", "dp", None),
        P("section", "dp", None, None),
        P("section", "dp", None, None),
    )
    body = functools.partial(shards, mesh.shape["section"], mesh.shape["dp"])
    return jax.shard_map(body, mesh=mesh, in_specs=in_specs, out_specs=out_specs, check_vma=False)
```

```python
import functools
import math

import jax
import jax.numpy as jnp
from jax import lax
from jax.experimental import pallas as pl
from jax.experimental.pallas import tpu as pltpu
from jax.sharding import PartitionSpec as P

D = 3072
BLOCK = 192
MICRO = 4
ROWS = 80
TOK_DEV = 320
LIVE = 240
NBLK = 16

PIECE = 80
PIECES = LIVE // PIECE
WIDE = 1024
LOAD = 512
PAIR = 2 * BLOCK
SIDE = 256
FLIGHT = 4

C_ZERO = 0.7978845608028654
C_ONE = 0.044715

BF = jnp.bfloat16
F32 = jnp.float32
VM = pl.BlockSpec(memory_space=pltpu.VMEM)
HB = pl.BlockSpec(memory_space=pl.ANY)
MIB = 1 << 20


def resident(x):
    return pltpu.with_memory_space_constraint(x, pltpu.VMEM)


def distant(x):
    return pltpu.with_memory_space_constraint(x, pltpu.HBM)


SMALL = pl.CostEstimate(flops=1000, bytes_accessed=1000, transcendentals=0)


def shape(*sizes, kind=BF):
    return jax.ShapeDtypeStruct(sizes, kind)


def near(*sizes, kind=BF):
    return pltpu.VMEM(sizes, kind)


def limit(size):
    return pltpu.CompilerParams(vmem_limit_bytes=size * MIB)


def swap(x, ranks, flip):
    return lax.ppermute(x, "dp", [(r, r ^ flip) for r in range(ranks)])


def contract_last(a, b):
    return lax.dot_general(a, b, (((1,), (1,)), ((), ())), preferred_element_type=F32)


def forward_columns(columns, held, w_ref, next_ref, slope_ref, piece):
    pre = jnp.dot(held[...], w_ref[:, columns], preferred_element_type=F32)
    square = pre * pre
    hyper = jnp.tanh(C_ZERO * (pre + C_ONE * pre * square))
    half = 0.5 * (1.0 + hyper)
    if next_ref is not None:
        next_ref[:, columns] = (held[:, columns].astype(F32) + pre * half).astype(BF)
    slope = half + 0.5 * pre * (1.0 - hyper * hyper) * C_ZERO * (1.0 + 3.0 * C_ONE * square)
    slope_ref[piece, :, columns] = slope.astype(BF)


def keep_columns(piece, span, held, stores):
    chips = len(stores) // len(span)
    width = D // chips
    chip = lax.div(lax.axis_index("dp"), 2)
    for k, index in enumerate(span):

        @pl.when(piece == index)
        def _():
            for offset in range(chips):
                columns = pl.ds(pl.multiple_of((chip ^ offset) * width, 128), width)
                stores[k * chips + offset][...] = held[:, columns]


def begin_kernel(sections, chips, counts_ref, tokens_ref, cot_ref, weight_ref, *refs):
    w_ref, next_ref, tok_out, cot_out, slope_ref = refs[:5]
    stores = refs[5 : 5 + chips]
    held, raw, counts, raw_sem, counts_sem, sems = refs[-6:]
    here = lax.axis_index("section")
    loads = [
        pltpu.make_async_copy(
            weight_ref.at[:, pl.ds(k * LOAD, LOAD)], w_ref.at[:, pl.ds(k * LOAD, LOAD)], sems.at[k]
        )
        for k in range(D // LOAD)
    ]
    copy_tokens = pltpu.make_async_copy(tokens_ref, raw, raw_sem)
    copy_cot = pltpu.make_async_copy(cot_ref, raw, raw_sem)
    copy_counts = pltpu.make_async_copy(counts_ref, counts, counts_sem)

    def pack(target):
        row = lax.broadcasted_iota(jnp.int32, (LIVE, TOK_DEV), 0)
        column = lax.broadcasted_iota(jnp.int32, (LIVE, TOK_DEV), 1)
        origin = row
        edge = jnp.int32(0)
        for micro in range(MICRO):
            count = counts[0, micro]
            edge = edge + count
            origin = origin + jnp.where(row >= edge, ROWS - count, 0)
        pick = (column == origin).astype(F32).astype(BF)
        for start in range(0, D, WIDE):
            part = jnp.dot(
                pick, raw[:, start : start + WIDE], preferred_element_type=F32
            ).astype(BF)
            for piece in range(PIECES):
                target[piece, :, start : start + WIDE] = part[piece * PIECE : (piece + 1) * PIECE]

    @pl.when(here == 0)
    def _():
        copy_counts.start()
        copy_tokens.start()
        for load in loads[:2]:
            load.start()
        copy_counts.wait()
        copy_tokens.wait()
        for load in loads[2:FLIGHT]:
            load.start()
        pack(tok_out)
        held[...] = tok_out[0]
        for k, load in enumerate(loads):
            load.wait()
            if k + FLIGHT < len(loads):
                loads[k + FLIGHT].start()
            forward_columns(pl.ds(k * LOAD, LOAD), held, w_ref, next_ref, slope_ref, 0)
        keep_columns(0, [0], held, stores)

    @pl.when(here > 0)
    def _():
        blocks = [
            pltpu.make_async_copy(
                weight_ref.at[pl.ds(k * LOAD, LOAD)], w_ref.at[pl.ds(k * LOAD, LOAD)], sems.at[k]
            )
            for k in range(D // LOAD)
        ]
        for block in blocks:
            block.start()
        for block in blocks:
            block.wait()

    @pl.when(jnp.logical_and(here == sections - 1, sections > 1))
    def _():
        copy_counts.start()
        copy_cot.start()
        copy_counts.wait()
        copy_cot.wait()
        pack(cot_out)


def begin(sections, chips, counts, tokens, cotangent, matrix):
    packed = near(PIECES, PIECE, D)
    return pl.pallas_call(
        functools.partial(begin_kernel, sections, chips),
        out_shape=(
            near(D, D),
            near(PIECE, D),
            packed,
            packed,
            near(PIECES, PIECE, D),
            *[near(PIECE, D // chips)] * (chips * PIECES),
            *[near(PIECE, D)] * PIECES,
        ),
        in_specs=[HB] * 4,
        out_specs=[VM] * (5 + chips) + [HB] * (chips * (PIECES - 1) + PIECES),
        scratch_shapes=[
            pltpu.VMEM((PIECE, D), BF),
            pltpu.VMEM((TOK_DEV, D), BF),
            pltpu.SMEM((1, MICRO), jnp.int32),
            pltpu.SemaphoreType.DMA,
            pltpu.SemaphoreType.DMA,
            pltpu.SemaphoreType.DMA((D // LOAD,)),
        ],
        compiler_params=limit(8),
        cost_estimate=SMALL,
    )(distant(counts), distant(tokens), distant(cotangent), distant(matrix))


def forward_kernel(tick, span, count, sends, from_ref, tok_ref, w_ref, *refs):
    outs = refs[1 + count :]
    slope_ref = outs[1]
    stores = outs[2 : 2 + count]
    next_ref = outs[2 + count] if sends else None
    held = outs[-1]
    here = lax.axis_index("section")
    piece = tick - here

    @pl.when(jnp.logical_and(piece >= 0, piece < PIECES))
    def _():
        if tick < PIECES:

            @pl.when(here == 0)
            def _():
                held[...] = tok_ref[tick]

        @pl.when(here > 0)
        def _():
            held[...] = from_ref[...]

        @pl.loop(0, D // WIDE)
        def _(step):
            columns = pl.ds(pl.multiple_of(step * WIDE, WIDE), WIDE)
            forward_columns(columns, held, w_ref, next_ref, slope_ref, piece)

        keep_columns(piece, span, held, stores)


def forward(tick, sections, arrived, tokens, matrix, slopes, stores):
    span = list(range(max(0, tick - sections + 1), min(PIECES - 1, tick) + 1))
    flat = [s for k in span for s in stores[k]]
    count = len(flat)
    sends = tick < PIECES + sections - 2
    outs = pl.pallas_call(
        functools.partial(forward_kernel, tick, span, count, sends),
        out_shape=(
            near(*matrix.shape),
            near(*slopes.shape),
            *[near(*s.shape) for s in flat],
            *[near(PIECE, D)] * sends,
        ),
        in_specs=[VM] * (4 + count),
        out_specs=[VM] * (2 + count + sends),
        scratch_shapes=[pltpu.VMEM((PIECE, D), BF)],
        input_output_aliases={2 + k: k for k in range(2 + count)},
        compiler_params=limit(4),
        cost_estimate=SMALL,
    )(
        resident(arrived),
        resident(tokens),
        resident(matrix),
        resident(slopes),
        *[resident(s) for s in flat],
    )
    stores = list(stores)
    chips = count // len(span)
    for k, index in enumerate(span):
        stores[index] = list(outs[2 + k * chips : 2 + (k + 1) * chips])
    return outs[-1], outs[0], outs[1], stores


def turn_kernel(w_ref, _, out_ref):
    @pl.when(lax.axis_index("section") > 0)
    def _():
        @pl.loop(0, D // LOAD)
        def _(step):
            rows = pl.ds(pl.multiple_of(step * LOAD, LOAD), LOAD)

            @pl.loop(0, D // LOAD)
            def _(other):
                columns = pl.ds(pl.multiple_of(other * LOAD, LOAD), LOAD)
                out_ref[columns, rows] = w_ref[rows, columns].T


def turn(matrix):
    return pl.pallas_call(
        turn_kernel,
        out_shape=(near(*matrix.shape), near(*matrix.shape)),
        in_specs=[VM],
        out_specs=(VM, VM),
        input_output_aliases={0: 0},
        compiler_params=limit(3),
        cost_estimate=SMALL,
    )(resident(matrix))


def backward_kernel(tick, sections, span, late, *refs):
    keeps = len(span)
    refs = refs[late:]
    w_ref, slope_ref = refs[:2]
    chained = tick > sections - 1
    opens = tick - (sections - 1) < PIECES
    cot_ref = refs[2] if opens else None
    from_ref = refs[2 + opens + keeps] if chained else None
    outs = refs[2 + opens + keeps + chained :]
    sends = tick < 2 * (sections - 1) + PIECES - 1
    kept = outs[1 : 1 + keeps]
    next_ref = outs[1 + keeps] if sends else None
    flow, scaled = outs[-2:]
    here = lax.axis_index("section")
    piece = tick - 2 * (sections - 1) + here

    @pl.when(jnp.logical_and(piece >= 0, piece < PIECES))
    def _():
        if opens:

            @pl.when(here == sections - 1)
            def _():
                flow[...] = cot_ref[tick - (sections - 1)]

        if from_ref is not None:

            @pl.when(here < sections - 1)
            def _():
                flow[...] = from_ref[...]

        scaled[...] = (flow[...].astype(F32) * slope_ref[piece].astype(F32)).astype(BF)
        for out, index in zip(kept, span):

            @pl.when(piece == index)
            def _():
                out[...] = scaled[...]

        @pl.when(jnp.logical_and(here > 0, sends))
        def _():
            @pl.loop(0, D // WIDE)
            def _(step):
                part = pl.ds(pl.multiple_of(step * WIDE, WIDE), WIDE)
                back = jnp.dot(scaled[...], w_ref[:, part], preferred_element_type=F32)
                if sends:
                    next_ref[:, part] = (flow[:, part].astype(F32) + back).astype(BF)


def backward(tick, sections, arrived, matrix, slopes, cotangent, kept, after):
    low = max(0, tick - 2 * (sections - 1))
    high = min(PIECES - 1, tick - (sections - 1))
    span = list(range(low, high + 1))
    first = [] if arrived is None else [resident(arrived)]
    sends = tick < 2 * (sections - 1) + PIECES - 1
    opens = [resident(cotangent)] if tick - (sections - 1) < PIECES else []
    base = 2 + len(after) + len(opens)
    out = pl.pallas_call(
        functools.partial(backward_kernel, tick, sections, span, len(after)),
        out_shape=(near(D, D), *[near(PIECE, D)] * (len(span) + sends)),
        in_specs=[HB] * len(after) + [VM] * (2 + len(opens) + len(span) + len(first)),
        out_specs=[VM] * (1 + len(span) + sends),
        scratch_shapes=[pltpu.VMEM((PIECE, D), BF), pltpu.VMEM((PIECE, D), BF)],
        input_output_aliases={
            len(after): 0,
            **{base + k: 1 + k for k in range(len(span))},
        },
        compiler_params=limit(4),
        cost_estimate=SMALL,
    )(
        *after,
        resident(matrix),
        resident(slopes),
        *opens,
        *[resident(kept[k]) for k in span],
        *first,
    )
    kept = list(kept)
    for k, index in enumerate(span):
        kept[index] = out[1 + k]
    return out[-1], out[0], kept


def prepare_kernel(chips, blocks, *refs):
    parts = refs[: chips * PIECES]
    pin_ref, pout_ref, gram_ref, left_ref, right_ref = refs[chips * PIECES : chips * PIECES + 5]
    turned = refs[chips * PIECES + 5 :]
    final = []
    width = gram_ref.shape[0]

    def keep(ref, some):
        columns = jnp.concatenate(some, axis=0).T
        for block in range(width // BLOCK):
            rows = slice(block * BLOCK, (block + 1) * BLOCK)
            ref[own_first(block * BLOCK, width // 2), :] = columns[rows]

    for piece in range(PIECES):
        some = [part[...] for part in parts[piece * chips : (piece + 1) * chips]]
        if piece < PIECES - 2:
            keep(turned[piece], some)
        else:
            keep(turned[piece], some[:-1])
            final.append(some[-1])
    keep(turned[PIECES], final)
    for block in range(2 * blocks):
        rows = slice(block * BLOCK, (block + 1) * BLOCK)
        gram = jnp.zeros((BLOCK, BLOCK), F32)
        for ref in turned:
            some = ref[rows, :]
            gram = gram + contract_last(some, some)
        gram_ref[rows, :] = gram
    for block in range(blocks):
        left_ref[block] = pin_ref[block].astype(BF)
    row = lax.broadcasted_iota(jnp.int32, (BLOCK, PAIR), 0)
    column = lax.broadcasted_iota(jnp.int32, (BLOCK, PAIR), 1)

    @pl.loop(0, NBLK // 2)
    def _(pair):
        for side in range(2):
            place = (column == row + side * BLOCK).astype(F32).astype(BF)
            wide = jnp.dot(pout_ref[2 * pair + side].astype(BF), place, preferred_element_type=F32)
            right_ref[pair, side * BLOCK : (side + 1) * BLOCK, :] = wide.astype(BF)


def prepare(parts, inverse_in, inverse_out):
    chips = len(parts[0])
    width = D // chips
    blocks = inverse_in.shape[0]
    flat = [p for piece in parts for p in piece]
    return pl.pallas_call(
        functools.partial(prepare_kernel, chips, blocks),
        out_shape=(
            near(width, BLOCK, kind=F32),
            near(blocks, BLOCK, BLOCK),
            near(NBLK // 2, PAIR, PAIR),
            *[near(width, chips * PIECE)] * (PIECES - 2),
            *[near(width, (chips - 1) * PIECE)] * 2,
            near(width, 2 * PIECE),
        ),
        in_specs=[VM] * (len(flat) + 2),
        out_specs=[VM] * (4 + PIECES),
        compiler_params=limit(8),
        cost_estimate=SMALL,
    )(*[resident(p) for p in flat], inverse_in, inverse_out)


def own_first(chunk, own):
    core = lax.rem(lax.axis_index("dp"), 2)
    first = lax.rem(chunk // own + core, 2) * own + chunk % own
    return pl.ds(pl.multiple_of(first, 16), min(own, BLOCK))


def add_gram(every, gram_ref, begins):
    width = gram_ref.shape[0]
    chip = lax.div(lax.axis_index("dp"), 2)
    columns = pl.ds(pl.multiple_of(chip * width, 128), width)
    turned = every[:, columns].T
    for block in range(width // BLOCK):
        rows = slice(block * BLOCK, (block + 1) * BLOCK)
        place = own_first(block * BLOCK, width // 2)
        gram = contract_last(turned[rows], turned[rows])
        gram_ref[place, :] = gram if begins else gram + gram_ref[place, :]


def fill(parts, every):
    for k, part in enumerate(parts):
        every[k * PIECE : (k + 1) * PIECE, :] = part[...]


def gather_kernel(count, begins, *refs):
    parts = refs[:count]
    xt_ref = refs[count]
    own_ref, other_ref, gram_ref, every = refs[-4:]
    fill(parts, every)
    add_gram(every, gram_ref, begins)
    own = own_ref.shape[0]

    @pl.loop(0, D // LOAD)
    def _(step):
        columns = pl.ds(pl.multiple_of(step * LOAD, LOAD), LOAD)
        term = jnp.dot(xt_ref[...], every[:, columns], preferred_element_type=F32)
        for acc_ref, some in ((own_ref, term[:own]), (other_ref, term[own:])):
            acc_ref[:, columns] = some if begins else acc_ref[:, columns] + some


def gather(parts, turned, so_far):
    count = len(parts)
    width = turned.shape[0]
    half = near(width // 2, D, kind=F32)
    return pl.pallas_call(
        functools.partial(gather_kernel, count, not so_far),
        out_shape=(half, half, near(width, BLOCK, kind=F32)),
        in_specs=[VM] * (count + 1 + len(so_far)),
        out_specs=(VM, VM, VM),
        scratch_shapes=[pltpu.VMEM((count * PIECE, D), BF)],
        input_output_aliases={count + 1 + k: k for k in range(len(so_far))},
        compiler_params=limit(8),
        cost_estimate=SMALL,
    )(*[resident(p) for p in parts], resident(turned), *[resident(a) for a in so_far])


def other_kernel(first, second, xt_ref, acc_ref, gram_in_ref, gram_ref, _, out_ref, part):
    rows = slice(acc_ref.shape[0], 2 * acc_ref.shape[0])
    fill((first, second), part)
    add_gram(part, gram_ref, False)
    out_ref[:, D : D + BLOCK] = gram_ref[rows, :].astype(BF)
    out_ref[:, D + SIDE : D + SIDE + BLOCK] = gram_in_ref[rows, :].astype(BF)

    @pl.loop(0, D // LOAD)
    def _(step):
        columns = pl.ds(pl.multiple_of(step * LOAD, LOAD), LOAD)
        term = jnp.dot(xt_ref[rows, :], part[:, columns], preferred_element_type=F32)
        out_ref[:, columns] = (term + acc_ref[:, columns]).astype(BF)


def other_half(parts, turned, acc, gram_in, gram_out):
    width = turned.shape[0]
    return pl.pallas_call(
        other_kernel,
        out_shape=(near(width, BLOCK, kind=F32), near(width // 2, D + 2 * SIDE)),
        in_specs=[VM] * 6,
        out_specs=(VM, VM),
        scratch_shapes=[pltpu.VMEM((2 * PIECE, D), BF)],
        input_output_aliases={5: 0},
        compiler_params=limit(8),
        cost_estimate=SMALL,
    )(
        *[resident(p) for p in parts],
        resident(turned),
        resident(acc),
        resident(gram_in),
        resident(gram_out),
    )


def own_kernel(first, second, xt_ref, acc_ref, out_ref, part):
    rows = slice(0, acc_ref.shape[0])
    fill((first, second), part)

    @pl.loop(0, D // LOAD)
    def _(step):
        columns = pl.ds(pl.multiple_of(step * LOAD, LOAD), LOAD)
        term = jnp.dot(xt_ref[rows, :], part[:, columns], preferred_element_type=F32)
        out_ref[:, columns] = term + acc_ref[:, columns]


def own_half(parts, turned, acc):
    return pl.pallas_call(
        own_kernel,
        out_shape=near(*acc.shape, kind=F32),
        in_specs=[VM] * 4,
        out_specs=VM,
        scratch_shapes=[pltpu.VMEM((2 * PIECE, D), BF)],
        input_output_aliases={3: 0},
        compiler_params=limit(8),
        cost_estimate=SMALL,
    )(*[resident(p) for p in parts], resident(turned), resident(acc))


def finish_kernel(blocks, total, own_ref, other_ref, left_ref, right_ref, *refs):
    gram_in_ref, gram_out_ref, update_ref, factor_in_ref, factor_out_ref, ready, grams, sems = refs
    scale = 1.0 / math.sqrt(total)
    pairs = D // PAIR
    copies = []
    for block in range(blocks):
        rows = slice(block * BLOCK, (block + 1) * BLOCK)
        mine = rows
        grams[1, block] = (
            gram_out_ref[mine, :] + other_ref[rows, D : D + BLOCK].astype(F32)
        ) * (1.0 / total)
        grams[0, block] = (
            gram_in_ref[mine, :] + other_ref[rows, D + SIDE : D + SIDE + BLOCK].astype(F32)
        ) * (1.0 / total)
    for k, ref in enumerate((factor_in_ref, factor_out_ref)):
        copy = pltpu.make_async_copy(grams.at[k], ref, sems.at[pairs + k])
        copy.start()
        copies.append(copy)
    for step in range(D // (2 * PAIR)):
        columns = slice(step * 2 * PAIR, (step + 1) * 2 * PAIR)
        grad = (own_ref[:, columns] + other_ref[:, columns].astype(F32)).astype(BF)
        for block in range(blocks):
            rows = slice(block * BLOCK, (block + 1) * BLOCK)
            ready[rows, columns] = jnp.dot(
                left_ref[block], grad[rows], preferred_element_type=F32
            ).astype(BF)
    for pair in range(pairs):
        columns = slice(pair * PAIR, (pair + 1) * PAIR)
        right = jnp.dot(ready[:, columns], right_ref[pair], preferred_element_type=F32)
        ready[:, columns] = (right * scale).astype(BF)
        copy = pltpu.make_async_copy(
            ready.at[:, columns], update_ref.at[:, columns], sems.at[pair]
        )
        copy.start()
        copies.append(copy)
    for copy in copies:
        copy.wait()


def finish(blocks, total, own, other, left, right, gram_in, gram_out):
    factor = shape(blocks, BLOCK, BLOCK, kind=F32)
    return pl.pallas_call(
        functools.partial(finish_kernel, blocks, total),
        out_shape=(shape(blocks * BLOCK, D), factor, factor),
        in_specs=[VM] * 6,
        out_specs=(HB, HB, HB),
        scratch_shapes=[
            pltpu.VMEM((blocks * BLOCK, D), BF),
            pltpu.VMEM((2, blocks, BLOCK, BLOCK), F32),
            pltpu.SemaphoreType.DMA((D // PAIR + 2,)),
        ],
        compiler_params=limit(8),
        cost_estimate=SMALL,
    )(
        resident(own),
        resident(other),
        resident(left),
        resident(right),
        resident(gram_in),
        resident(gram_out),
    )


def shards(sections, ranks, tokens, cotangent, live_counts, weight, inverse_in, inverse_out):
    total = float(TOK_DEV * ranks)
    chips = ranks // 2
    begun = begin(sections, chips, live_counts, tokens, cotangent, weight[0])
    matrix, ahead, packed_tokens, packed_cot, slopes = begun[:5]
    stores = [list(begun[5 + k * chips : 5 + (k + 1) * chips]) for k in range(PIECES)]
    kept = list(begun[5 + chips * PIECES :])
    behind = None
    parts = []
    crossed = []
    last_turn = 2 * (sections - 1)
    single = [1 << b for b in range(chips.bit_length() - 1)]
    acc = []
    for tick in range(PIECES + last_turn):
        done = tick - last_turn
        known = tick - (sections - 1)
        arrived_ahead = arrived_behind = None
        if 0 < tick < PIECES + sections - 1:
            pairs = [(s - 1, s) for s in range(1, sections) if 0 <= tick - s < PIECES]
            arrived_ahead = lax.ppermute(ahead, "section", pairs)
            ahead, matrix, slopes, stores = forward(
                tick, sections, arrived_ahead, packed_tokens, matrix, slopes, stores
            )
        if tick == sections - 2:
            matrix, turned = turn(matrix)
        if tick > sections - 1:
            pairs = [(s + 1, s) for s in range(sections - 1) if 0 <= tick - last_turn + s < PIECES]
            arrived_behind = lax.ppermute(behind, "section", pairs)
        if tick >= sections - 1:
            after = []
            if 1 <= known <= PIECES:
                after = crossed[known - 1][1:]
            if known == PIECES:
                gram_in, left, right, *rows_turned = prepare(
                    crossed, inverse_in[0], inverse_out[0]
                )
            if 1 <= done == PIECES - 1:
                after = after + [parts[done - 1][o] for o in reversed(single)]
            if done >= 2:
                acc = gather(parts[done - 2], rows_turned[done - 2], acc)
                after = after + [acc[2]]
            behind, turned, kept = backward(
                tick, sections, arrived_behind, turned, slopes, packed_cot, kept, after
            )
        if 0 <= known < PIECES:
            swapped = [swap(stores[known][o], ranks, 2 * o) for o in range(1, chips)]
            crossed.append([stores[known][0]] + swapped)
        if 0 <= done < PIECES:
            piece = [kept[done]]
            for offset in range(1, chips):
                bit = offset & -offset if done % 2 else 1 << (offset.bit_length() - 1)
                if done < PIECES - 2:
                    bit = offset
                piece.append(swap(piece[offset ^ bit], ranks, 2 * bit))
            parts.append(piece)
    for index in range(PIECES - 2, PIECES):
        acc = gather(parts[index][:-1], rows_turned[index], acc)
    final = [parts[-2][-1], parts[-1][-1]]
    gram_out, other = other_half(final, rows_turned[-1], acc[1], gram_in, acc[2])
    other = swap(other, ranks, 1)
    own = own_half(final, rows_turned[-1], acc[0])
    update, factor_in, factor_out = finish(
        inverse_in.shape[1], total, own, other, left, right, gram_in, gram_out
    )
    return (update[None], factor_in[None], factor_out[None])


def solution(mesh):
    in_specs = (
        P("dp", None),
        P("dp", None),
        P("dp", None),
        P("section", None, None),
        P("section", "dp", None, None),
        P("section", None, None, None),
    )
    out_specs = (
        P("section", "dp", None),
        P("section", "dp", None, None),
        P("section", "dp", None, None),
    )
    body = functools.partial(shards, mesh.shape["section"], mesh.shape["dp"])
    return jax.shard_map(body, mesh=mesh, in_specs=in_specs, out_specs=out_specs, check_vma=False)
```

```python
import functools
import math

import jax
import jax.numpy as jnp
from jax import lax
from jax.experimental import pallas as pl
from jax.experimental.pallas import tpu as pltpu
from jax.sharding import PartitionSpec as P

D = 3072
BLOCK = 192
MICRO = 4
ROWS = 80
TOK_DEV = 320
LIVE = 240
NBLK = 16

PIECE = 80
PIECES = LIVE // PIECE
WIDE = 1024
LOAD = 512
PAIR = 2 * BLOCK
SIDE = 256
FLIGHT = 4

C_ZERO = 0.7978845608028654
C_ONE = 0.044715

BF = jnp.bfloat16
F32 = jnp.float32
VM = pl.BlockSpec(memory_space=pltpu.VMEM)
HB = pl.BlockSpec(memory_space=pl.ANY)
MIB = 1 << 20


def resident(x):
    return pltpu.with_memory_space_constraint(x, pltpu.VMEM)


def distant(x):
    return pltpu.with_memory_space_constraint(x, pltpu.HBM)


SMALL = pl.CostEstimate(flops=1000, bytes_accessed=1000, transcendentals=0)


def shape(*sizes, kind=BF):
    return jax.ShapeDtypeStruct(sizes, kind)


def near(*sizes, kind=BF):
    return pltpu.VMEM(sizes, kind)


def limit(size):
    return pltpu.CompilerParams(vmem_limit_bytes=size * MIB)


def swap(x, ranks, flip):
    return lax.ppermute(x, "dp", [(r, r ^ flip) for r in range(ranks)])


def contract_last(a, b):
    return lax.dot_general(a, b, (((1,), (1,)), ((), ())), preferred_element_type=F32)


def forward_columns(columns, held, w_ref, next_ref, slope_ref, piece):
    pre = jnp.dot(held[...], w_ref[:, columns], preferred_element_type=F32)
    square = pre * pre
    hyper = jnp.tanh(C_ZERO * (pre + C_ONE * pre * square))
    half = 0.5 * (1.0 + hyper)
    if next_ref is not None:
        next_ref[:, columns] = (held[:, columns].astype(F32) + pre * half).astype(BF)
    slope = half + 0.5 * pre * (1.0 - hyper * hyper) * C_ZERO * (1.0 + 3.0 * C_ONE * square)
    slope_ref[piece, :, columns] = slope.astype(BF)


def keep_columns(piece, span, held, stores):
    chips = len(stores) // len(span)
    width = D // chips
    chip = lax.div(lax.axis_index("dp"), 2)
    for k, index in enumerate(span):

        @pl.when(piece == index)
        def _():
            for offset in range(chips):
                columns = pl.ds(pl.multiple_of((chip ^ offset) * width, 128), width)
                stores[k * chips + offset][...] = held[:, columns]


def begin_kernel(sections, chips, counts_ref, tokens_ref, cot_ref, weight_ref, *refs):
    w_ref, next_ref, tok_out, cot_out, slope_ref = refs[:5]
    stores = refs[5 : 5 + chips]
    held, raw, counts, raw_sem, counts_sem, sems = refs[-6:]
    here = lax.axis_index("section")
    loads = [
        pltpu.make_async_copy(
            weight_ref.at[:, pl.ds(k * LOAD, LOAD)], w_ref.at[:, pl.ds(k * LOAD, LOAD)], sems.at[k]
        )
        for k in range(D // LOAD)
    ]
    copy_tokens = pltpu.make_async_copy(tokens_ref, raw, raw_sem)
    copy_cot = pltpu.make_async_copy(cot_ref, raw, raw_sem)
    copy_counts = pltpu.make_async_copy(counts_ref, counts, counts_sem)

    def pack(target):
        row = lax.broadcasted_iota(jnp.int32, (LIVE, TOK_DEV), 0)
        column = lax.broadcasted_iota(jnp.int32, (LIVE, TOK_DEV), 1)
        origin = row
        edge = jnp.int32(0)
        for micro in range(MICRO):
            count = counts[0, micro]
            edge = edge + count
            origin = origin + jnp.where(row >= edge, ROWS - count, 0)
        pick = (column == origin).astype(F32).astype(BF)
        for start in range(0, D, WIDE):
            part = jnp.dot(
                pick, raw[:, start : start + WIDE], preferred_element_type=F32
            ).astype(BF)
            for piece in range(PIECES):
                target[piece, :, start : start + WIDE] = part[piece * PIECE : (piece + 1) * PIECE]

    @pl.when(here == 0)
    def _():
        copy_counts.start()
        copy_tokens.start()
        for load in loads[:2]:
            load.start()
        copy_counts.wait()
        copy_tokens.wait()
        for load in loads[2:FLIGHT]:
            load.start()
        pack(tok_out)
        held[...] = tok_out[0]
        for k, load in enumerate(loads):
            load.wait()
            if k + FLIGHT < len(loads):
                loads[k + FLIGHT].start()
            forward_columns(pl.ds(k * LOAD, LOAD), held, w_ref, next_ref, slope_ref, 0)
        keep_columns(0, [0], held, stores)

    @pl.when(here > 0)
    def _():
        blocks = [
            pltpu.make_async_copy(
                weight_ref.at[pl.ds(k * LOAD, LOAD)], w_ref.at[pl.ds(k * LOAD, LOAD)], sems.at[k]
            )
            for k in range(D // LOAD)
        ]
        for block in blocks:
            block.start()
        for block in blocks:
            block.wait()

    @pl.when(jnp.logical_and(here == sections - 1, sections > 1))
    def _():
        copy_counts.start()
        copy_cot.start()
        copy_counts.wait()
        copy_cot.wait()
        pack(cot_out)


def begin(sections, chips, counts, tokens, cotangent, matrix):
    packed = near(PIECES, PIECE, D)
    return pl.pallas_call(
        functools.partial(begin_kernel, sections, chips),
        out_shape=(
            near(D, D),
            near(PIECE, D),
            packed,
            packed,
            near(PIECES, PIECE, D),
            *[near(PIECE, D // chips)] * (chips * PIECES),
            *[near(PIECE, D)] * PIECES,
        ),
        in_specs=[HB] * 4,
        out_specs=[VM] * (5 + chips) + [HB] * (chips * (PIECES - 1) + PIECES),
        scratch_shapes=[
            pltpu.VMEM((PIECE, D), BF),
            pltpu.VMEM((TOK_DEV, D), BF),
            pltpu.SMEM((1, MICRO), jnp.int32),
            pltpu.SemaphoreType.DMA,
            pltpu.SemaphoreType.DMA,
            pltpu.SemaphoreType.DMA((D // LOAD,)),
        ],
        compiler_params=limit(8),
        cost_estimate=SMALL,
    )(distant(counts), distant(tokens), distant(cotangent), distant(matrix))


def forward_kernel(tick, span, count, sends, from_ref, tok_ref, w_ref, *refs):
    outs = refs[1 + count :]
    slope_ref = outs[1]
    stores = outs[2 : 2 + count]
    next_ref = outs[2 + count] if sends else None
    held = outs[-1]
    here = lax.axis_index("section")
    piece = tick - here

    @pl.when(jnp.logical_and(piece >= 0, piece < PIECES))
    def _():
        if tick < PIECES:

            @pl.when(here == 0)
            def _():
                held[...] = tok_ref[tick]

        @pl.when(here > 0)
        def _():
            held[...] = from_ref[...]

        @pl.loop(0, D // WIDE)
        def _(step):
            columns = pl.ds(pl.multiple_of(step * WIDE, WIDE), WIDE)
            forward_columns(columns, held, w_ref, next_ref, slope_ref, piece)

        keep_columns(piece, span, held, stores)


def forward(tick, sections, arrived, tokens, matrix, slopes, stores):
    span = list(range(max(0, tick - sections + 1), min(PIECES - 1, tick) + 1))
    flat = [s for k in span for s in stores[k]]
    count = len(flat)
    sends = tick < PIECES + sections - 2
    outs = pl.pallas_call(
        functools.partial(forward_kernel, tick, span, count, sends),
        out_shape=(
            near(*matrix.shape),
            near(*slopes.shape),
            *[near(*s.shape) for s in flat],
            *[near(PIECE, D)] * sends,
        ),
        in_specs=[VM] * (4 + count),
        out_specs=[VM] * (2 + count + sends),
        scratch_shapes=[pltpu.VMEM((PIECE, D), BF)],
        input_output_aliases={2 + k: k for k in range(2 + count)},
        compiler_params=limit(4),
        cost_estimate=SMALL,
    )(
        resident(arrived),
        resident(tokens),
        resident(matrix),
        resident(slopes),
        *[resident(s) for s in flat],
    )
    stores = list(stores)
    chips = count // len(span)
    for k, index in enumerate(span):
        stores[index] = list(outs[2 + k * chips : 2 + (k + 1) * chips])
    return outs[-1], outs[0], outs[1], stores


def turn_kernel(w_ref, _, out_ref):
    @pl.when(lax.axis_index("section") > 0)
    def _():
        @pl.loop(0, D // LOAD)
        def _(step):
            rows = pl.ds(pl.multiple_of(step * LOAD, LOAD), LOAD)

            @pl.loop(0, D // LOAD)
            def _(other):
                columns = pl.ds(pl.multiple_of(other * LOAD, LOAD), LOAD)
                out_ref[columns, rows] = w_ref[rows, columns].T


def turn(matrix):
    return pl.pallas_call(
        turn_kernel,
        out_shape=(near(*matrix.shape), near(*matrix.shape)),
        in_specs=[VM],
        out_specs=(VM, VM),
        input_output_aliases={0: 0},
        compiler_params=limit(3),
        cost_estimate=SMALL,
    )(resident(matrix))


def backward_kernel(tick, sections, span, late, *refs):
    keeps = len(span)
    refs = refs[late:]
    w_ref, slope_ref = refs[:2]
    chained = tick > sections - 1
    opens = tick - (sections - 1) < PIECES
    cot_ref = refs[2] if opens else None
    from_ref = refs[2 + opens + keeps] if chained else None
    outs = refs[2 + opens + keeps + chained :]
    sends = tick < 2 * (sections - 1) + PIECES - 1
    kept = outs[1 : 1 + keeps]
    next_ref = outs[1 + keeps] if sends else None
    flow, scaled = outs[-2:]
    here = lax.axis_index("section")
    piece = tick - 2 * (sections - 1) + here

    @pl.when(jnp.logical_and(piece >= 0, piece < PIECES))
    def _():
        if opens:

            @pl.when(here == sections - 1)
            def _():
                flow[...] = cot_ref[tick - (sections - 1)]

        if from_ref is not None:

            @pl.when(here < sections - 1)
            def _():
                flow[...] = from_ref[...]

        scaled[...] = (flow[...].astype(F32) * slope_ref[piece].astype(F32)).astype(BF)
        for out, index in zip(kept, span):

            @pl.when(piece == index)
            def _():
                out[...] = scaled[...]

        @pl.when(jnp.logical_and(here > 0, sends))
        def _():
            @pl.loop(0, D // WIDE)
            def _(step):
                part = pl.ds(pl.multiple_of(step * WIDE, WIDE), WIDE)
                back = jnp.dot(scaled[...], w_ref[:, part], preferred_element_type=F32)
                if sends:
                    next_ref[:, part] = (flow[:, part].astype(F32) + back).astype(BF)


def backward(tick, sections, arrived, matrix, slopes, cotangent, kept, after):
    low = max(0, tick - 2 * (sections - 1))
    high = min(PIECES - 1, tick - (sections - 1))
    span = list(range(low, high + 1))
    first = [] if arrived is None else [resident(arrived)]
    sends = tick < 2 * (sections - 1) + PIECES - 1
    opens = [resident(cotangent)] if tick - (sections - 1) < PIECES else []
    base = 2 + len(after) + len(opens)
    out = pl.pallas_call(
        functools.partial(backward_kernel, tick, sections, span, len(after)),
        out_shape=(near(D, D), *[near(PIECE, D)] * (len(span) + sends)),
        in_specs=[HB] * len(after) + [VM] * (2 + len(opens) + len(span) + len(first)),
        out_specs=[VM] * (1 + len(span) + sends),
        scratch_shapes=[pltpu.VMEM((PIECE, D), BF), pltpu.VMEM((PIECE, D), BF)],
        input_output_aliases={
            len(after): 0,
            **{base + k: 1 + k for k in range(len(span))},
        },
        compiler_params=limit(4),
        cost_estimate=SMALL,
    )(
        *after,
        resident(matrix),
        resident(slopes),
        *opens,
        *[resident(kept[k]) for k in span],
        *first,
    )
    kept = list(kept)
    for k, index in enumerate(span):
        kept[index] = out[1 + k]
    return out[-1], out[0], kept


def prepare_kernel(chips, blocks, *refs):
    parts = refs[: chips * PIECES]
    pin_ref, pout_ref, gram_ref, left_ref, right_ref = refs[chips * PIECES : chips * PIECES + 5]
    turned = refs[chips * PIECES + 5 :]
    final = []
    width = gram_ref.shape[0]

    def keep(ref, some):
        columns = jnp.concatenate(some, axis=0).T
        for block in range(width // BLOCK):
            rows = slice(block * BLOCK, (block + 1) * BLOCK)
            ref[own_first(block * BLOCK, width // 2), :] = columns[rows]

    for piece in range(PIECES):
        some = [part[...] for part in parts[piece * chips : (piece + 1) * chips]]
        if piece < PIECES - 2:
            keep(turned[piece], some)
        else:
            keep(turned[piece], some[:-1])
            final.append(some[-1])
    keep(turned[PIECES], final)
    for block in range(2 * blocks):
        rows = slice(block * BLOCK, (block + 1) * BLOCK)
        gram = jnp.zeros((BLOCK, BLOCK), F32)
        for ref in turned:
            some = ref[rows, :]
            gram = gram + contract_last(some, some)
        gram_ref[rows, :] = gram
    for block in range(blocks):
        left_ref[block] = pin_ref[block].astype(BF)
    row = lax.broadcasted_iota(jnp.int32, (BLOCK, PAIR), 0)
    column = lax.broadcasted_iota(jnp.int32, (BLOCK, PAIR), 1)

    @pl.loop(0, NBLK // 2)
    def _(pair):
        for side in range(2):
            place = (column == row + side * BLOCK).astype(F32).astype(BF)
            wide = jnp.dot(pout_ref[2 * pair + side].astype(BF), place, preferred_element_type=F32)
            right_ref[pair, side * BLOCK : (side + 1) * BLOCK, :] = wide.astype(BF)


def prepare(parts, inverse_in, inverse_out):
    chips = len(parts[0])
    width = D // chips
    blocks = inverse_in.shape[0]
    flat = [p for piece in parts for p in piece]
    return pl.pallas_call(
        functools.partial(prepare_kernel, chips, blocks),
        out_shape=(
            near(width, BLOCK, kind=F32),
            near(blocks, BLOCK, BLOCK),
            near(NBLK // 2, PAIR, PAIR),
            *[near(width, chips * PIECE)] * (PIECES - 2),
            *[near(width, (chips - 1) * PIECE)] * 2,
            near(width, 2 * PIECE),
        ),
        in_specs=[VM] * (len(flat) + 2),
        out_specs=[VM] * (4 + PIECES),
        compiler_params=limit(8),
        cost_estimate=SMALL,
    )(*[resident(p) for p in flat], inverse_in, inverse_out)


def own_first(chunk, own):
    core = lax.rem(lax.axis_index("dp"), 2)
    first = lax.rem(chunk // own + core, 2) * own + chunk % own
    return pl.ds(pl.multiple_of(first, 16), min(own, BLOCK))


def add_gram(every, gram_ref, begins):
    width = gram_ref.shape[0]
    chip = lax.div(lax.axis_index("dp"), 2)
    columns = pl.ds(pl.multiple_of(chip * width, 128), width)
    turned = every[:, columns].T
    for block in range(width // BLOCK):
        rows = slice(block * BLOCK, (block + 1) * BLOCK)
        place = own_first(block * BLOCK, width // 2)
        gram = contract_last(turned[rows], turned[rows])
        gram_ref[place, :] = gram if begins else gram + gram_ref[place, :]


def hold_kernel(*refs):
    pass


def hold(x, after):
    return pl.pallas_call(
        hold_kernel,
        out_shape=near(*x.shape),
        in_specs=[VM, HB],
        out_specs=VM,
        input_output_aliases={0: 0},
        compiler_params=limit(1),
        cost_estimate=SMALL,
    )(resident(x), after)


def fill(parts, every):
    for k, part in enumerate(parts):
        every[k * PIECE : (k + 1) * PIECE, :] = part[...]


def gather_kernel(count, begins, *refs):
    parts = refs[:count]
    xt_ref = refs[count]
    own_ref, other_ref, gram_ref, every = refs[-4:]
    fill(parts, every)
    add_gram(every, gram_ref, begins)
    own = own_ref.shape[0]

    @pl.loop(0, D // LOAD)
    def _(step):
        columns = pl.ds(pl.multiple_of(step * LOAD, LOAD), LOAD)
        term = jnp.dot(xt_ref[...], every[:, columns], preferred_element_type=F32)
        for acc_ref, some in ((own_ref, term[:own]), (other_ref, term[own:])):
            acc_ref[:, columns] = some if begins else acc_ref[:, columns] + some


def gather(parts, turned, so_far):
    count = len(parts)
    width = turned.shape[0]
    half = near(width // 2, D, kind=F32)
    return pl.pallas_call(
        functools.partial(gather_kernel, count, not so_far),
        out_shape=(half, half, near(width, BLOCK, kind=F32)),
        in_specs=[VM] * (count + 1 + len(so_far)),
        out_specs=(VM, VM, VM),
        scratch_shapes=[pltpu.VMEM((count * PIECE, D), BF)],
        input_output_aliases={count + 1 + k: k for k in range(len(so_far))},
        compiler_params=limit(8),
        cost_estimate=SMALL,
    )(*[resident(p) for p in parts], resident(turned), *[resident(a) for a in so_far])


def other_kernel(first, second, xt_ref, acc_ref, gram_in_ref, gram_ref, _, out_ref, part):
    rows = slice(acc_ref.shape[0], 2 * acc_ref.shape[0])
    fill((first, second), part)
    add_gram(part, gram_ref, False)
    out_ref[:, D : D + BLOCK] = gram_ref[rows, :].astype(BF)
    out_ref[:, D + SIDE : D + SIDE + BLOCK] = gram_in_ref[rows, :].astype(BF)

    @pl.loop(0, D // LOAD)
    def _(step):
        columns = pl.ds(pl.multiple_of(step * LOAD, LOAD), LOAD)
        term = jnp.dot(xt_ref[rows, :], part[:, columns], preferred_element_type=F32)
        out_ref[:, columns] = (term + acc_ref[:, columns]).astype(BF)


def other_half(parts, turned, acc, gram_in, gram_out):
    width = turned.shape[0]
    return pl.pallas_call(
        other_kernel,
        out_shape=(near(width, BLOCK, kind=F32), near(width // 2, D + 2 * SIDE)),
        in_specs=[VM] * 6,
        out_specs=(VM, VM),
        scratch_shapes=[pltpu.VMEM((2 * PIECE, D), BF)],
        input_output_aliases={5: 0},
        compiler_params=limit(8),
        cost_estimate=SMALL,
    )(
        *[resident(p) for p in parts],
        resident(turned),
        resident(acc),
        resident(gram_in),
        resident(gram_out),
    )


def own_kernel(first, second, xt_ref, acc_ref, out_ref, part):
    rows = slice(0, acc_ref.shape[0])
    fill((first, second), part)

    @pl.loop(0, D // LOAD)
    def _(step):
        columns = pl.ds(pl.multiple_of(step * LOAD, LOAD), LOAD)
        term = jnp.dot(xt_ref[rows, :], part[:, columns], preferred_element_type=F32)
        out_ref[:, columns] = term + acc_ref[:, columns]


def own_half(parts, turned, acc):
    return pl.pallas_call(
        own_kernel,
        out_shape=near(*acc.shape, kind=F32),
        in_specs=[VM] * 4,
        out_specs=VM,
        scratch_shapes=[pltpu.VMEM((2 * PIECE, D), BF)],
        input_output_aliases={3: 0},
        compiler_params=limit(8),
        cost_estimate=SMALL,
    )(*[resident(p) for p in parts], resident(turned), resident(acc))


def finish_kernel(blocks, total, own_ref, other_ref, left_ref, right_ref, *refs):
    gram_in_ref, gram_out_ref, update_ref, factor_in_ref, factor_out_ref, ready, grams, sems = refs
    scale = 1.0 / math.sqrt(total)
    pairs = D // PAIR
    copies = []
    for block in range(blocks):
        rows = slice(block * BLOCK, (block + 1) * BLOCK)
        mine = rows
        grams[1, block] = (
            gram_out_ref[mine, :] + other_ref[rows, D : D + BLOCK].astype(F32)
        ) * (1.0 / total)
        grams[0, block] = (
            gram_in_ref[mine, :] + other_ref[rows, D + SIDE : D + SIDE + BLOCK].astype(F32)
        ) * (1.0 / total)
    for k, ref in enumerate((factor_in_ref, factor_out_ref)):
        copy = pltpu.make_async_copy(grams.at[k], ref, sems.at[pairs + k])
        copy.start()
        copies.append(copy)
    for step in range(D // (2 * PAIR)):
        columns = slice(step * 2 * PAIR, (step + 1) * 2 * PAIR)
        grad = (own_ref[:, columns] + other_ref[:, columns].astype(F32)).astype(BF)
        for block in range(blocks):
            rows = slice(block * BLOCK, (block + 1) * BLOCK)
            ready[rows, columns] = jnp.dot(
                left_ref[block], grad[rows], preferred_element_type=F32
            ).astype(BF)
    for pair in range(pairs):
        columns = slice(pair * PAIR, (pair + 1) * PAIR)
        right = jnp.dot(ready[:, columns], right_ref[pair], preferred_element_type=F32)
        ready[:, columns] = (right * scale).astype(BF)
        copy = pltpu.make_async_copy(
            ready.at[:, columns], update_ref.at[:, columns], sems.at[pair]
        )
        copy.start()
        copies.append(copy)
    for copy in copies:
        copy.wait()


def finish(blocks, total, own, other, left, right, gram_in, gram_out):
    factor = shape(blocks, BLOCK, BLOCK, kind=F32)
    return pl.pallas_call(
        functools.partial(finish_kernel, blocks, total),
        out_shape=(shape(blocks * BLOCK, D), factor, factor),
        in_specs=[VM] * 6,
        out_specs=(HB, HB, HB),
        scratch_shapes=[
            pltpu.VMEM((blocks * BLOCK, D), BF),
            pltpu.VMEM((2, blocks, BLOCK, BLOCK), F32),
            pltpu.SemaphoreType.DMA((D // PAIR + 2,)),
        ],
        compiler_params=limit(8),
        cost_estimate=SMALL,
    )(
        resident(own),
        resident(other),
        resident(left),
        resident(right),
        resident(gram_in),
        resident(gram_out),
    )


def shards(sections, ranks, tokens, cotangent, live_counts, weight, inverse_in, inverse_out):
    total = float(TOK_DEV * ranks)
    chips = ranks // 2
    begun = begin(sections, chips, live_counts, tokens, cotangent, weight[0])
    matrix, ahead, packed_tokens, packed_cot, slopes = begun[:5]
    stores = [list(begun[5 + k * chips : 5 + (k + 1) * chips]) for k in range(PIECES)]
    kept = list(begun[5 + chips * PIECES :])
    behind = None
    parts = []
    crossed = []
    last_turn = 2 * (sections - 1)
    single = [1 << b for b in range(chips.bit_length() - 1)]
    acc = []
    for tick in range(PIECES + last_turn):
        done = tick - last_turn
        known = tick - (sections - 1)
        arrived_ahead = arrived_behind = None
        if 0 < tick < PIECES + sections - 1:
            pairs = [(s - 1, s) for s in range(1, sections) if 0 <= tick - s < PIECES]
            arrived_ahead = lax.ppermute(ahead, "section", pairs)
            ahead, matrix, slopes, stores = forward(
                tick, sections, arrived_ahead, packed_tokens, matrix, slopes, stores
            )
        if tick == sections - 2:
            matrix, turned = turn(matrix)
        if tick > sections - 1:
            pairs = [(s + 1, s) for s in range(sections - 1) if 0 <= tick - last_turn + s < PIECES]
            arrived_behind = lax.ppermute(behind, "section", pairs)
        if tick >= sections - 1:
            after = []
            if 1 <= known <= PIECES:
                after = crossed[known - 1][1:]
            if known == PIECES:
                gram_in, left, right, *rows_turned = prepare(
                    crossed, inverse_in[0], inverse_out[0]
                )
            if 1 <= done == PIECES - 1:
                after = after + [parts[done - 1][o] for o in reversed(single)]
            if done >= 2:
                acc = gather(parts[done - 2], rows_turned[done - 2], acc)
                after = after + [acc[2]]
            behind, turned, kept = backward(
                tick, sections, arrived_behind, turned, slopes, packed_cot, kept, after
            )
        if 0 <= known < PIECES:
            swapped = [swap(stores[known][o], ranks, 2 * o) for o in range(1, chips)]
            crossed.append([stores[known][0]] + swapped)
        if 0 <= done < PIECES:
            piece = [kept[done]] + [None] * (chips - 1)
            for bit in single:
                piece[bit] = swap(kept[done], ranks, 2 * bit)
            parts.append(piece)
            ready = [done]
            if done == PIECES - 2:
                ready = []
            elif done == PIECES - 1:
                for bit in single:
                    parts[-2][bit] = hold(parts[-2][bit], piece[1])
                ready = [PIECES - 1, PIECES - 2]
            for index in ready:
                piece = parts[index]
                for offset in range(1, chips):
                    if offset in single:
                        continue
                    bit = offset & -offset if index % 2 else 1 << (offset.bit_length() - 1)
                    if index < PIECES - 2:
                        bit = offset
                    piece[offset] = swap(piece[offset ^ bit], ranks, 2 * bit)
    for index in range(PIECES - 2, PIECES):
        acc = gather(parts[index][:-1], rows_turned[index], acc)
    final = [parts[-2][-1], parts[-1][-1]]
    gram_out, other = other_half(final, rows_turned[-1], acc[1], gram_in, acc[2])
    other = swap(other, ranks, 1)
    own = own_half(final, rows_turned[-1], acc[0])
    update, factor_in, factor_out = finish(
        inverse_in.shape[1], total, own, other, left, right, gram_in, gram_out
    )
    return (update[None], factor_in[None], factor_out[None])


def solution(mesh):
    in_specs = (
        P("dp", None),
        P("dp", None),
        P("dp", None),
        P("section", None, None),
        P("section", "dp", None, None),
        P("section", None, None, None),
    )
    out_specs = (
        P("section", "dp", None),
        P("section", "dp", None, None),
        P("section", "dp", None, None),
    )
    body = functools.partial(shards, mesh.shape["section"], mesh.shape["dp"])
    return jax.shard_map(body, mesh=mesh, in_specs=in_specs, out_specs=out_specs, check_vma=False)
```

```python
import functools
import math

import jax
import jax.numpy as jnp
from jax import lax
from jax.experimental import pallas as pl
from jax.experimental.pallas import tpu as pltpu
from jax.sharding import PartitionSpec as P

D = 3072
BLOCK = 192
MICRO = 4
ROWS = 80
TOK_DEV = 320
LIVE = 240
NBLK = 16

PIECE = 80
PIECES = LIVE // PIECE
WIDE = 1024
LOAD = 512
PAIR = 2 * BLOCK
SIDE = 256
FLIGHT = 4

C_ZERO = 0.7978845608028654
C_ONE = 0.044715

BF = jnp.bfloat16
F32 = jnp.float32
VM = pl.BlockSpec(memory_space=pltpu.VMEM)
HB = pl.BlockSpec(memory_space=pl.ANY)
MIB = 1 << 20


def resident(x):
    return pltpu.with_memory_space_constraint(x, pltpu.VMEM)


def distant(x):
    return pltpu.with_memory_space_constraint(x, pltpu.HBM)


SMALL = pl.CostEstimate(flops=1000, bytes_accessed=1000, transcendentals=0)


def shape(*sizes, kind=BF):
    return jax.ShapeDtypeStruct(sizes, kind)


def near(*sizes, kind=BF):
    return pltpu.VMEM(sizes, kind)


def limit(size):
    return pltpu.CompilerParams(vmem_limit_bytes=size * MIB)


def swap(x, ranks, flip):
    return lax.ppermute(x, "dp", [(r, r ^ flip) for r in range(ranks)])


def contract_last(a, b):
    return lax.dot_general(a, b, (((1,), (1,)), ((), ())), preferred_element_type=F32)


def forward_columns(columns, held, w_ref, next_ref, slope_ref, piece):
    pre = jnp.dot(held[...], w_ref[:, columns], preferred_element_type=F32)
    square = pre * pre
    hyper = jnp.tanh(C_ZERO * (pre + C_ONE * pre * square))
    half = 0.5 * (1.0 + hyper)
    if next_ref is not None:
        next_ref[:, columns] = (held[:, columns].astype(F32) + pre * half).astype(BF)
    slope = half + 0.5 * pre * (1.0 - hyper * hyper) * C_ZERO * (1.0 + 3.0 * C_ONE * square)
    slope_ref[piece, :, columns] = slope.astype(BF)


def keep_columns(piece, span, held, stores):
    chips = len(stores) // len(span)
    width = D // chips
    chip = lax.div(lax.axis_index("dp"), 2)
    for k, index in enumerate(span):

        @pl.when(piece == index)
        def _():
            for offset in range(chips):
                columns = pl.ds(pl.multiple_of((chip ^ offset) * width, 128), width)
                stores[k * chips + offset][...] = held[:, columns]


def begin_kernel(sections, chips, counts_ref, tokens_ref, cot_ref, weight_ref, *refs):
    w_ref, next_ref, tok_out, cot_out, slope_ref = refs[:5]
    stores = refs[5 : 5 + chips]
    held, raw, counts, raw_sem, counts_sem, sems = refs[-6:]
    here = lax.axis_index("section")
    loads = [
        pltpu.make_async_copy(
            weight_ref.at[:, pl.ds(k * LOAD, LOAD)], w_ref.at[:, pl.ds(k * LOAD, LOAD)], sems.at[k]
        )
        for k in range(D // LOAD)
    ]
    copy_tokens = pltpu.make_async_copy(tokens_ref, raw, raw_sem)
    copy_cot = pltpu.make_async_copy(cot_ref, raw, raw_sem)
    copy_counts = pltpu.make_async_copy(counts_ref, counts, counts_sem)

    def pack(target):
        row = lax.broadcasted_iota(jnp.int32, (LIVE, TOK_DEV), 0)
        column = lax.broadcasted_iota(jnp.int32, (LIVE, TOK_DEV), 1)
        origin = row
        edge = jnp.int32(0)
        for micro in range(MICRO):
            count = counts[0, micro]
            edge = edge + count
            origin = origin + jnp.where(row >= edge, ROWS - count, 0)
        pick = (column == origin).astype(F32).astype(BF)
        for start in range(0, D, WIDE):
            part = jnp.dot(
                pick, raw[:, start : start + WIDE], preferred_element_type=F32
            ).astype(BF)
            for piece in range(PIECES):
                target[piece, :, start : start + WIDE] = part[piece * PIECE : (piece + 1) * PIECE]

    @pl.when(here == 0)
    def _():
        copy_counts.start()
        copy_tokens.start()
        for load in loads[:2]:
            load.start()
        copy_counts.wait()
        copy_tokens.wait()
        for load in loads[2:FLIGHT]:
            load.start()
        pack(tok_out)
        held[...] = tok_out[0]
        for k, load in enumerate(loads):
            load.wait()
            if k + FLIGHT < len(loads):
                loads[k + FLIGHT].start()
            forward_columns(pl.ds(k * LOAD, LOAD), held, w_ref, next_ref, slope_ref, 0)
        keep_columns(0, [0], held, stores)

    @pl.when(here > 0)
    def _():
        blocks = [
            pltpu.make_async_copy(
                weight_ref.at[pl.ds(k * LOAD, LOAD)], w_ref.at[pl.ds(k * LOAD, LOAD)], sems.at[k]
            )
            for k in range(D // LOAD)
        ]
        for block in blocks:
            block.start()
        for block in blocks:
            block.wait()

    @pl.when(jnp.logical_and(here == sections - 1, sections > 1))
    def _():
        copy_counts.start()
        copy_cot.start()
        copy_counts.wait()
        copy_cot.wait()
        pack(cot_out)


def begin(sections, chips, counts, tokens, cotangent, matrix):
    packed = near(PIECES, PIECE, D)
    return pl.pallas_call(
        functools.partial(begin_kernel, sections, chips),
        out_shape=(
            near(D, D),
            near(PIECE, D),
            packed,
            packed,
            near(PIECES, PIECE, D),
            *[near(PIECE, D // chips)] * (chips * PIECES),
            *[near(PIECE, D)] * PIECES,
        ),
        in_specs=[HB] * 4,
        out_specs=[VM] * (5 + chips) + [HB] * (chips * (PIECES - 1) + PIECES),
        scratch_shapes=[
            pltpu.VMEM((PIECE, D), BF),
            pltpu.VMEM((TOK_DEV, D), BF),
            pltpu.SMEM((1, MICRO), jnp.int32),
            pltpu.SemaphoreType.DMA,
            pltpu.SemaphoreType.DMA,
            pltpu.SemaphoreType.DMA((D // LOAD,)),
        ],
        compiler_params=limit(8),
        cost_estimate=SMALL,
    )(distant(counts), distant(tokens), distant(cotangent), distant(matrix))


def forward_kernel(tick, span, count, sends, from_ref, tok_ref, w_ref, *refs):
    outs = refs[1 + count :]
    slope_ref = outs[1]
    stores = outs[2 : 2 + count]
    next_ref = outs[2 + count] if sends else None
    held = outs[-1]
    here = lax.axis_index("section")
    piece = tick - here

    @pl.when(jnp.logical_and(piece >= 0, piece < PIECES))
    def _():
        if tick < PIECES:

            @pl.when(here == 0)
            def _():
                held[...] = tok_ref[tick]

        @pl.when(here > 0)
        def _():
            held[...] = from_ref[...]

        @pl.loop(0, D // WIDE)
        def _(step):
            columns = pl.ds(pl.multiple_of(step * WIDE, WIDE), WIDE)
            forward_columns(columns, held, w_ref, next_ref, slope_ref, piece)

        keep_columns(piece, span, held, stores)


def forward(tick, sections, arrived, tokens, matrix, slopes, stores):
    span = list(range(max(0, tick - sections + 1), min(PIECES - 1, tick) + 1))
    flat = [s for k in span for s in stores[k]]
    count = len(flat)
    sends = tick < PIECES + sections - 2
    outs = pl.pallas_call(
        functools.partial(forward_kernel, tick, span, count, sends),
        out_shape=(
            near(*matrix.shape),
            near(*slopes.shape),
            *[near(*s.shape) for s in flat],
            *[near(PIECE, D)] * sends,
        ),
        in_specs=[VM] * (4 + count),
        out_specs=[VM] * (2 + count + sends),
        scratch_shapes=[pltpu.VMEM((PIECE, D), BF)],
        input_output_aliases={2 + k: k for k in range(2 + count)},
        compiler_params=limit(4),
        cost_estimate=SMALL,
    )(
        resident(arrived),
        resident(tokens),
        resident(matrix),
        resident(slopes),
        *[resident(s) for s in flat],
    )
    stores = list(stores)
    chips = count // len(span)
    for k, index in enumerate(span):
        stores[index] = list(outs[2 + k * chips : 2 + (k + 1) * chips])
    return outs[-1], outs[0], outs[1], stores


def turn_kernel(w_ref, _, out_ref):
    @pl.when(lax.axis_index("section") > 0)
    def _():
        @pl.loop(0, D // LOAD)
        def _(step):
            rows = pl.ds(pl.multiple_of(step * LOAD, LOAD), LOAD)

            @pl.loop(0, D // LOAD)
            def _(other):
                columns = pl.ds(pl.multiple_of(other * LOAD, LOAD), LOAD)
                out_ref[columns, rows] = w_ref[rows, columns].T


def turn(matrix):
    return pl.pallas_call(
        turn_kernel,
        out_shape=(near(*matrix.shape), near(*matrix.shape)),
        in_specs=[VM],
        out_specs=(VM, VM),
        input_output_aliases={0: 0},
        compiler_params=limit(3),
        cost_estimate=SMALL,
    )(resident(matrix))


def backward_kernel(tick, sections, span, late, *refs):
    keeps = len(span)
    refs = refs[late:]
    w_ref, slope_ref = refs[:2]
    chained = tick > sections - 1
    opens = tick - (sections - 1) < PIECES
    cot_ref = refs[2] if opens else None
    from_ref = refs[2 + opens + keeps] if chained else None
    outs = refs[2 + opens + keeps + chained :]
    sends = tick < 2 * (sections - 1) + PIECES - 1
    kept = outs[1 : 1 + keeps]
    next_ref = outs[1 + keeps] if sends else None
    flow, scaled = outs[-2:]
    here = lax.axis_index("section")
    piece = tick - 2 * (sections - 1) + here

    @pl.when(jnp.logical_and(piece >= 0, piece < PIECES))
    def _():
        if opens:

            @pl.when(here == sections - 1)
            def _():
                flow[...] = cot_ref[tick - (sections - 1)]

        if from_ref is not None:

            @pl.when(here < sections - 1)
            def _():
                flow[...] = from_ref[...]

        scaled[...] = (flow[...].astype(F32) * slope_ref[piece].astype(F32)).astype(BF)
        for out, index in zip(kept, span):

            @pl.when(piece == index)
            def _():
                out[...] = scaled[...]

        @pl.when(jnp.logical_and(here > 0, sends))
        def _():
            @pl.loop(0, D // WIDE)
            def _(step):
                part = pl.ds(pl.multiple_of(step * WIDE, WIDE), WIDE)
                back = jnp.dot(scaled[...], w_ref[:, part], preferred_element_type=F32)
                if sends:
                    next_ref[:, part] = (flow[:, part].astype(F32) + back).astype(BF)


def backward(tick, sections, arrived, matrix, slopes, cotangent, kept, after):
    low = max(0, tick - 2 * (sections - 1))
    high = min(PIECES - 1, tick - (sections - 1))
    span = list(range(low, high + 1))
    first = [] if arrived is None else [resident(arrived)]
    sends = tick < 2 * (sections - 1) + PIECES - 1
    opens = [resident(cotangent)] if tick - (sections - 1) < PIECES else []
    base = 2 + len(after) + len(opens)
    out = pl.pallas_call(
        functools.partial(backward_kernel, tick, sections, span, len(after)),
        out_shape=(near(D, D), *[near(PIECE, D)] * (len(span) + sends)),
        in_specs=[HB] * len(after) + [VM] * (2 + len(opens) + len(span) + len(first)),
        out_specs=[VM] * (1 + len(span) + sends),
        scratch_shapes=[pltpu.VMEM((PIECE, D), BF), pltpu.VMEM((PIECE, D), BF)],
        input_output_aliases={
            len(after): 0,
            **{base + k: 1 + k for k in range(len(span))},
        },
        compiler_params=limit(4),
        cost_estimate=SMALL,
    )(
        *after,
        resident(matrix),
        resident(slopes),
        *opens,
        *[resident(kept[k]) for k in span],
        *first,
    )
    kept = list(kept)
    for k, index in enumerate(span):
        kept[index] = out[1 + k]
    return out[-1], out[0], kept


def prepare_kernel(chips, blocks, *refs):
    parts = refs[: chips * PIECES]
    pin_ref, pout_ref, gram_ref, left_ref, right_ref = refs[chips * PIECES : chips * PIECES + 5]
    turned = refs[chips * PIECES + 5 :]
    final = []
    width = gram_ref.shape[0]

    def keep(ref, some):
        columns = jnp.concatenate(some, axis=0).T
        for block in range(width // BLOCK):
            rows = slice(block * BLOCK, (block + 1) * BLOCK)
            ref[own_first(block * BLOCK, width // 2), :] = columns[rows]

    for piece in range(PIECES):
        some = [part[...] for part in parts[piece * chips : (piece + 1) * chips]]
        if piece < PIECES - 2:
            keep(turned[piece], some)
        else:
            keep(turned[piece], some[:-1])
            final.append(some[-1])
    keep(turned[PIECES], final)
    for block in range(2 * blocks):
        rows = slice(block * BLOCK, (block + 1) * BLOCK)
        gram = jnp.zeros((BLOCK, BLOCK), F32)
        for ref in turned:
            some = ref[rows, :]
            gram = gram + contract_last(some, some)
        gram_ref[rows, :] = gram
    for block in range(blocks):
        left_ref[block] = pin_ref[block].astype(BF)
    row = lax.broadcasted_iota(jnp.int32, (BLOCK, PAIR), 0)
    column = lax.broadcasted_iota(jnp.int32, (BLOCK, PAIR), 1)

    @pl.loop(0, NBLK // 2)
    def _(pair):
        for side in range(2):
            place = (column == row + side * BLOCK).astype(F32).astype(BF)
            wide = jnp.dot(pout_ref[2 * pair + side].astype(BF), place, preferred_element_type=F32)
            right_ref[pair, side * BLOCK : (side + 1) * BLOCK, :] = wide.astype(BF)


def prepare(parts, inverse_in, inverse_out):
    chips = len(parts[0])
    width = D // chips
    blocks = inverse_in.shape[0]
    flat = [p for piece in parts for p in piece]
    return pl.pallas_call(
        functools.partial(prepare_kernel, chips, blocks),
        out_shape=(
            near(width, BLOCK, kind=F32),
            near(blocks, BLOCK, BLOCK),
            near(NBLK // 2, PAIR, PAIR),
            *[near(width, chips * PIECE)] * (PIECES - 2),
            *[near(width, (chips - 1) * PIECE)] * 2,
            near(width, 2 * PIECE),
        ),
        in_specs=[VM] * (len(flat) + 2),
        out_specs=[VM] * (4 + PIECES),
        compiler_params=limit(8),
        cost_estimate=SMALL,
    )(*[resident(p) for p in flat], inverse_in, inverse_out)


def own_first(chunk, own):
    core = lax.rem(lax.axis_index("dp"), 2)
    first = lax.rem(chunk // own + core, 2) * own + chunk % own
    return pl.ds(pl.multiple_of(first, 16), min(own, BLOCK))


def add_gram(every, gram_ref, begins):
    width = gram_ref.shape[0]
    chip = lax.div(lax.axis_index("dp"), 2)
    columns = pl.ds(pl.multiple_of(chip * width, 128), width)
    turned = every[:, columns].T
    for block in range(width // BLOCK):
        rows = slice(block * BLOCK, (block + 1) * BLOCK)
        place = own_first(block * BLOCK, width // 2)
        gram = contract_last(turned[rows], turned[rows])
        gram_ref[place, :] = gram if begins else gram + gram_ref[place, :]


def fill(parts, every):
    for k, part in enumerate(parts):
        every[k * PIECE : (k + 1) * PIECE, :] = part[...]


def gather_kernel(count, begins, *refs):
    parts = refs[:count]
    xt_ref = refs[count]
    own_ref, other_ref, gram_ref, every = refs[-4:]
    fill(parts, every)
    add_gram(every, gram_ref, begins)
    own = own_ref.shape[0]

    @pl.loop(0, D // LOAD)
    def _(step):
        columns = pl.ds(pl.multiple_of(step * LOAD, LOAD), LOAD)
        term = jnp.dot(xt_ref[...], every[:, columns], preferred_element_type=F32)
        for acc_ref, some in ((own_ref, term[:own]), (other_ref, term[own:])):
            acc_ref[:, columns] = some if begins else acc_ref[:, columns] + some


def gather(parts, turned, so_far):
    count = len(parts)
    width = turned.shape[0]
    half = near(width // 2, D, kind=F32)
    return pl.pallas_call(
        functools.partial(gather_kernel, count, not so_far),
        out_shape=(half, half, near(width, BLOCK, kind=F32)),
        in_specs=[VM] * (count + 1 + len(so_far)),
        out_specs=(VM, VM, VM),
        scratch_shapes=[pltpu.VMEM((count * PIECE, D), BF)],
        input_output_aliases={count + 1 + k: k for k in range(len(so_far))},
        compiler_params=limit(8),
        cost_estimate=SMALL,
    )(*[resident(p) for p in parts], resident(turned), *[resident(a) for a in so_far])


def other_kernel(first, second, xt_ref, acc_ref, gram_in_ref, gram_ref, _, out_ref, part):
    rows = slice(acc_ref.shape[0], 2 * acc_ref.shape[0])
    fill((first, second), part)
    add_gram(part, gram_ref, False)
    out_ref[:, D : D + BLOCK] = gram_ref[rows, :].astype(BF)
    out_ref[:, D + SIDE : D + SIDE + BLOCK] = gram_in_ref[rows, :].astype(BF)

    @pl.loop(0, D // LOAD)
    def _(step):
        columns = pl.ds(pl.multiple_of(step * LOAD, LOAD), LOAD)
        term = jnp.dot(xt_ref[rows, :], part[:, columns], preferred_element_type=F32)
        out_ref[:, columns] = (term + acc_ref[:, columns]).astype(BF)


def other_half(parts, turned, acc, gram_in, gram_out):
    width = turned.shape[0]
    return pl.pallas_call(
        other_kernel,
        out_shape=(near(width, BLOCK, kind=F32), near(width // 2, D + 2 * SIDE)),
        in_specs=[VM] * 6,
        out_specs=(VM, VM),
        scratch_shapes=[pltpu.VMEM((2 * PIECE, D), BF)],
        input_output_aliases={5: 0},
        compiler_params=limit(8),
        cost_estimate=SMALL,
    )(
        *[resident(p) for p in parts],
        resident(turned),
        resident(acc),
        resident(gram_in),
        resident(gram_out),
    )


def own_kernel(first, second, xt_ref, acc_ref, out_ref, part):
    rows = slice(0, acc_ref.shape[0])
    fill((first, second), part)

    @pl.loop(0, D // LOAD)
    def _(step):
        columns = pl.ds(pl.multiple_of(step * LOAD, LOAD), LOAD)
        term = jnp.dot(xt_ref[rows, :], part[:, columns], preferred_element_type=F32)
        out_ref[:, columns] = term + acc_ref[:, columns]


def own_half(parts, turned, acc):
    return pl.pallas_call(
        own_kernel,
        out_shape=near(*acc.shape, kind=F32),
        in_specs=[VM] * 4,
        out_specs=VM,
        scratch_shapes=[pltpu.VMEM((2 * PIECE, D), BF)],
        input_output_aliases={3: 0},
        compiler_params=limit(8),
        cost_estimate=SMALL,
    )(*[resident(p) for p in parts], resident(turned), resident(acc))


def finish_kernel(blocks, total, own_ref, other_ref, left_ref, right_ref, *refs):
    gram_in_ref, gram_out_ref, update_ref, factor_in_ref, factor_out_ref, ready, grams, sems = refs
    scale = 1.0 / math.sqrt(total)
    pairs = D // PAIR
    copies = []
    for block in range(blocks):
        rows = slice(block * BLOCK, (block + 1) * BLOCK)
        mine = rows
        grams[1, block] = (
            gram_out_ref[mine, :] + other_ref[rows, D : D + BLOCK].astype(F32)
        ) * (1.0 / total)
        grams[0, block] = (
            gram_in_ref[mine, :] + other_ref[rows, D + SIDE : D + SIDE + BLOCK].astype(F32)
        ) * (1.0 / total)
    for k, ref in enumerate((factor_in_ref, factor_out_ref)):
        copy = pltpu.make_async_copy(grams.at[k], ref, sems.at[pairs + k])
        copy.start()
        copies.append(copy)
    for step in range(D // (2 * PAIR)):
        columns = slice(step * 2 * PAIR, (step + 1) * 2 * PAIR)
        grad = (own_ref[:, columns] + other_ref[:, columns].astype(F32)).astype(BF)
        for block in range(blocks):
            rows = slice(block * BLOCK, (block + 1) * BLOCK)
            ready[rows, columns] = jnp.dot(
                left_ref[block], grad[rows], preferred_element_type=F32
            ).astype(BF)
    for pair in range(pairs):
        columns = slice(pair * PAIR, (pair + 1) * PAIR)
        right = jnp.dot(ready[:, columns], right_ref[pair], preferred_element_type=F32)
        ready[:, columns] = (right * scale).astype(BF)
        copy = pltpu.make_async_copy(
            ready.at[:, columns], update_ref.at[:, columns], sems.at[pair]
        )
        copy.start()
        copies.append(copy)
    for copy in copies:
        copy.wait()


def finish(blocks, total, own, other, left, right, gram_in, gram_out):
    factor = shape(blocks, BLOCK, BLOCK, kind=F32)
    return pl.pallas_call(
        functools.partial(finish_kernel, blocks, total),
        out_shape=(shape(blocks * BLOCK, D), factor, factor),
        in_specs=[VM] * 6,
        out_specs=(HB, HB, HB),
        scratch_shapes=[
            pltpu.VMEM((blocks * BLOCK, D), BF),
            pltpu.VMEM((2, blocks, BLOCK, BLOCK), F32),
            pltpu.SemaphoreType.DMA((D // PAIR + 2,)),
        ],
        compiler_params=limit(8),
        cost_estimate=SMALL,
    )(
        resident(own),
        resident(other),
        resident(left),
        resident(right),
        resident(gram_in),
        resident(gram_out),
    )


def shards(sections, ranks, tokens, cotangent, live_counts, weight, inverse_in, inverse_out):
    total = float(TOK_DEV * ranks)
    chips = ranks // 2
    begun = begin(sections, chips, live_counts, tokens, cotangent, weight[0])
    matrix, ahead, packed_tokens, packed_cot, slopes = begun[:5]
    stores = [list(begun[5 + k * chips : 5 + (k + 1) * chips]) for k in range(PIECES)]
    kept = list(begun[5 + chips * PIECES :])
    behind = None
    parts = []
    crossed = []
    last_turn = 2 * (sections - 1)
    single = [1 << b for b in range(chips.bit_length() - 1)]
    acc = []
    for tick in range(PIECES + last_turn):
        done = tick - last_turn
        known = tick - (sections - 1)
        arrived_ahead = arrived_behind = None
        if 0 < tick < PIECES + sections - 1:
            pairs = [(s - 1, s) for s in range(1, sections) if 0 <= tick - s < PIECES]
            arrived_ahead = lax.ppermute(ahead, "section", pairs)
            ahead, matrix, slopes, stores = forward(
                tick, sections, arrived_ahead, packed_tokens, matrix, slopes, stores
            )
        if tick == sections - 2:
            matrix, turned = turn(matrix)
        if tick > sections - 1:
            pairs = [(s + 1, s) for s in range(sections - 1) if 0 <= tick - last_turn + s < PIECES]
            arrived_behind = lax.ppermute(behind, "section", pairs)
        if tick >= sections - 1:
            after = []
            if 1 <= known <= PIECES:
                after = crossed[known - 1][1:]
            if known == PIECES:
                gram_in, left, right, *rows_turned = prepare(
                    crossed, inverse_in[0], inverse_out[0]
                )
            if 1 <= done == PIECES - 1:
                after = after + [parts[done - 1][1]]
            if done >= 2:
                acc = gather(parts[done - 2], rows_turned[done - 2], acc)
                after = after + [acc[2]]
            behind, turned, kept = backward(
                tick, sections, arrived_behind, turned, slopes, packed_cot, kept, after
            )
        if 0 <= known < PIECES:
            swapped = [swap(stores[known][o], ranks, 2 * o) for o in range(1, chips)]
            crossed.append([stores[known][0]] + swapped)
        if 0 <= done < PIECES:
            piece = [kept[done]]
            for offset in range(1, chips):
                bit = offset & -offset if done % 2 else 1 << (offset.bit_length() - 1)
                piece.append(swap(piece[offset ^ bit], ranks, 2 * bit))
            parts.append(piece)
    for index in range(PIECES - 2, PIECES):
        acc = gather(parts[index][:-1], rows_turned[index], acc)
    final = [parts[-2][-1], parts[-1][-1]]
    gram_out, other = other_half(final, rows_turned[-1], acc[1], gram_in, acc[2])
    other = swap(other, ranks, 1)
    own = own_half(final, rows_turned[-1], acc[0])
    update, factor_in, factor_out = finish(
        inverse_in.shape[1], total, own, other, left, right, gram_in, gram_out
    )
    return (update[None], factor_in[None], factor_out[None])


def solution(mesh):
    in_specs = (
        P("dp", None),
        P("dp", None),
        P("dp", None),
        P("section", None, None),
        P("section", "dp", None, None),
        P("section", None, None, None),
    )
    out_specs = (
        P("section", "dp", None),
        P("section", "dp", None, None),
        P("section", "dp", None, None),
    )
    body = functools.partial(shards, mesh.shape["section"], mesh.shape["dp"])
    return jax.shard_map(body, mesh=mesh, in_specs=in_specs, out_specs=out_specs, check_vma=False)
```

```python
import functools
import math

import jax
import jax.numpy as jnp
from jax import lax
from jax.experimental import pallas as pl
from jax.experimental.pallas import tpu as pltpu
from jax.sharding import PartitionSpec as P

D = 3072
BLOCK = 192
MICRO = 4
ROWS = 80
TOK_DEV = 320
LIVE = 240
NBLK = 16

PIECE = 80
PIECES = LIVE // PIECE
WIDE = 1024
LOAD = 512
PAIR = 2 * BLOCK
SIDE = 256
HALF = D // 2
FLIGHT = 4

C_ZERO = 0.7978845608028654
C_ONE = 0.044715

BF = jnp.bfloat16
F32 = jnp.float32
VM = pl.BlockSpec(memory_space=pltpu.VMEM)
HB = pl.BlockSpec(memory_space=pl.ANY)
MIB = 1 << 20


def resident(x):
    return pltpu.with_memory_space_constraint(x, pltpu.VMEM)


def distant(x):
    return pltpu.with_memory_space_constraint(x, pltpu.HBM)


SMALL = pl.CostEstimate(flops=1000, bytes_accessed=1000, transcendentals=0)


def shape(*sizes, kind=BF):
    return jax.ShapeDtypeStruct(sizes, kind)


def near(*sizes, kind=BF):
    return pltpu.VMEM(sizes, kind)


def limit(size):
    return pltpu.CompilerParams(vmem_limit_bytes=size * MIB)


def swap(x, ranks, flip):
    return lax.ppermute(x, "dp", [(r, r ^ flip) for r in range(ranks)])


def contract_last(a, b):
    return lax.dot_general(a, b, (((1,), (1,)), ((), ())), preferred_element_type=F32)


def forward_columns(columns, held, w_ref, next_ref, slope_ref, piece):
    pre = jnp.dot(held[...], w_ref[:, columns], preferred_element_type=F32)
    square = pre * pre
    hyper = jnp.tanh(C_ZERO * (pre + C_ONE * pre * square))
    half = 0.5 * (1.0 + hyper)
    if next_ref is not None:
        next_ref[:, columns] = (held[:, columns].astype(F32) + pre * half).astype(BF)
    slope = half + 0.5 * pre * (1.0 - hyper * hyper) * C_ZERO * (1.0 + 3.0 * C_ONE * square)
    slope_ref[piece, :, columns] = slope.astype(BF)


def keep_columns(piece, span, held, stores):
    chips = len(stores) // len(span)
    width = D // chips
    chip = lax.div(lax.axis_index("dp"), 2)
    for k, index in enumerate(span):

        @pl.when(piece == index)
        def _():
            for offset in range(chips):
                columns = pl.ds(pl.multiple_of((chip ^ offset) * width, 128), width)
                stores[k * chips + offset][...] = held[:, columns]


def begin_kernel(sections, chips, counts_ref, tokens_ref, cot_ref, weight_ref, *refs):
    w_ref, next_ref, tok_out, cot_out, slope_ref = refs[:5]
    stores = refs[5 : 5 + chips]
    held, raw, counts, raw_sem, counts_sem, sems = refs[-6:]
    here = lax.axis_index("section")
    loads = [
        pltpu.make_async_copy(
            weight_ref.at[:, pl.ds(k * LOAD, LOAD)], w_ref.at[:, pl.ds(k * LOAD, LOAD)], sems.at[k]
        )
        for k in range(D // LOAD)
    ]
    copy_tokens = pltpu.make_async_copy(tokens_ref, raw, raw_sem)
    copy_cot = pltpu.make_async_copy(cot_ref, raw, raw_sem)
    copy_counts = pltpu.make_async_copy(counts_ref, counts, counts_sem)

    def pack(target):
        row = lax.broadcasted_iota(jnp.int32, (LIVE, TOK_DEV), 0)
        column = lax.broadcasted_iota(jnp.int32, (LIVE, TOK_DEV), 1)
        origin = row
        edge = jnp.int32(0)
        for micro in range(MICRO):
            count = counts[0, micro]
            edge = edge + count
            origin = origin + jnp.where(row >= edge, ROWS - count, 0)
        pick = (column == origin).astype(F32).astype(BF)
        for start in range(0, D, WIDE):
            part = jnp.dot(
                pick, raw[:, start : start + WIDE], preferred_element_type=F32
            ).astype(BF)
            for piece in range(PIECES):
                target[piece, :, start : start + WIDE] = part[piece * PIECE : (piece + 1) * PIECE]

    @pl.when(here == 0)
    def _():
        copy_counts.start()
        copy_tokens.start()
        for load in loads[:2]:
            load.start()
        copy_counts.wait()
        copy_tokens.wait()
        for load in loads[2:FLIGHT]:
            load.start()
        pack(tok_out)
        held[...] = tok_out[0]
        for k, load in enumerate(loads):
            load.wait()
            if k + FLIGHT < len(loads):
                loads[k + FLIGHT].start()
            forward_columns(pl.ds(k * LOAD, LOAD), held, w_ref, next_ref, slope_ref, 0)
        keep_columns(0, [0], held, stores)

    @pl.when(here > 0)
    def _():
        blocks = [
            pltpu.make_async_copy(
                weight_ref.at[pl.ds(k * LOAD, LOAD)], w_ref.at[pl.ds(k * LOAD, LOAD)], sems.at[k]
            )
            for k in range(D // LOAD)
        ]
        for block in blocks:
            block.start()
        for block in blocks:
            block.wait()

    @pl.when(jnp.logical_and(here == sections - 1, sections > 1))
    def _():
        copy_counts.start()
        copy_cot.start()
        copy_counts.wait()
        copy_cot.wait()
        pack(cot_out)


def begin(sections, chips, counts, tokens, cotangent, matrix):
    packed = near(PIECES, PIECE, D)
    return pl.pallas_call(
        functools.partial(begin_kernel, sections, chips),
        out_shape=(
            near(D, D),
            near(PIECE, D),
            packed,
            packed,
            near(PIECES, PIECE, D),
            *[near(PIECE, D // chips)] * (chips * PIECES),
            *[near(PIECE, D)] * PIECES,
        ),
        in_specs=[HB] * 4,
        out_specs=[VM] * (5 + chips) + [HB] * (chips * (PIECES - 1) + PIECES),
        scratch_shapes=[
            pltpu.VMEM((PIECE, D), BF),
            pltpu.VMEM((TOK_DEV, D), BF),
            pltpu.SMEM((1, MICRO), jnp.int32),
            pltpu.SemaphoreType.DMA,
            pltpu.SemaphoreType.DMA,
            pltpu.SemaphoreType.DMA((D // LOAD,)),
        ],
        compiler_params=limit(8),
        cost_estimate=SMALL,
    )(distant(counts), distant(tokens), distant(cotangent), distant(matrix))


def forward_kernel(tick, span, count, sends, from_ref, tok_ref, w_ref, *refs):
    outs = refs[1 + count :]
    slope_ref = outs[1]
    stores = outs[2 : 2 + count]
    next_ref = outs[2 + count] if sends else None
    held = outs[-1]
    here = lax.axis_index("section")
    piece = tick - here

    @pl.when(jnp.logical_and(piece >= 0, piece < PIECES))
    def _():
        if tick < PIECES:

            @pl.when(here == 0)
            def _():
                held[...] = tok_ref[tick]

        @pl.when(here > 0)
        def _():
            held[...] = from_ref[...]

        @pl.loop(0, D // WIDE)
        def _(step):
            columns = pl.ds(pl.multiple_of(step * WIDE, WIDE), WIDE)
            forward_columns(columns, held, w_ref, next_ref, slope_ref, piece)

        keep_columns(piece, span, held, stores)


def forward(tick, sections, arrived, tokens, matrix, slopes, stores):
    span = list(range(max(0, tick - sections + 1), min(PIECES - 1, tick) + 1))
    flat = [s for k in span for s in stores[k]]
    count = len(flat)
    sends = tick < PIECES + sections - 2
    outs = pl.pallas_call(
        functools.partial(forward_kernel, tick, span, count, sends),
        out_shape=(
            near(*matrix.shape),
            near(*slopes.shape),
            *[near(*s.shape) for s in flat],
            *[near(PIECE, D)] * sends,
        ),
        in_specs=[VM] * (4 + count),
        out_specs=[VM] * (2 + count + sends),
        scratch_shapes=[pltpu.VMEM((PIECE, D), BF)],
        input_output_aliases={2 + k: k for k in range(2 + count)},
        compiler_params=limit(4),
        cost_estimate=SMALL,
    )(
        resident(arrived),
        resident(tokens),
        resident(matrix),
        resident(slopes),
        *[resident(s) for s in flat],
    )
    stores = list(stores)
    chips = count // len(span)
    for k, index in enumerate(span):
        stores[index] = list(outs[2 + k * chips : 2 + (k + 1) * chips])
    return outs[-1], outs[0], outs[1], stores


def turn_kernel(w_ref, _, out_ref):
    @pl.when(lax.axis_index("section") > 0)
    def _():
        @pl.loop(0, D // LOAD)
        def _(step):
            rows = pl.ds(pl.multiple_of(step * LOAD, LOAD), LOAD)

            @pl.loop(0, D // LOAD)
            def _(other):
                columns = pl.ds(pl.multiple_of(other * LOAD, LOAD), LOAD)
                out_ref[columns, rows] = w_ref[rows, columns].T


def turn(matrix):
    return pl.pallas_call(
        turn_kernel,
        out_shape=(near(*matrix.shape), near(*matrix.shape)),
        in_specs=[VM],
        out_specs=(VM, VM),
        input_output_aliases={0: 0},
        compiler_params=limit(3),
        cost_estimate=SMALL,
    )(resident(matrix))


def backward_kernel(tick, sections, span, late, *refs):
    keeps = len(span)
    refs = refs[late:]
    w_ref, slope_ref = refs[:2]
    chained = tick > sections - 1
    opens = tick - (sections - 1) < PIECES
    cot_ref = refs[2] if opens else None
    from_ref = refs[2 + opens + keeps] if chained else None
    outs = refs[2 + opens + keeps + chained :]
    sends = tick < 2 * (sections - 1) + PIECES - 1
    kept = outs[1 : 1 + keeps]
    next_ref = outs[1 + keeps] if sends else None
    flow, scaled = outs[-2:]
    here = lax.axis_index("section")
    piece = tick - 2 * (sections - 1) + here

    @pl.when(jnp.logical_and(piece >= 0, piece < PIECES))
    def _():
        if opens:

            @pl.when(here == sections - 1)
            def _():
                flow[...] = cot_ref[tick - (sections - 1)]

        if from_ref is not None:

            @pl.when(here < sections - 1)
            def _():
                flow[...] = from_ref[...]

        scaled[...] = (flow[...].astype(F32) * slope_ref[piece].astype(F32)).astype(BF)
        for out, index in zip(kept, span):

            @pl.when(piece == index)
            def _():
                out[...] = scaled[...]

        @pl.when(jnp.logical_and(here > 0, sends))
        def _():
            @pl.loop(0, D // WIDE)
            def _(step):
                part = pl.ds(pl.multiple_of(step * WIDE, WIDE), WIDE)
                back = jnp.dot(scaled[...], w_ref[:, part], preferred_element_type=F32)
                if sends:
                    next_ref[:, part] = (flow[:, part].astype(F32) + back).astype(BF)


def backward(tick, sections, arrived, matrix, slopes, cotangent, kept, after):
    low = max(0, tick - 2 * (sections - 1))
    high = min(PIECES - 1, tick - (sections - 1))
    span = list(range(low, high + 1))
    first = [] if arrived is None else [resident(arrived)]
    sends = tick < 2 * (sections - 1) + PIECES - 1
    opens = [resident(cotangent)] if tick - (sections - 1) < PIECES else []
    base = 2 + len(after) + len(opens)
    out = pl.pallas_call(
        functools.partial(backward_kernel, tick, sections, span, len(after)),
        out_shape=(near(D, D), *[near(PIECE, D)] * (len(span) + sends)),
        in_specs=[HB] * len(after) + [VM] * (2 + len(opens) + len(span) + len(first)),
        out_specs=[VM] * (1 + len(span) + sends),
        scratch_shapes=[pltpu.VMEM((PIECE, D), BF), pltpu.VMEM((PIECE, D), BF)],
        input_output_aliases={
            len(after): 0,
            **{base + k: 1 + k for k in range(len(span))},
        },
        compiler_params=limit(4),
        cost_estimate=SMALL,
    )(
        *after,
        resident(matrix),
        resident(slopes),
        *opens,
        *[resident(kept[k]) for k in span],
        *first,
    )
    kept = list(kept)
    for k, index in enumerate(span):
        kept[index] = out[1 + k]
    return out[-1], out[0], kept


def prepare_kernel(chips, blocks, *refs):
    parts = refs[: chips * PIECES]
    pin_ref, pout_ref, gram_ref, left_ref, right_ref = refs[chips * PIECES : chips * PIECES + 5]
    turned = refs[chips * PIECES + 5 :]
    final = []
    width = gram_ref.shape[0]

    def keep(ref, some):
        columns = jnp.concatenate(some, axis=0).T
        for block in range(width // BLOCK):
            rows = slice(block * BLOCK, (block + 1) * BLOCK)
            ref[own_first(block * BLOCK, width // 2), :] = columns[rows]

    for piece in range(PIECES):
        some = [part[...] for part in parts[piece * chips : (piece + 1) * chips]]
        if piece < PIECES - 2:
            keep(turned[piece], some)
        else:
            keep(turned[piece], some[:-1])
            final.append(some[-1])
    keep(turned[PIECES], final)
    for block in range(2 * blocks):
        rows = slice(block * BLOCK, (block + 1) * BLOCK)
        gram = jnp.zeros((BLOCK, BLOCK), F32)
        for ref in turned:
            some = ref[rows, :]
            gram = gram + contract_last(some, some)
        gram_ref[rows, :] = gram
    for block in range(blocks):
        left_ref[block] = pin_ref[block].astype(BF)
    row = lax.broadcasted_iota(jnp.int32, (BLOCK, PAIR), 0)
    column = lax.broadcasted_iota(jnp.int32, (BLOCK, PAIR), 1)

    @pl.loop(0, NBLK // 2)
    def _(pair):
        for side in range(2):
            place = (column == row + side * BLOCK).astype(F32).astype(BF)
            wide = jnp.dot(pout_ref[2 * pair + side].astype(BF), place, preferred_element_type=F32)
            right_ref[pair, side * BLOCK : (side + 1) * BLOCK, :] = wide.astype(BF)


def prepare(parts, inverse_in, inverse_out):
    chips = len(parts[0])
    width = D // chips
    blocks = inverse_in.shape[0]
    flat = [p for piece in parts for p in piece]
    return pl.pallas_call(
        functools.partial(prepare_kernel, chips, blocks),
        out_shape=(
            near(width, BLOCK, kind=F32),
            near(blocks, BLOCK, BLOCK),
            near(NBLK // 2, PAIR, PAIR),
            *[near(width, chips * PIECE)] * (PIECES - 2),
            *[near(width, (chips - 1) * PIECE)] * 2,
            near(width, 2 * PIECE),
        ),
        in_specs=[VM] * (len(flat) + 2),
        out_specs=[VM] * (4 + PIECES),
        compiler_params=limit(8),
        cost_estimate=SMALL,
    )(*[resident(p) for p in flat], inverse_in, inverse_out)


def own_first(chunk, own):
    core = lax.rem(lax.axis_index("dp"), 2)
    first = lax.rem(chunk // own + core, 2) * own + chunk % own
    return pl.ds(pl.multiple_of(first, 16), min(own, BLOCK))


def add_gram(every, gram_ref, begins):
    width = gram_ref.shape[0]
    chip = lax.div(lax.axis_index("dp"), 2)
    columns = pl.ds(pl.multiple_of(chip * width, 128), width)
    turned = every[:, columns].T
    for block in range(width // BLOCK):
        rows = slice(block * BLOCK, (block + 1) * BLOCK)
        place = own_first(block * BLOCK, width // 2)
        gram = contract_last(turned[rows], turned[rows])
        gram_ref[place, :] = gram if begins else gram + gram_ref[place, :]


def fill(parts, every):
    for k, part in enumerate(parts):
        every[k * PIECE : (k + 1) * PIECE, :] = part[...]


def gather_kernel(count, begins, *refs):
    parts = refs[:count]
    xt_ref = refs[count]
    own_ref, other_ref, gram_ref, every = refs[-4:]
    fill(parts, every)
    add_gram(every, gram_ref, begins)
    own = own_ref.shape[0]

    @pl.loop(0, D // LOAD)
    def _(step):
        columns = pl.ds(pl.multiple_of(step * LOAD, LOAD), LOAD)
        term = jnp.dot(xt_ref[...], every[:, columns], preferred_element_type=F32)
        for acc_ref, some in ((own_ref, term[:own]), (other_ref, term[own:])):
            acc_ref[:, columns] = some if begins else acc_ref[:, columns] + some


def gather(parts, turned, so_far):
    count = len(parts)
    width = turned.shape[0]
    half = near(width // 2, D, kind=F32)
    return pl.pallas_call(
        functools.partial(gather_kernel, count, not so_far),
        out_shape=(half, half, near(width, BLOCK, kind=F32)),
        in_specs=[VM] * (count + 1 + len(so_far)),
        out_specs=(VM, VM, VM),
        scratch_shapes=[pltpu.VMEM((count * PIECE, D), BF)],
        input_output_aliases={count + 1 + k: k for k in range(len(so_far))},
        compiler_params=limit(8),
        cost_estimate=SMALL,
    )(*[resident(p) for p in parts], resident(turned), *[resident(a) for a in so_far])


def other_kernel(side, first, second, xt_ref, acc_ref, *refs):
    out_ref, part = refs[-2:]
    own = acc_ref.shape[0]
    rows = slice(own, 2 * own)
    fill((first, second), part)
    if side:
        gram_in_ref, gram_ref = refs[0], refs[2]
        add_gram(part, gram_ref, False)
        out_ref[:, HALF : HALF + BLOCK] = gram_ref[rows, :].astype(BF)
        out_ref[:, HALF + SIDE : HALF + SIDE + BLOCK] = gram_in_ref[rows, :].astype(BF)

    @pl.loop(0, HALF // LOAD)
    def _(step):
        place = pl.ds(pl.multiple_of(step * LOAD, LOAD), LOAD)
        columns = pl.ds(pl.multiple_of(side * HALF + step * LOAD, LOAD), LOAD)
        term = jnp.dot(xt_ref[rows, :], part[:, columns], preferred_element_type=F32)
        out_ref[:, place] = (term + acc_ref[:, columns]).astype(BF)


def other_half(side, parts, turned, acc, grams):
    own = acc.shape[0]
    outs = pl.pallas_call(
        functools.partial(other_kernel, side),
        out_shape=[near(*g.shape, kind=F32) for g in grams[1:]]
        + [near(own, HALF + 2 * SIDE * side)],
        in_specs=[VM] * (4 + len(grams)),
        out_specs=[VM] * max(1, len(grams)),
        scratch_shapes=[pltpu.VMEM((2 * PIECE, D), BF)],
        input_output_aliases={5: 0} if side else {},
        compiler_params=limit(8),
        cost_estimate=SMALL,
    )(
        *[resident(p) for p in parts],
        resident(turned),
        resident(acc),
        *[resident(g) for g in grams],
    )
    return outs


def own_kernel(first, second, xt_ref, acc_ref, out_ref, part):
    rows = slice(0, acc_ref.shape[0])
    fill((first, second), part)

    @pl.loop(0, D // LOAD)
    def _(step):
        columns = pl.ds(pl.multiple_of(step * LOAD, LOAD), LOAD)
        term = jnp.dot(xt_ref[rows, :], part[:, columns], preferred_element_type=F32)
        out_ref[:, columns] = term + acc_ref[:, columns]


def own_half(parts, turned, acc):
    return pl.pallas_call(
        own_kernel,
        out_shape=near(*acc.shape, kind=F32),
        in_specs=[VM] * 4,
        out_specs=VM,
        scratch_shapes=[pltpu.VMEM((2 * PIECE, D), BF)],
        input_output_aliases={3: 0},
        compiler_params=limit(8),
        cost_estimate=SMALL,
    )(*[resident(p) for p in parts], resident(turned), resident(acc))


def finish_kernel(side, blocks, total, own_ref, other_ref, left_ref, right_ref, *refs):
    scale = 1.0 / math.sqrt(total)
    pairs = HALF // PAIR
    base = side * HALF
    copies = []
    if side:
        gram_in_ref, gram_out_ref, update_ref, factor_in_ref, factor_out_ref = refs[:5]
        ready, grams, sems = refs[5:]
        for block in range(blocks):
            rows = slice(block * BLOCK, (block + 1) * BLOCK)
            for k, (gram, begins) in enumerate(((gram_in_ref, SIDE), (gram_out_ref, 0))):
                columns = slice(HALF + begins, HALF + begins + BLOCK)
                grams[k, block] = (gram[rows, :] + other_ref[rows, columns].astype(F32)) * (
                    1.0 / total
                )
        for k, ref in enumerate((factor_in_ref, factor_out_ref)):
            copy = pltpu.make_async_copy(grams.at[k], ref, sems.at[pairs + k])
            copy.start()
            copies.append(copy)
    else:
        update_ref, ready, sems = refs[1:]
    for step in range(pairs // 2):
        columns = slice(step * 2 * PAIR, (step + 1) * 2 * PAIR)
        wide = slice(base + step * 2 * PAIR, base + (step + 1) * 2 * PAIR)
        grad = (own_ref[:, wide] + other_ref[:, columns].astype(F32)).astype(BF)
        for block in range(blocks):
            rows = slice(block * BLOCK, (block + 1) * BLOCK)
            ready[rows, columns] = jnp.dot(
                left_ref[block], grad[rows], preferred_element_type=F32
            ).astype(BF)
    for pair in range(pairs):
        columns = slice(pair * PAIR, (pair + 1) * PAIR)
        wide = slice(base + pair * PAIR, base + (pair + 1) * PAIR)
        right = jnp.dot(
            ready[:, columns], right_ref[side * pairs + pair], preferred_element_type=F32
        )
        ready[:, columns] = (right * scale).astype(BF)
        copy = pltpu.make_async_copy(ready.at[:, columns], update_ref.at[:, wide], sems.at[pair])
        copy.start()
        copies.append(copy)
    for copy in copies:
        copy.wait()


def finish(side, blocks, total, own, other, left, right, grams, update):
    factor = shape(blocks, BLOCK, BLOCK, kind=F32)
    scratch = [pltpu.VMEM((blocks * BLOCK, HALF), BF)]
    if side:
        scratch.append(pltpu.VMEM((2, blocks, BLOCK, BLOCK), F32))
    return pl.pallas_call(
        functools.partial(finish_kernel, side, blocks, total),
        out_shape=[shape(blocks * BLOCK, D)] + [factor, factor] * side,
        in_specs=[VM] * (4 + len(grams)) + [HB] * len(update),
        out_specs=[HB] * (1 + 2 * side),
        scratch_shapes=[*scratch, pltpu.SemaphoreType.DMA((HALF // PAIR + 2,))],
        input_output_aliases={} if side else {4: 0},
        compiler_params=limit(8),
        cost_estimate=SMALL,
    )(
        resident(own),
        resident(other),
        resident(left),
        resident(right),
        *[resident(g) for g in grams],
        *[distant(u) for u in update],
    )


def shards(sections, ranks, tokens, cotangent, live_counts, weight, inverse_in, inverse_out):
    total = float(TOK_DEV * ranks)
    chips = ranks // 2
    begun = begin(sections, chips, live_counts, tokens, cotangent, weight[0])
    matrix, ahead, packed_tokens, packed_cot, slopes = begun[:5]
    stores = [list(begun[5 + k * chips : 5 + (k + 1) * chips]) for k in range(PIECES)]
    kept = list(begun[5 + chips * PIECES :])
    behind = None
    parts = []
    crossed = []
    last_turn = 2 * (sections - 1)
    single = [1 << b for b in range(chips.bit_length() - 1)]
    acc = []
    for tick in range(PIECES + last_turn):
        done = tick - last_turn
        known = tick - (sections - 1)
        arrived_ahead = arrived_behind = None
        if 0 < tick < PIECES + sections - 1:
            pairs = [(s - 1, s) for s in range(1, sections) if 0 <= tick - s < PIECES]
            arrived_ahead = lax.ppermute(ahead, "section", pairs)
            ahead, matrix, slopes, stores = forward(
                tick, sections, arrived_ahead, packed_tokens, matrix, slopes, stores
            )
        if tick == sections - 2:
            matrix, turned = turn(matrix)
        if tick > sections - 1:
            pairs = [(s + 1, s) for s in range(sections - 1) if 0 <= tick - last_turn + s < PIECES]
            arrived_behind = lax.ppermute(behind, "section", pairs)
        if tick >= sections - 1:
            after = []
            if 1 <= known <= PIECES:
                after = crossed[known - 1][1:]
            if known == PIECES:
                gram_in, left, right, *rows_turned = prepare(
                    crossed, inverse_in[0], inverse_out[0]
                )
            if 1 <= done == PIECES - 1:
                after = after + [parts[done - 1][1]]
            if done >= 2:
                acc = gather(parts[done - 2], rows_turned[done - 2], acc)
                after = after + [acc[2]]
            behind, turned, kept = backward(
                tick, sections, arrived_behind, turned, slopes, packed_cot, kept, after
            )
        if 0 <= known < PIECES:
            swapped = [swap(stores[known][o], ranks, 2 * o) for o in range(1, chips)]
            crossed.append([stores[known][0]] + swapped)
        if 0 <= done < PIECES:
            piece = [kept[done]]
            for offset in range(1, chips):
                bit = offset & -offset if done % 2 else 1 << (offset.bit_length() - 1)
                piece.append(swap(piece[offset ^ bit], ranks, 2 * bit))
            parts.append(piece)
    for index in range(PIECES - 2, PIECES):
        acc = gather(parts[index][:-1], rows_turned[index], acc)
    final = [parts[-2][-1], parts[-1][-1]]
    (first,) = other_half(0, final, rows_turned[-1], acc[1], [])
    first = swap(first, ranks, 1)
    gram_out, second = other_half(1, final, rows_turned[-1], acc[1], [gram_in, acc[2]])
    second = swap(second, ranks, 1)
    own = own_half(final, rows_turned[-1], acc[0])
    blocks = inverse_in.shape[1]
    update, factor_in, factor_out = finish(
        1, blocks, total, own, second, left, right, [gram_in, gram_out], []
    )
    (update,) = finish(0, blocks, total, own, first, left, right, [], [update])
    return (update[None], factor_in[None], factor_out[None])


def solution(mesh):
    in_specs = (
        P("dp", None),
        P("dp", None),
        P("dp", None),
        P("section", None, None),
        P("section", "dp", None, None),
        P("section", None, None, None),
    )
    out_specs = (
        P("section", "dp", None),
        P("section", "dp", None, None),
        P("section", "dp", None, None),
    )
    body = functools.partial(shards, mesh.shape["section"], mesh.shape["dp"])
    return jax.shard_map(body, mesh=mesh, in_specs=in_specs, out_specs=out_specs, check_vma=False)
```
